32 devices in a mesh: rows: 8 (over z, y), seq: 4 (over x, core).
Axes of the slice: x: 2, y: 2, z: 4, core: 2. Of those that a mesh axis runs over, the one named last changes fastest.
Arguments:
- noisy_mel: bfloat16 [8, 3328, 100], P('rows', 'seq'), may hold values from -6 to 6
- cond_mel: bfloat16 [8, 3328, 100], P('rows', 'seq'), may hold values from -6 to 6
- text_feat: bfloat16 [8, 3328, 512], P('rows', 'seq'), may hold values from -6 to 6
- time_embed: bfloat16 [8, 1024], P('rows'), may hold values from -6 to 6
- seg_lengths: int32 [8, 8], P('rows'), may hold values from 1 to 3224, as said below
- audio_drop: int32 [8, 8], P('rows'), may hold values 0 or 1
- text_drop: int32 [8, 8], P('rows'), may hold values 0 or 1
- w_in: bfloat16 [712, 1024], replicated, may hold values from -0.21875 to 0.21875
- b_in: bfloat16 [1024], replicated, may hold values from -1 to 1
- ada_w: bfloat16 [1024, 6144], replicated, may hold values from -0.1875 to 0.1875
- ada_b: bfloat16 [6144], replicated, may hold values from -1 to 1
- w_qkv: bfloat16 [1024, 3072], replicated, may hold values from -0.1875 to 0.1875
- b_qkv: bfloat16 [3072], replicated, may hold values from -1 to 1
- w_out: bfloat16 [1024, 1024], replicated, may hold values from -3 to 3
- b_out: bfloat16 [1024], replicated, may hold values from -1 to 1
- w_up: bfloat16 [1024, 2048], replicated, may hold values from -0.1875 to 0.1875
- b_up: bfloat16 [2048], replicated, may hold values from -1 to 1
- w_down: bfloat16 [2048, 1024], replicated, may hold values from -0.125 to 0.125
- b_down: bfloat16 [1024], replicated, may hold values from -1 to 1
- cotangent: bfloat16 [8, 3328, 1024], P('rows', 'seq'), may hold values from -6 to 6
Outputs:
- out: bfloat16 [8, 3328, 1024], P('rows', 'seq')
- noisy_grad: float32 [8, 3328, 100], P('rows', 'seq')
- cond_grad: float32 [8, 3328, 100], P('rows', 'seq')
- text_grad: float32 [8, 3328, 512], P('rows', 'seq')
- time_grad: float32 [8, 1024], P('rows')
- w_in_grad: float32 [712, 1024], P(None, 'seq')
- b_in_grad: float32 [1024], P('seq')
- ada_w_grad: float32 [1024, 6144], P('seq')
- ada_b_grad: float32 [6144], P('seq')
- w_qkv_grad: float32 [1024, 3072], P('seq')
- b_qkv_grad: float32 [3072], P('seq')
- w_out_grad: float32 [1024, 1024], P('seq')
- b_out_grad: float32 [1024], P('seq')
- w_up_grad: float32 [1024, 2048], P('seq')
- b_up_grad: float32 [2048], P('seq')
- w_down_grad: float32 [2048, 1024], P('seq')
- b_down_grad: float32 [1024], P('seq')
The draws below stay inside these ranges and needn't reach their ends.
Inputs may be any that keep to these rules, and one draw needn't show every extreme that they name: `seg_lengths`: each row's 8 lengths are positive and sum to 3328; in one row of each group of 1 row one segment other than the last has exactly 3224 frames.
All inputs are finite; a program needn't handle non-finite values. No bound on the sum of `audio_drop` or of `text_drop` on one device may be relied on, other than what follows from the above.
Results may differ from the reference program's by a relative error of at most 0.02.
Values may be sent and summed in bfloat16 or wider, within the bound.
No kernel may reach another device: no remote copies, remote signals or barrier semaphores. Data moves between devices by JAX's collectives and lax.ppermute only.
A program may use at most 448 MiB of HBM per device.

```python
import math
import jax
import jax.numpy as jnp
from jax import lax

D = 1024
HEADS = 16
HD = 64
FF = 2048
MEL = 100
TEXT = 512
IN_DIM = 712
LEN = 3328
SEGS = 8
ROWS_DEV = 1
ROWS = 8


def draw_seg_lengths(key, part):
    key = jax.random.fold_in(key, 11)
    subkeys = jax.random.split(key, 6)
    shares = jax.random.randint(subkeys[0], (ROWS, SEGS - 1), 8, 64)
    pad_wide = jax.random.randint(subkeys[1], (ROWS,), LEN // 32, LEN // 8)
    rest_total = LEN // 32
    rest_extra = rest_total - (SEGS - 1)
    cut_scores = jax.random.randint(subkeys[3], (ROWS, SEGS - 2), 0, rest_extra + 1)
    cut_points = jnp.sort(cut_scores, axis=1)
    lower = jnp.concatenate([jnp.zeros((ROWS, 1), jnp.int32), cut_points], axis=1)
    upper = jnp.concatenate([cut_points, jnp.full((ROWS, 1), rest_extra, jnp.int32)], axis=1)
    rest_pieces = (upper - lower + 1).astype(jnp.int32)
    chosen = jax.random.randint(subkeys[4], (ROWS // ROWS_DEV,), 0, ROWS_DEV)
    special = jnp.arange(ROWS) % ROWS_DEV == jnp.repeat(chosen, ROWS_DEV)
    place = jax.random.randint(subkeys[5], (ROWS, 1), 0, SEGS - 1)
    columns = jnp.arange(SEGS, dtype=jnp.int32)[None, :]
    before_index = jnp.clip(columns, 0, SEGS - 2)
    after_index = jnp.clip(columns - 1, 0, SEGS - 2)
    before_vals = jnp.take_along_axis(rest_pieces, jnp.broadcast_to(before_index, (ROWS, SEGS)), axis=1)
    after_vals = jnp.take_along_axis(rest_pieces, jnp.broadcast_to(after_index, (ROWS, SEGS)), axis=1)
    long_len = LEN - rest_total
    special_rows = jnp.where(columns < place, before_vals, jnp.where(columns == place, long_len, after_vals))
    filled = LEN - pad_wide
    spread = shares * filled[:, None] // jnp.sum(shares, axis=1, keepdims=True)
    spread = spread.at[:, -1].add(filled - jnp.sum(spread, axis=1))
    normal_rows = jnp.concatenate([spread, pad_wide[:, None]], axis=1)
    return jnp.where(special[:, None], special_rows, normal_rows).astype(jnp.int32)


def plant(drawn, key, low, high):
    longest = drawn.shape.index(max(drawn.shape))
    spots = []
    for shift in (0, 1):
        where = [jax.random.randint(jax.random.fold_in(key, axis), (), 0, length) for axis, length in enumerate(drawn.shape)]
        where[longest] = (where[longest] + shift) % drawn.shape[longest]
        spots.append(tuple(where))
    return drawn.at[spots[0]].set(low).at[spots[1]].set(high)


def block_scale(key, extent, cuts, least, high):
    def one(dim, blocks):
        draws = jax.random.uniform(jax.random.fold_in(jax.random.fold_in(key, 6), dim), (blocks,), jnp.float32, least / len(cuts), high / len(cuts))
        return jnp.repeat(jnp.exp(draws), extent[dim] // blocks).reshape((-1,) + (1,) * (len(extent) - dim - 1))

    gain = one(*cuts[0])
    for cut in cuts[1:]:
        gain = gain * one(*cut)
    return gain


def noise(key, dims, deviation, reach, pieces=(), held_as=jnp.bfloat16):
    array = jax.random.normal(key, dims, jnp.float32) * deviation
    if len(pieces) > 0:
        array = block_scale(key, dims, pieces, -0.22, 0.18) * array
    return jnp.clip(array, min=-reach, max=reach).astype(held_as)


def setup_inputs(seed: int = 0) -> dict:
    splits = jax.random.split(jax.random.key(seed), 21)
    noisy_mel = noise(splits[0], (ROWS, LEN, MEL), 1.0, 6.0, ((0, 8), (1, 4)))
    cond_mel = noise(splits[1], (ROWS, LEN, MEL), 1.0, 6.0, ((0, 8), (1, 4)))
    text_feat = noise(splits[2], (ROWS, LEN, TEXT), 1.0, 6.0, ((0, 8), (1, 4)))
    time_embed = noise(splits[3], (ROWS, D), 1.0, 6.0, ((0, 8),))
    seg_lengths = draw_seg_lengths(jax.random.fold_in(splits[20], 71), 0)
    audio_drop = plant((jax.random.randint(splits[5], (ROWS, SEGS), 0, 10) < 3).astype(jnp.int32), jax.random.fold_in(splits[5], 1), 0, 1)
    text_drop = plant((jax.random.randint(splits[6], (ROWS, SEGS), 0, 10) < 2).astype(jnp.int32), jax.random.fold_in(splits[6], 1), 0, 1)
    w_in = noise(splits[7], (IN_DIM, D), IN_DIM ** -0.5, 0.21875)
    b_in = noise(splits[8], (D,), 0.2, 1.0)
    ada_w = noise(splits[9], (D, 6 * D), D ** -0.5, 0.1875)
    ada_b = noise(splits[10], (6 * D,), 0.2, 1.0)
    w_qkv = noise(splits[11], (D, 3 * D), D ** -0.5, 0.1875)
    b_qkv = noise(splits[12], (3 * D,), 0.2, 1.0)
    w_out = noise(splits[13], (D, D), (max(1, D // 256)) ** -0.5, 3.0)
    b_out = noise(splits[14], (D,), 0.2, 1.0)
    w_up = noise(splits[15], (D, FF), D ** -0.5, 0.1875)
    b_up = noise(splits[16], (FF,), 0.2, 1.0)
    w_down = noise(splits[17], (FF, D), FF ** -0.5, 0.125)
    b_down = noise(splits[18], (D,), 0.2, 1.0)
    cotangent = noise(splits[19], (ROWS, LEN, D), 1.0, 6.0, ((0, 8), (1, 4)))
    return dict(noisy_mel=noisy_mel, cond_mel=cond_mel, text_feat=text_feat, time_embed=time_embed, seg_lengths=seg_lengths, audio_drop=audio_drop, text_drop=text_drop, w_in=w_in, b_in=b_in, ada_w=ada_w, ada_b=ada_b, w_qkv=w_qkv, b_qkv=b_qkv, w_out=w_out, b_out=b_out, w_up=w_up, b_up=b_up, w_down=w_down, b_down=b_down, cotangent=cotangent)


@jax.custom_vjp
def low(v):
    return lax.optimization_barrier(v.astype(jnp.bfloat16)).astype(jnp.float32)

@jax.custom_vjp
def low_back(v):
    return v

def low_keep(v):
    return (low(v), None)

def low_pass(kept, grad):
    return (grad,)

def back_keep(v):
    return (v, None)

def back_low(kept, grad):
    return (low(grad),)
low.defvjp(low_keep, low_pass)
low_back.defvjp(back_keep, back_low)
EPS = 1e-06
THETA = 10000.0
MASKED = -1e+30

def matmul(left_rows, right_rows):
    return jnp.dot(left_rows, right_rows, precision=lax.Precision.HIGHEST)

def frame_table(row_lengths, first_frame, frame_count):
    seg_ends = jnp.cumsum(row_lengths).astype(jnp.int32)
    starts = (seg_ends - row_lengths).astype(jnp.int32)
    frames = (first_frame + jnp.arange(frame_count, dtype=jnp.int32)).astype(jnp.int32)
    inside = ((frames[:, None] >= starts[None, :]) & (frames[:, None] < seg_ends[None, :])).astype(jnp.int32)
    numbers = jnp.arange(row_lengths.shape[0], dtype=jnp.int32)
    labels = lax.optimization_barrier(jnp.sum(inside * numbers[None, :], axis=1)).astype(jnp.int32)
    offsets = (frames - lax.optimization_barrier(jnp.sum(inside * starts[None, :], axis=1))).astype(jnp.int32)
    return (inside.astype(jnp.float32), labels, offsets)

def rotary_tables(offsets, head_dim):
    halves = head_dim // 2
    frequency = jnp.exp(-math.log(THETA) * 2.0 * jnp.arange(halves, dtype=jnp.float32) / head_dim)
    angles = offsets.astype(jnp.float32)[..., None] * frequency
    return (jnp.cos(angles), jnp.sin(angles))

def rotate(values, cos_table, sin_table, head_count):
    full_shape = values.shape
    split_parts = values.reshape(full_shape[:-1] + (head_count, 2, full_shape[-1] // (2 * head_count)))
    first_half = split_parts[..., 0, :]
    second_half = split_parts[..., 1, :]
    cos_part = cos_table[..., None, :]
    sin_part = sin_table[..., None, :]
    turned = jnp.stack([first_half * cos_part - second_half * sin_part, second_half * cos_part + first_half * sin_part], axis=-2)
    return turned.reshape(full_shape)

def layer_norm(stream):
    center = stream - lax.optimization_barrier(jnp.mean(stream, axis=-1, keepdims=True))
    return center * lax.rsqrt(lax.optimization_barrier(jnp.mean(center * center, axis=-1, keepdims=True)) + EPS)

def attend(query_block, label_block, key_heads, value_heads, key_label_row):
    scores = jnp.einsum('qhd,khd->hqk', query_block, key_heads, precision=lax.Precision.HIGHEST) * HD ** (-0.5)
    scores = low_back(scores)
    matches = label_block[None, :, None] == key_label_row[None, None, :]
    masked = jnp.where(matches, scores, MASKED)
    highest = lax.optimization_barrier(jnp.max(masked, axis=2, keepdims=True))
    weights = jnp.exp(masked - highest)
    probs = weights / lax.optimization_barrier(jnp.sum(weights, axis=2, keepdims=True))
    return jnp.einsum('hqk,khd->qhd', low(probs), value_heads, precision=lax.Precision.HIGHEST)

def query_blocks():
    if LEN % 4 == 0 and LEN >= 2048:
        return 4
    return 1

def row_forward(params, noisy_row, cond_row, text_row, time_row, row_lengths, audio_row, text_mask):
    w_in, b_in, ada_w, ada_b, w_qkv, b_qkv, w_out, b_out, w_up, b_up, w_down, b_down = params
    member, labels, offsets = frame_table(row_lengths, 0, LEN)
    keep_audio = 1.0 - matmul(member, audio_row.astype(jnp.float32))
    keep_text = 1.0 - matmul(member, text_mask.astype(jnp.float32))
    frame_valid = 1.0 - member[:, SEGS - 1]
    inputs = jnp.concatenate([noisy_row, cond_row * keep_audio[:, None], text_row * keep_text[:, None]], axis=1)
    resid_zero = low_back(matmul(inputs, w_in) + b_in)
    embedding = low_back(matmul(low(jax.nn.silu(time_row))[None, :], ada_w)[0] + ada_b)
    shift_one, scale_one, gate_one, shift_two, scale_two, gate_two = jnp.split(embedding, 6)
    mod_one = low(layer_norm(resid_zero) * (1.0 + scale_one) + shift_one)
    projected = low_back(matmul(mod_one, w_qkv) + b_qkv)
    cos_table, sin_table = rotary_tables(offsets, HD)
    queries = low(rotate(projected[:, :D], cos_table, sin_table, HEADS))
    key_rows = low(rotate(projected[:, D:2 * D], cos_table, sin_table, HEADS))
    value_rows = low(projected[:, 2 * D:])
    block_count = query_blocks()
    query_split = queries.reshape(block_count, LEN // block_count, HEADS, HD)
    label_split = labels.reshape(block_count, LEN // block_count)
    key_heads = key_rows.reshape(LEN, HEADS, HD)
    value_heads = value_rows.reshape(LEN, HEADS, HD)
    attended = lax.map(jax.checkpoint(lambda block_pair: attend(block_pair[0], block_pair[1], key_heads, value_heads, labels)), (query_split, label_split))
    mixed = low(low_back(attended.reshape(LEN, D)))
    branch = low_back(matmul(mixed, w_out) + b_out)
    resid_one = resid_zero + gate_one * branch * frame_valid[:, None]
    mod_two = low(layer_norm(resid_one) * (1.0 + scale_two) + shift_two)
    hidden = low_back(matmul(mod_two, w_up) + b_up)
    activated = low(jax.nn.gelu(hidden, approximate=True))
    ff_out = low_back(matmul(activated, w_down) + b_down)
    return resid_one + gate_two * ff_out

def reference(noisy_mel, cond_mel, text_feat, time_embed, seg_lengths, audio_drop, text_drop, w_in, b_in, ada_w, ada_b, w_qkv, b_qkv, w_out, b_out, w_up, b_up, w_down, b_down, cotangent):
    params = tuple((item.astype(jnp.float32) for item in (w_in, b_in, ada_w, ada_b, w_qkv, b_qkv, w_out, b_out, w_up, b_up, w_down, b_down)))

    def whole(weights, noisy_float, cond_float, text_float, time_float):

        def one_row(row_data):
            return row_forward(weights, *row_data)
        return lax.map(jax.checkpoint(one_row), (noisy_float, cond_float, text_float, time_float, seg_lengths, audio_drop, text_drop))
    outputs, pullback = jax.vjp(whole, params, noisy_mel.astype(jnp.float32), cond_mel.astype(jnp.float32), text_feat.astype(jnp.float32), time_embed.astype(jnp.float32))
    param_grads, noisy_grad, cond_grad, text_grad, time_grad = pullback(cotangent.astype(jnp.float32))
    return (outputs.astype(jnp.bfloat16), noisy_grad, cond_grad, text_grad, time_grad, param_grads[0], param_grads[1], param_grads[2], param_grads[3], param_grads[4], param_grads[5], param_grads[6], param_grads[7], param_grads[8], param_grads[9], param_grads[10], param_grads[11])
```

```python
import functools
import math

import jax
import jax.numpy as jnp
from jax import lax
from jax.experimental import pallas as pl
from jax.experimental.pallas import tpu as pltpu
from jax.sharding import Mesh, PartitionSpec as P

HEADS = 16
EPS = 1e-06
THETA = 10000.0
MASKED = -1e30
F32 = jnp.float32
BF = jnp.bfloat16
MIB = 2**20


def dot_nn(a, b):
    return jnp.dot(a, b, preferred_element_type=F32)


def dot_tn(a, b):
    return lax.dot_general(a, b, (((0,), (0,)), ((), ())), preferred_element_type=F32)


def dot_nt(a, b):
    return lax.dot_general(a, b, (((1,), (1,)), ((), ())), preferred_element_type=F32)


def shift(v, axis, step):
    size = lax.axis_size(axis)
    return lax.ppermute(v, axis, [(i, (i + step) % size) for i in range(size)])


def flip(v, axis, bit):
    size = lax.axis_size(axis)
    return lax.ppermute(v, axis, [(i, i ^ bit) for i in range(size)])


def bits(axis):
    size = lax.axis_size(axis)
    assert size & (size - 1) == 0
    return [1 << b for b in range(size.bit_length() - 1)]


def sum_small(v, axis):
    for bit in bits(axis):
        v = v + flip(v, axis, bit)
    return v


def gather_small(v, axis):
    for bit in bits(axis):
        v = jnp.concatenate([v, flip(v, axis, bit)], axis=0)
    return v


def pick(v, index):
    return lax.dynamic_index_in_dim(v, index, 0, keepdims=False)


def add_bf16(a, b):
    return (a.astype(F32) + b.astype(F32)).astype(BF)


def scatter_seq(g):
    core, sx = lax.axis_index("core"), lax.axis_index("sx")
    chips = lax.axis_size("sx")
    g = g.reshape((chips, 2) + g.shape[1:])
    recv = flip(lax.dynamic_index_in_dim(g, 1 - core, 1, keepdims=False), "core", 1)
    part = add_bf16(lax.dynamic_index_in_dim(g, core, 1, keepdims=False), recv)
    total = pick(part, sx)
    for t in range(1, chips):
        total = add_bf16(total, shift(pick(part, (sx + t) % chips), "sx", t))
    return total


def sum_rows(v):
    sent = []
    for axis in ("ry", "rz"):
        for bit in reversed(bits(axis)):
            half = v.shape[0] // 2
            upper = (lax.axis_index(axis) // bit) % 2
            two = v.reshape((2, half) + v.shape[1:])
            recv = flip(pick(two, 1 - upper), axis, bit)
            v = add_bf16(pick(two, upper), recv)
            sent.append((axis, bit, upper))
    for axis, bit, upper in reversed(sent):
        recv = flip(v, axis, bit)
        low = upper == 0
        v = jnp.concatenate([jnp.where(low, v, recv), jnp.where(low, recv, v)], axis=0)
    return v


def total_grad(g):
    seq = lax.axis_size("sx") * 2
    return sum_rows(scatter_seq(g.reshape((seq, g.shape[0] // seq) + g.shape[1:])))


def turn(x, cos, sin, lane):
    partner = jnp.where(lane % 64 < 32, pltpu.roll(x, 96, 1), pltpu.roll(x, 32, 1))
    return x * cos + partner * sin


def front_kernel(core, x_ref, win_ref, bin_ref, shift_ref, scale_ref, *rest, parts):
    weights = rest[: 2 * len(parts)]
    cos_ref, sin_ref = rest[2 * len(parts) : 2 * len(parts) + 2]
    mod_ref = rest[2 * len(parts) + 2]
    outs = rest[2 * len(parts) + 3 :]
    resid = dot_nn(x_ref[...], win_ref[...]) + bin_ref[...]
    center = resid - jnp.mean(resid, axis=1, keepdims=True)
    inv = lax.rsqrt(jnp.mean(center * center, axis=1, keepdims=True) + EPS)
    mod = (center * inv * (1.0 + scale_ref[...]) + shift_ref[...]).astype(BF)
    mod_ref[...] = mod
    lane = lax.broadcasted_iota(jnp.int32, (1, 128), 1)
    for n, part in enumerate(parts):
        y = dot_nn(mod, weights[2 * n][...]) + weights[2 * n + 1][...]
        if part == "v":
            outs[n][...] = y.astype(BF)
            continue
        scale = 0.125 if part == "q" else 1.0
        for t in range(0, y.shape[1], 128):
            z = turn(y[:, t : t + 128], cos_ref[...], sin_ref[...], lane)
            outs[n][:, t : t + 128] = (z * scale).astype(BF)


def front(core, x, w_in, b_in, shift_one, scale_one, w_qkv, b_qkv, cos, sin, parts):
    rows, n, width = x.shape
    model = w_in.shape[1]
    half = model // 2
    block = 416 if n % 416 == 0 else n
    place = {"q": 0, "k": 1, "v": 2}
    frame = lambda w: pl.BlockSpec((None, block, w), lambda r, i, c: (r, i, 0))
    row = lambda w: pl.BlockSpec((None, 1, w), lambda r, i, c: (r, 0, 0))
    whole = lambda a, b: pl.BlockSpec((a, b), lambda r, i, c: (0, 0))
    w_specs, w_args = [], []
    for part in parts:
        j = place[part]
        w_specs.append(pl.BlockSpec((model, half), lambda r, i, c, j=j: (0, 2 * j + c[0])))
        w_specs.append(pl.BlockSpec((1, half), lambda r, i, c, j=j: (0, 2 * j + c[0])))
        w_args += [w_qkv, b_qkv]
    return pl.pallas_call(
        functools.partial(front_kernel, parts=parts),
        grid_spec=pltpu.PrefetchScalarGridSpec(
            num_scalar_prefetch=1,
            grid=(rows, n // block),
            in_specs=[frame(width), whole(width, model), whole(1, model), row(model), row(model)]
            + w_specs
            + [frame(128), frame(128)],
            out_specs=[frame(model)] + [frame(half)] * len(parts),
        ),
        out_shape=[jax.ShapeDtypeStruct((rows, n, model), BF)]
        + [jax.ShapeDtypeStruct((rows, n, half), BF)] * len(parts),
        compiler_params=pltpu.CompilerParams(vmem_limit_bytes=48 * MIB),
        cost_estimate=pl.CostEstimate(
            flops=2 * rows * n * model * (width + half * len(parts)),
            bytes_accessed=rows * n * 2 * (width + model + half * len(parts)) + 8 * MIB,
            transcendentals=0,
        ),
        name="front",
    )(core, x, w_in, b_in, shift_one, scale_one, *w_args, cos, sin)


def attend_kernel(q_ref, qx_ref, k_ref, kx_ref, v_ref, o_ref, l_ref, s_ref, m_ref, acc_ref):
    frames = k_ref.shape[0]
    h, phase = pl.program_id(2), pl.program_id(3)
    lane = lax.broadcasted_iota(jnp.int32, (1, 128), 1)
    mine = (lane // 64) == h
    zero = jnp.zeros((), BF)
    step = 256 if frames % 256 == 0 else frames

    @pl.when(phase == 0)
    def _():
        q2 = jnp.concatenate([q_ref[...], qx_ref[...]], axis=1)
        top = None
        for c in range(0, frames, step):
            keys = jnp.where(mine, k_ref[c : c + step, :], zero)
            s = dot_nt(q2, jnp.concatenate([keys, kx_ref[c : c + step, :]], axis=1))
            s_ref[:, c : c + step] = s
            for t in range(0, step, 128):
                part = s[:, t : t + 128]
                top = part if top is None else jnp.maximum(top, part)
        m_ref[...] = jnp.broadcast_to(jnp.max(top, axis=1, keepdims=True), m_ref.shape)

    @pl.when(phase == 1)
    def _():
        top = m_ref[:, :1]
        ones = jnp.broadcast_to(jnp.where(mine, 1.0, 0.0).astype(BF), (step, 128))
        acc = None
        for c in range(0, frames, step):
            p = jnp.exp(s_ref[:, c : c + step] - top).astype(BF)
            values = jnp.where(mine, v_ref[c : c + step, :], zero)
            d = dot_nn(p, jnp.concatenate([values, ones], axis=1))
            acc = d if acc is None else acc + d

        @pl.when(h == 0)
        def _():
            acc_ref[...] = acc
            l_ref[...] = m_ref[...]

        @pl.when(h == 1)
        def _():
            both = acc + acc_ref[...]
            total = both[:, 128:]
            o_ref[...] = (both[:, :128] / total).astype(BF)
            l_ref[...] = jnp.where(mine, m_ref[...], l_ref[...]) + jnp.log(total)


def attend(q, qx, k, kx, v):
    rows, m, width = q.shape
    n = k.shape[1]
    pairs = width // 128
    qs = pl.BlockSpec((None, m, 128), lambda r, p, h, f: (r, 0, p))
    q0 = pl.BlockSpec((None, m, 128), lambda r, p, h, f: (r, 0, 0))
    ks = pl.BlockSpec((None, n, 128), lambda r, p, h, f: (r, 0, p))
    k0 = pl.BlockSpec((None, n, 128), lambda r, p, h, f: (r, 0, 0))
    return pl.pallas_call(
        attend_kernel,
        grid=(rows, pairs, 2, 2),
        in_specs=[qs, q0, ks, k0, ks],
        out_specs=[qs, qs],
        out_shape=[
            jax.ShapeDtypeStruct((rows, m, width), BF),
            jax.ShapeDtypeStruct((rows, m, width), F32),
        ],
        scratch_shapes=[
            pltpu.VMEM((m, n), F32),
            pltpu.VMEM((m, 128), F32),
            pltpu.VMEM((m, 256), F32),
        ],
        compiler_params=pltpu.CompilerParams(vmem_limit_bytes=56 * MIB),
        cost_estimate=pl.CostEstimate(
            flops=16 * rows * pairs * m * n * 256,
            bytes_accessed=rows * width * (m * 8 + n * 4),
            transcendentals=rows * pairs * 2 * m * n,
        ),
        name="attend",
    )(q, qx, k, kx, v)


def split3(x, lane, rest):
    hi = x.astype(BF).astype(F32)
    mid = (x - hi).astype(BF).astype(F32)
    low = x - hi - mid
    place = lane % 64
    return jnp.where(
        place == 8, hi, jnp.where(place == 9, mid, jnp.where(place == 10, low, rest))
    ).astype(BF)


def attend_back_kernel(
    q_ref, qx_ref, k_ref, kx_ref, v_ref, o_ref, do_ref, l_ref, cq_ref, sq_ref, ck_ref, sk_ref,
    dq_ref, dk_ref, dv_ref,
    q2, d2, k2, v2, kk, qt, dt, p_s, s_s, dq_s, dk_s, dv_s,
):
    m, n = q_ref.shape[0], k_ref.shape[0]
    h, phase = pl.program_id(2), pl.program_id(3)
    lane = lax.broadcasted_iota(jnp.int32, (1, 128), 1)
    mine = (lane // 64) == h
    zero = jnp.zeros((), BF)
    step = 256 if n % 256 == 0 else n
    half = pl.ds(pl.multiple_of(h * 64, 64), 64)

    @pl.when((phase == 0) & (h == 0))
    def _():
        q2[:, :128] = q_ref[...]
        q2[:, 128:] = split3(l_ref[...], lane, qx_ref[...].astype(F32))
        prod = do_ref[...].astype(F32) * o_ref[...].astype(F32)
        same = (
            lax.broadcasted_iota(jnp.int32, (128, 128), 0) // 64
            == lax.broadcasted_iota(jnp.int32, (128, 128), 1) // 64
        )
        same = jnp.where(same, 1.0, 0.0).astype(BF)
        hi = prod.astype(BF)
        low = (prod - hi.astype(F32)).astype(BF)
        delta = dot_nn(
            jnp.concatenate([hi, low], axis=1), jnp.concatenate([same, same], axis=0)
        )
        d2[:, :128] = do_ref[...]
        d2[:, 128:] = split3(delta, lane, jnp.zeros((m, 128), F32))
        qt[...] = q_ref[...].T
        dt[...] = do_ref[...].T

    @pl.when(phase == 0)
    def _():
        keys = jnp.where(mine, k_ref[...], zero)
        kk[...] = keys
        k2[:128, :] = keys.T
        less = (lane - 64 * h >= 8) & (lane - 64 * h < 11)
        k2[128:, :] = jnp.where(less, -1.0, kx_ref[...].astype(F32)).astype(BF).T
        v2[:128, :] = jnp.where(mine, v_ref[...], zero).T
        v2[128:, :] = jnp.broadcast_to(jnp.where(less, -1.0, 0.0), (n, 128)).astype(BF).T

    @pl.when(phase == 1)
    def _():
        for c in range(0, n, step):
            s = dot_nn(q2[...], k2[:, c : c + step])
            d = dot_nn(d2[...], v2[:, c : c + step])
            p = jnp.exp(s)
            p_s[:, c : c + step] = p.astype(BF)
            s_s[:, c : c + step] = (p * d).astype(BF)

    @pl.when(phase == 2)
    def _():
        acc = dot_nn(s_s[...], kk[...])

        @pl.when(h == 0)
        def _():
            dq_s[...] = acc

        @pl.when(h == 1)
        def _():
            total = (dq_s[...] + acc) * 0.125
            dq_ref[...] = turn(total, cq_ref[...], -sq_ref[...], lane).astype(BF)

    @pl.when(phase == 3)
    def _():
        for c in range(0, n, step):
            dk_s[half, c : c + step] = dot_nn(qt[half, :], s_s[:, c : c + step])
            dv_s[half, c : c + step] = dot_nn(dt[half, :], p_s[:, c : c + step])

        @pl.when(h == 1)
        def _():
            dk_ref[...] = turn(dk_s[...].T, ck_ref[...], -sk_ref[...], lane).astype(BF)
            dv_ref[...] = dv_s[...].astype(BF).T


def attend_back(q, qx, k, kx, v, o, do, l, cos_q, sin_q, cos_k, sin_k):
    rows, m, width = q.shape
    n = k.shape[1]
    pairs = width // 128
    qs = pl.BlockSpec((None, m, 128), lambda r, p, h, f: (r, 0, p))
    q0 = pl.BlockSpec((None, m, 128), lambda r, p, h, f: (r, 0, 0))
    ks = pl.BlockSpec((None, n, 128), lambda r, p, h, f: (r, 0, p))
    k0 = pl.BlockSpec((None, n, 128), lambda r, p, h, f: (r, 0, 0))
    return pl.pallas_call(
        attend_back_kernel,
        grid=(rows, pairs, 2, 4),
        in_specs=[qs, q0, ks, k0, ks, qs, qs, qs, q0, q0, k0, k0],
        out_specs=[qs, ks, ks],
        out_shape=[
            jax.ShapeDtypeStruct((rows, m, width), BF),
            jax.ShapeDtypeStruct((rows, n, width), BF),
            jax.ShapeDtypeStruct((rows, n, width), BF),
        ],
        scratch_shapes=[
            pltpu.VMEM((m, 256), BF),
            pltpu.VMEM((m, 256), BF),
            pltpu.VMEM((256, n), BF),
            pltpu.VMEM((256, n), BF),
            pltpu.VMEM((n, 128), BF),
            pltpu.VMEM((128, m), BF),
            pltpu.VMEM((128, m), BF),
            pltpu.VMEM((m, n), BF),
            pltpu.VMEM((m, n), BF),
            pltpu.VMEM((m, 128), F32),
            pltpu.VMEM((128, n), F32),
            pltpu.VMEM((128, n), F32),
        ],
        compiler_params=pltpu.CompilerParams(vmem_limit_bytes=60 * MIB),
        cost_estimate=pl.CostEstimate(
            flops=40 * rows * pairs * m * n * 256,
            bytes_accessed=rows * width * (m * 12 + n * 8),
            transcendentals=rows * pairs * 2 * m * n,
        ),
        name="attend_back",
    )(q, qx, k, kx, v, o, do, l, cos_q, sin_q, cos_k, sin_k)


def frame_table(seg_lengths, frames):
    ends = jnp.cumsum(seg_lengths, axis=1)
    starts = ends - seg_lengths
    at = frames[None, :, None]
    inside = (at >= starts[:, None, :]) & (at < ends[:, None, :])
    offsets = frames[None, :] - jnp.sum(jnp.where(inside, starts[:, None, :], 0), axis=2)
    return inside.astype(F32), offsets


def rotary_tables(offsets, head_dim):
    halves = head_dim // 2
    place = jnp.arange(128, dtype=jnp.int32)
    index = (place % halves).astype(F32)
    frequency = jnp.exp(-math.log(THETA) * 2.0 * index / head_dim)
    angles = offsets.astype(F32)[..., None] * frequency
    sign = jnp.where(place % head_dim < halves, -1.0, 1.0)
    return jnp.cos(angles), jnp.sin(angles) * sign


def normalize(stream):
    center = stream - jnp.mean(stream, axis=-1, keepdims=True)
    inv_std = lax.rsqrt(jnp.mean(center * center, axis=-1, keepdims=True) + EPS)
    return (center * inv_std, inv_std)


def normalize_back(normed, inv_std, upstream):
    return inv_std * (
        upstream
        - jnp.mean(upstream, axis=-1, keepdims=True)
        - normed * jnp.mean(upstream * normed, axis=-1, keepdims=True)
    )


def shards(
    noisy_mel, cond_mel, text_feat, time_embed, seg_lengths, audio_drop, text_drop, w_in, b_in,
    ada_w, ada_b, w_qkv, b_qkv, w_out, b_out, w_up, b_up, w_down, b_down, cotangent,
):
    rows, span, mel = noisy_mel.shape
    model = w_qkv.shape[0]
    half = model // 2
    head_dim = model // HEADS
    frames = rows * span
    core, sx = lax.axis_index("core"), lax.axis_index("sx")
    chips = lax.axis_size("sx")
    seq = chips * 2
    seq_index = sx * 2 + core
    core_arg = core.astype(jnp.int32).reshape(1)
    as_row = lambda v: v.astype(F32).reshape(1, -1)

    ramp = jnp.arange(span, dtype=jnp.int32)

    def chip_frames(chip):
        return jnp.concatenate([(chip * 2 + core) * span + ramp, (chip * 2 + 1 - core) * span + ramp])

    member, _ = frame_table(seg_lengths, seq_index * span + ramp)
    keep_audio = 1.0 - jnp.einsum("rcs,rs->rc", member, audio_drop.astype(F32))
    keep_text = 1.0 - jnp.einsum("rcs,rs->rc", member, text_drop.astype(F32))
    frame_valid = 1.0 - member[:, :, -1]
    inputs = jnp.concatenate(
        [
            noisy_mel,
            cond_mel * keep_audio[..., None].astype(BF),
            text_feat * keep_text[..., None].astype(BF),
        ],
        axis=2,
    )
    inputs_local = jnp.concatenate([inputs, flip(inputs, "core", 1)], axis=1)
    far = []
    for t in range(1, chips):
        block = shift(inputs, "sx", -t)
        far += [block, flip(block, "core", 1)]
    inputs_far = jnp.concatenate(far, axis=1)

    time_float = time_embed.astype(F32)
    time_act = jax.nn.silu(time_float).astype(BF)
    embedding = dot_nn(time_act, ada_w) + ada_b.astype(F32)
    shift_one, scale_one, gate_one, shift_two, scale_two, gate_two = [
        part[:, None, :] for part in jnp.split(embedding, 6, axis=1)
    ]

    def tables(frame_ids):
        inside, offsets = frame_table(seg_lengths, frame_ids)
        cos, sin = rotary_tables(offsets, head_dim)
        pad = jnp.zeros(inside.shape[:2] + (128 - inside.shape[2],), F32)
        return jnp.concatenate([inside, pad], axis=2), cos, sin

    inside_near, cos_near, sin_near = tables(chip_frames(sx))
    inside_far, cos_far, sin_far = tables(
        jnp.concatenate([chip_frames((sx + t) % chips) for t in range(1, chips)])
    )
    segs = seg_lengths.shape[1]
    lanes = jnp.arange(128)
    qx = jnp.where(lanes < segs, 1.0 - inside_near, 0.0).astype(BF)
    kx = (MASKED * jnp.concatenate([inside_far, inside_near], axis=1)).astype(BF)
    cos_all = jnp.concatenate([cos_far, cos_near], axis=1)
    sin_all = jnp.concatenate([sin_far, sin_near], axis=1)

    bq = as_row(b_qkv)
    mod_near, q, k_near, v_near = front(
        core_arg, inputs_local, w_in, as_row(b_in), shift_one, scale_one, w_qkv, bq,
        cos_near, sin_near, ("q", "k", "v"),
    )
    mod_far, k_far, v_far = front(
        core_arg, inputs_far, w_in, as_row(b_in), shift_one, scale_one, w_qkv, bq,
        cos_far, sin_far, ("k", "v"),
    )
    k = jnp.concatenate([k_far, k_near], axis=1)
    v = jnp.concatenate([v_far, v_near], axis=1)
    o, lse = attend(q, qx, k, kx, v)

    o_other = flip(o[:, span:], "core", 1)
    mixed = jnp.concatenate([o[:, :span], o_other], axis=2).reshape(frames, model)
    own = lax.dynamic_slice_in_dim
    w_out_two = w_out.reshape(2, half, model)
    w_out_turned = jnp.concatenate([pick(w_out_two, core), pick(w_out_two, 1 - core)], axis=0)
    resid_zero = (
        dot_nn(inputs.reshape(frames, -1), w_in) + b_in.astype(F32)
    ).reshape(rows, span, model)
    branch = (dot_nn(mixed, w_out_turned) + b_out.astype(F32)).reshape(rows, span, model)
    resid_one = resid_zero + gate_one * branch * frame_valid[..., None]
    normed_two, inv_two = normalize(resid_one)
    mod_two = (normed_two * (1.0 + scale_two) + shift_two).astype(BF).reshape(frames, model)
    hidden = dot_nn(mod_two, w_up) + b_up.astype(F32)
    activated = jax.nn.gelu(hidden, approximate=True).astype(BF)
    ff_out = (dot_nn(activated, w_down) + b_down.astype(F32)).reshape(rows, span, model)
    result = (resid_one + gate_two * ff_out).astype(BF)

    grad_out = cotangent.astype(F32)
    d_gate_two = jnp.sum(grad_out * ff_out, axis=1)
    d_ff = (grad_out * gate_two).astype(BF).reshape(frames, model)
    w_down_grad = total_grad(dot_tn(activated, d_ff).astype(BF))
    b_down_grad = jnp.sum(d_ff.astype(F32), axis=0)
    grad_act = dot_nt(d_ff, w_down)
    _, gelu_pull = jax.vjp(lambda pre: jax.nn.gelu(pre, approximate=True), hidden)
    d_hidden = gelu_pull(grad_act)[0].astype(BF)
    w_up_grad = total_grad(dot_tn(mod_two, d_hidden).astype(BF))
    b_up_grad = jnp.sum(d_hidden.astype(F32), axis=0)
    d_mod_two = dot_nt(d_hidden, w_up).reshape(rows, span, model)
    d_shift_two = jnp.sum(d_mod_two, axis=1)
    d_scale_two = jnp.sum(d_mod_two * normed_two, axis=1)
    d_resid_one = grad_out + normalize_back(normed_two, inv_two, d_mod_two * (1.0 + scale_two))
    d_gate_one = jnp.sum(d_resid_one * branch * frame_valid[..., None], axis=1)
    d_branch = (
        (d_resid_one * gate_one * frame_valid[..., None]).astype(BF).reshape(frames, model)
    )
    w_out_turned_grad = dot_tn(mixed, d_branch).astype(BF).reshape(2, half, model)
    w_out_grad = total_grad(
        jnp.concatenate([pick(w_out_turned_grad, core), pick(w_out_turned_grad, 1 - core)], axis=0)
    )
    b_out_grad = jnp.sum(d_branch.astype(F32), axis=0)
    d_mixed = dot_nt(d_branch, w_out_turned).astype(BF).reshape(rows, span, model)
    d_o = jnp.concatenate([d_mixed[..., :half], flip(d_mixed[..., half:], "core", 1)], axis=1)

    dq, dk, dv = attend_back(
        q, qx, k, kx, v, o, d_o, lse, cos_near, sin_near, cos_all, sin_all
    )

    chip_span = 2 * span
    far_span = k_far.shape[1]
    w_parts = w_qkv.reshape(model, 3, 2, half)
    w_mine = lax.dynamic_index_in_dim(w_parts, core, 2, keepdims=False)
    mod_all = jnp.concatenate([mod_far, mod_near], axis=1).reshape(-1, model)
    flat = lambda a: a.reshape(-1, a.shape[-1])
    w_q_grad = dot_tn(flat(mod_near), flat(dq)).astype(BF)
    w_k_grad = dot_tn(mod_all, flat(dk)).astype(BF)
    w_v_grad = dot_tn(mod_all, flat(dv)).astype(BF)
    near = jnp.concatenate([dq, dk[:, far_span:], dv[:, far_span:]], axis=2)
    d_mod_near = dot_nt(flat(near), w_mine.reshape(model, 3 * half)).astype(BF)
    far_grads = jnp.concatenate([dk[:, :far_span], dv[:, :far_span]], axis=2)
    d_mod_far = dot_nt(flat(far_grads), w_mine[:, 1:].reshape(model, 2 * half)).astype(BF)
    d_mod_near = d_mod_near.reshape(rows, 2, span, model)
    d_mod_far = d_mod_far.reshape(rows, chips - 1, 2, span, model)
    far_sum = add_bf16(d_mod_far[:, :, 0], flip(d_mod_far[:, :, 1], "core", 1))
    d_mod_one = d_mod_near[:, 0].astype(F32) + flip(d_mod_near[:, 1], "core", 1).astype(F32)
    for t in range(1, chips):
        d_mod_one = d_mod_one + shift(far_sum[:, t - 1], "sx", t).astype(F32)

    stacked = jnp.stack([w_q_grad, w_k_grad, w_v_grad], axis=0)
    stacked = stacked.reshape(3, chips, 2, model // seq, half)
    to_other = flip(lax.dynamic_index_in_dim(stacked, 1 - core, 2, keepdims=False), "core", 1)
    to_own = lax.dynamic_index_in_dim(stacked, core, 2, keepdims=False)
    low = core == 0
    both = jnp.stack([jnp.where(low, to_own, to_other), jnp.where(low, to_other, to_own)], axis=3)
    part = jnp.transpose(both, (1, 2, 0, 3, 4)).reshape(chips, model // seq, 3 * model)
    w_qkv_grad = pick(part, sx)
    for t in range(1, chips):
        w_qkv_grad = add_bf16(w_qkv_grad, shift(pick(part, (sx + t) % chips), "sx", t))
    w_qkv_grad = sum_rows(w_qkv_grad)
    b_mine = jnp.stack(
        [jnp.sum(flat(a).astype(F32), axis=0) for a in (dq, dk, dv)], axis=0
    )
    gap = jnp.zeros_like(b_mine)
    b_qkv_grad = jnp.stack([jnp.where(low, b_mine, gap), jnp.where(low, gap, b_mine)], axis=1)

    normed_one, inv_one = normalize(resid_zero)
    d_shift_one = jnp.sum(d_mod_one, axis=1)
    d_scale_one = jnp.sum(d_mod_one * normed_one, axis=1)
    d_resid_zero = (
        (d_resid_one + normalize_back(normed_one, inv_one, d_mod_one * (1.0 + scale_one)))
        .astype(BF)
        .reshape(frames, model)
    )
    w_in_grad = total_grad(dot_tn(d_resid_zero, inputs.reshape(frames, -1)).astype(BF)).T
    b_in_grad = jnp.sum(d_resid_zero.astype(F32), axis=0)
    d_inputs = dot_nt(d_resid_zero, w_in).reshape(rows, span, -1)
    noisy_grad = d_inputs[..., :mel]
    cond_grad = d_inputs[..., mel : 2 * mel] * keep_audio[..., None]
    text_grad = d_inputs[..., 2 * mel :] * keep_text[..., None]

    emb_partial = jnp.concatenate(
        [d_shift_one, d_scale_one, d_gate_one, d_shift_two, d_scale_two, d_gate_two], axis=1
    )
    bias_sizes = [model, 3 * model, model, w_up.shape[1], model]
    biases = jnp.concatenate(
        [b_in_grad, b_qkv_grad.reshape(-1), b_out_grad, b_up_grad, b_down_grad]
    )
    vector = jnp.concatenate([emb_partial.reshape(-1), biases])
    for axis in ("core", "sx"):
        vector = sum_small(vector, axis)
    emb_size = rows * 6 * model
    d_embedding = vector[:emb_size].reshape(rows, 6 * model).astype(BF)
    biases = vector[emb_size:]
    for axis in ("ry", "rz"):
        biases = sum_small(biases, axis)
    pieces, at = [], 0
    for size in bias_sizes:
        share = size // seq
        pieces.append(lax.dynamic_slice_in_dim(biases, at + seq_index * share, share, 0))
        at += size
    b_in_grad, b_qkv_grad, b_out_grad, b_up_grad, b_down_grad = pieces

    _, silu_pull = jax.vjp(jax.nn.silu, time_float)
    time_grad = silu_pull(dot_nt(d_embedding, ada_w))[0]
    width_share = model // seq
    emb_share = 6 * model // seq
    act_share = lax.dynamic_slice_in_dim(time_act, seq_index * width_share, width_share, 1)
    joined = jnp.concatenate([act_share, d_embedding], axis=1)
    for axis in ("ry", "rz"):
        joined = gather_small(joined, axis)
    all_act, all_emb = joined[:, :width_share], joined[:, width_share:]
    ada_w_grad = dot_tn(all_act, all_emb)
    ada_b_grad = lax.dynamic_slice_in_dim(
        jnp.sum(all_emb.astype(F32), axis=0), seq_index * emb_share, emb_share, 0
    )
    return (
        result,
        noisy_grad,
        cond_grad,
        text_grad,
        time_grad,
        w_in_grad.astype(F32),
        b_in_grad,
        ada_w_grad,
        ada_b_grad,
        w_qkv_grad.astype(F32),
        b_qkv_grad,
        w_out_grad.astype(F32),
        b_out_grad,
        w_up_grad.astype(F32),
        b_up_grad,
        w_down_grad.astype(F32),
        b_down_grad,
    )


def solution(mesh):
    rows, seq = mesh.shape["rows"], mesh.shape["seq"]
    mesh = Mesh(mesh.devices.reshape(rows // 2, 2, seq // 2, 2), ("rz", "ry", "sx", "core"))
    r, s = ("rz", "ry"), ("sx", "core")
    in_specs = (
        (P(r, s, None),) * 3 + (P(r, None),) * 4 + (P(),) * 12 + (P(r, s, None),)
    )
    out_specs = (
        (P(r, s, None),) * 4
        + (P(r, None), P(None, s), P(s))
        + (P(s, None), P(s)) * 5
    )
    return jax.shard_map(shards, mesh=mesh, in_specs=in_specs, out_specs=out_specs, check_vma=False)
```

```python
import functools
import math

import jax
import jax.numpy as jnp
from jax import lax
from jax.experimental import pallas as pl
from jax.experimental.pallas import tpu as pltpu
from jax.sharding import Mesh, PartitionSpec as P

HEADS = 16
EPS = 1e-06
THETA = 10000.0
MASKED = -1e30
F32 = jnp.float32
BF = jnp.bfloat16
MIB = 2**20
QUICK = pl.CostEstimate(flops=10**8, bytes_accessed=10**5, transcendentals=0)


def dot_nn(a, b):
    return jnp.dot(a, b, preferred_element_type=F32)


def dot_tn(a, b):
    return lax.dot_general(a, b, (((0,), (0,)), ((), ())), preferred_element_type=F32)


def dot_nt(a, b):
    return lax.dot_general(a, b, (((1,), (1,)), ((), ())), preferred_element_type=F32)


def shift(v, axis, step):
    size = lax.axis_size(axis)
    return lax.ppermute(v, axis, [(i, (i + step) % size) for i in range(size)])


def flip(v, axis, bit):
    size = lax.axis_size(axis)
    return lax.ppermute(v, axis, [(i, i ^ bit) for i in range(size)])


def bits(axis):
    size = lax.axis_size(axis)
    assert size & (size - 1) == 0
    return [1 << b for b in range(size.bit_length() - 1)]


def sum_small(v, axis):
    for bit in bits(axis):
        v = v + flip(v, axis, bit)
    return v


def gather_small(v, axis):
    for bit in bits(axis):
        v = jnp.concatenate([v, flip(v, axis, bit)], axis=0)
    return v


def pick(v, index):
    return lax.dynamic_index_in_dim(v, index, 0, keepdims=False)


def part_of(v, index, count):
    size = v.shape[0] // count
    return lax.dynamic_slice_in_dim(v, index * size, size, 0)


def total(terms):
    acc = terms[0].astype(F32)
    for term in terms[1:]:
        acc = acc + term.astype(F32)
    return acc.astype(BF)


def rows_give(terms):
    return total([part_of(t, 1 - lax.axis_index("ry"), 2) for t in terms])


def rows_mine(terms, recv):
    return total([part_of(t, lax.axis_index("ry"), 2) for t in terms] + [recv])


def rows_turn(mine):
    z, deep = lax.axis_index("rz"), lax.axis_size("rz")
    got = [shift(part_of(mine, (z + t) % deep, deep), "rz", t) for t in range(1, deep)]
    return [part_of(mine, z, deep)] + got


def rows_spread(block):
    return [shift(block, "rz", t) for t in range(lax.axis_size("rz") - 1, 0, -1)] + [block]


def rows_half(ring):
    z, deep = lax.axis_index("rz"), lax.axis_size("rz")
    ring = jnp.concatenate(ring + ring[:-1], axis=0)
    size = ring.shape[0] // (2 * deep - 1)
    return lax.dynamic_slice_in_dim(ring, (deep - 1 - z) * size, deep * size, 0)


def rows_join(mine):
    y = lax.axis_index("ry")
    recv = flip(mine, "ry", 1)
    return jnp.where(y == 0, mine, recv), jnp.where(y == 0, recv, mine)


def sum_rows(terms):
    recv = flip(rows_give(terms), "ry", 1)
    return rows_join(rows_half(rows_spread(total(rows_turn(rows_mine(terms, recv))))))


def sum_chips(blocks):
    return list(blocks[0]) + [shift(total(blocks[t]), "sx", t) for t in range(1, len(blocks))]


def turn(x, cos, sin, lane):
    partner = jnp.where(lane % 64 < 32, pltpu.roll(x, 96, 1), pltpu.roll(x, 32, 1))
    return x * cos + partner * sin


def wide_tables(angles):
    cos, sin = angles[0], angles[1]
    return (
        jnp.concatenate([cos, cos, cos, cos], axis=0).T,
        jnp.concatenate([-sin, sin, -sin, sin], axis=0).T,
    )


def front_kernel(core, x0_ref, x1_ref, win_ref, bin_ref, emb_ref, *rest, parts):
    weights = rest[: 2 * len(parts)]
    angle_ref, mod_ref = rest[2 * len(parts) : 2 * len(parts) + 2]
    outs = rest[2 * len(parts) + 2 :]
    x = jnp.where(pl.program_id(1) == 0, x0_ref[...], x1_ref[...])[:, : win_ref.shape[0]]
    cos, sin = wide_tables(angle_ref)
    resid = dot_nn(x, win_ref[...]) + bin_ref[...]
    center = resid - jnp.mean(resid, axis=1, keepdims=True)
    inv = lax.rsqrt(jnp.mean(center * center, axis=1, keepdims=True) + EPS)
    mod = (center * inv * (1.0 + emb_ref[1:2, :]) + emb_ref[0:1, :]).astype(BF)
    mod_ref[...] = mod.T
    lane = lax.broadcasted_iota(jnp.int32, (1, 128), 1)
    for n, part in enumerate(parts):
        y = dot_nn(mod, weights[2 * n][...]) + weights[2 * n + 1][...]
        if part == "v":
            outs[n][...] = y.astype(BF)
            continue
        scale = 0.125 if part == "q" else 1.0
        for t in range(0, y.shape[1], 128):
            z = turn(y[:, t : t + 128], cos, sin, lane)
            outs[n][:, t : t + 128] = (z * scale).astype(BF)


def front(core, x0, x1, w_in, b_in, emb, w_qkv, b_qkv, angles, parts):
    rows, span, width = x0.shape
    n = 2 * span
    model = w_in.shape[1]
    half = model // 2
    place = {"q": 0, "k": 1, "v": 2}
    one = pl.BlockSpec((None, span, width), lambda r, i, c: (r, 0, 0))
    frame = lambda w: pl.BlockSpec((None, span, w), lambda r, i, c: (r, i, 0))
    whole = lambda a, b: pl.BlockSpec((a, b), lambda r, i, c: (0, 0))
    w_specs, w_args = [], []
    for part in parts:
        j = place[part]
        w_specs.append(pl.BlockSpec((model, half), lambda r, i, c, j=j: (0, 2 * j + c[0])))
        w_specs.append(pl.BlockSpec((1, half), lambda r, i, c, j=j: (0, 2 * j + c[0])))
        w_args += [w_qkv, b_qkv]
    return pl.pallas_call(
        functools.partial(front_kernel, parts=parts),
        grid_spec=pltpu.PrefetchScalarGridSpec(
            num_scalar_prefetch=1,
            grid=(rows, 2),
            in_specs=[one, one, whole(*w_in.shape), whole(1, model)]
            + [pl.BlockSpec((None, 6, model), lambda r, i, c: (r, 0, 0))]
            + w_specs
            + [pl.BlockSpec((None, None, 2, 32, span), lambda r, i, c: (r, i, 0, 0, 0))],
            out_specs=[pl.BlockSpec((None, None, model, span), lambda r, i, c: (r, i, 0, 0))]
            + [frame(half)] * len(parts),
        ),
        out_shape=[jax.ShapeDtypeStruct((rows, 2, model, span), BF)]
        + [jax.ShapeDtypeStruct((rows, n, half), BF)] * len(parts),
        compiler_params=pltpu.CompilerParams(vmem_limit_bytes=56 * MIB),
        cost_estimate=QUICK,
        name="front",
    )(core, x0, x1, w_in, b_in, emb, *w_args, angles)


def mid_kernel(
    core, x_ref, om_ref, oo_ref, g_ref, valid_ref, emb_ref,
    win_ref, bin_ref, wom_ref, woo_ref, bout_ref, wup_ref, bup_ref, wdn_ref, bdn_ref,
    out_ref, dres_ref, dom_ref, doo_ref, mod_ref, act_ref, dhid_ref, dff_ref, dbr_ref,
    sums_ref, bupg_ref, slope_ref,
):
    hidden_width = wup_ref.shape[1]
    step = 512
    gate_one, shift_two = emb_ref[2:3, :], emb_ref[3:4, :]
    scale_two, gate_two = emb_ref[4:5, :], emb_ref[5:6, :]
    total = lambda v: jnp.sum(v, axis=0, keepdims=True)
    mean = lambda v: jnp.mean(v, axis=1, keepdims=True)
    resid = dot_nn(x_ref[:, : win_ref.shape[0]], win_ref[...]) + bin_ref[...]
    branch = dot_nn(om_ref[...], wom_ref[...]) + dot_nn(oo_ref[...], woo_ref[...]) + bout_ref[...]
    branch = branch * valid_ref[...]
    resid = resid + gate_one * branch
    center = resid - mean(resid)
    inv = lax.rsqrt(mean(center * center) + EPS)
    normed = center * inv
    mod = (normed * (1.0 + scale_two) + shift_two).astype(BF)
    mod_ref[...] = mod
    ff = None
    for j in range(0, hidden_width, step):
        h = dot_nn(mod, wup_ref[:, j : j + step]) + bup_ref[:, j : j + step]
        square = h * h
        t = jnp.tanh(h * (0.7978845608028654 + 0.035677408136300125 * square))
        up = 0.5 + 0.5 * t
        act = (h * up).astype(BF)
        act_ref[:, j : j + step] = act
        slope = up + h * (0.5 - 0.5 * t * t) * (0.7978845608028654 + 0.10703222440890037 * square)
        slope_ref[:, j : j + step] = slope.astype(BF)
        part = dot_nn(act, wdn_ref[j : j + step, :])
        ff = part if ff is None else ff + part
    ff = ff + bdn_ref[...]
    out_ref[...] = (resid + gate_two * ff).astype(BF)
    g = g_ref[...].astype(F32)
    sums_ref[0:1, :] = total(g * ff)
    d_ff = (g * gate_two).astype(BF)
    dff_ref[...] = d_ff
    sums_ref[1:2, :] = total(d_ff.astype(F32))
    d_mod = None
    for j in range(0, hidden_width, step):
        d_act = dot_nt(d_ff, wdn_ref[j : j + step, :])
        d_hid = (d_act * slope_ref[:, j : j + step].astype(F32)).astype(BF)
        dhid_ref[:, j : j + step] = d_hid
        bupg_ref[:, j : j + step] = total(d_hid.astype(F32))
        part = dot_nt(d_hid, wup_ref[:, j : j + step])
        d_mod = part if d_mod is None else d_mod + part
    sums_ref[2:3, :] = total(d_mod)
    sums_ref[3:4, :] = total(d_mod * normed)
    u = d_mod * (1.0 + scale_two)
    d_res = g + inv * (u - mean(u) - normed * mean(u * normed))
    dres_ref[...] = d_res
    sums_ref[4:5, :] = total(d_res * branch)
    d_branch = (d_res * gate_one * valid_ref[...]).astype(BF)
    dbr_ref[...] = d_branch
    sums_ref[5:6, :] = total(d_branch.astype(F32))
    dom_ref[...] = dot_nt(d_branch, wom_ref[...]).astype(BF)
    doo_ref[...] = dot_nt(d_branch, woo_ref[...]).astype(BF)


def mid(core, x, o_mine, o_other, g, valid, emb, w_in, b_in, w_out, b_out, w_up, b_up, w_down, b_down):
    rows, span, width = x.shape
    model, hidden = w_up.shape
    half = model // 2
    frame = lambda w: pl.BlockSpec((None, span, w), lambda r, c: (r, 0, 0))
    whole = lambda a, b: pl.BlockSpec(
        (a, b), lambda r, c: (0, 0), pipeline_mode=pl.Buffered(buffer_count=1)
    )
    out_half = lambda f: pl.BlockSpec(
        (half, model), lambda r, c: (f(c[0]), 0), pipeline_mode=pl.Buffered(buffer_count=1)
    )
    shape = lambda w, t: jax.ShapeDtypeStruct((rows, span, w), t)
    return pl.pallas_call(
        mid_kernel,
        grid_spec=pltpu.PrefetchScalarGridSpec(
            num_scalar_prefetch=1,
            grid=(rows,),
            in_specs=[
                frame(width), frame(half), frame(half), frame(model), frame(1),
                pl.BlockSpec((None, 6, model), lambda r, c: (r, 0, 0)),
                whole(*w_in.shape), whole(1, model),
                out_half(lambda c: c), out_half(lambda c: 1 - c), whole(1, model),
                whole(model, hidden), whole(1, hidden), whole(hidden, model), whole(1, model),
            ],
            out_specs=[
                frame(model), frame(model), frame(half), frame(half), frame(model),
                frame(hidden), frame(hidden), frame(model), frame(model),
                pl.BlockSpec((None, 8, model), lambda r, c: (r, 0, 0)),
                pl.BlockSpec((None, 1, hidden), lambda r, c: (r, 0, 0)),
            ],
            scratch_shapes=[pltpu.VMEM((span, hidden), BF)],
        ),
        out_shape=[
            shape(model, BF), shape(model, F32), shape(half, BF), shape(half, BF), shape(model, BF),
            shape(hidden, BF), shape(hidden, BF), shape(model, BF), shape(model, BF),
            jax.ShapeDtypeStruct((rows, 8, model), F32),
            jax.ShapeDtypeStruct((rows, 1, hidden), F32),
        ],
        compiler_params=pltpu.CompilerParams(vmem_limit_bytes=62 * MIB),
        cost_estimate=QUICK,
        name="mid",
    )(core, x, o_mine, o_other, g, valid, emb, w_in, b_in, w_out, w_out, b_out, w_up, b_up, w_down, b_down)


def outer_kernel(core, mod_ref, act_ref, om_ref, oo_ref, dhid_ref, dff_ref, dbr_ref, out_ref):
    step = pl.program_id(0)
    seq, model = out_ref.shape[0], out_ref.shape[2]
    r = model // seq

    def put(left, right, size, first, at):
        product = dot_nn(left.T, right).astype(BF)
        for n in range(model // size):
            out_ref[first + n, at : at + size, :] = product[n * size : (n + 1) * size]

    @pl.when(step < 2)
    def _():
        product = dot_nn(mod_ref[...].T, dhid_ref[...]).astype(BF)
        for j in range(2):
            @pl.when(step == j)
            def _():
                for n in range(seq):
                    out_ref[n, j * r : (j + 1) * r, :] = product[n * r : (n + 1) * r]

    @pl.when((step >= 2) & (step < 4))
    def _():
        product = dot_nn(act_ref[...].T, dff_ref[...]).astype(BF)
        for j in range(2):
            @pl.when(step == 2 + j)
            def _():
                for n in range(seq // 2):
                    out_ref[j * (seq // 2) + n, 2 * r : 4 * r, :] = product[
                        n * 2 * r : (n + 1) * 2 * r
                    ]

    @pl.when(step == 4)
    def _():
        mine, other = om_ref[...], oo_ref[...]
        low = core[0] == 0
        mixed = jnp.concatenate([jnp.where(low, mine, other), jnp.where(low, other, mine)], axis=1)
        product = dot_nn(mixed.T, dbr_ref[...]).astype(BF)
        for n in range(seq):
            out_ref[n, 4 * r :, :] = product[n * r : (n + 1) * r]


def outer(core, mod, act, o_mine, o_other, d_hid, d_ff, d_br):
    n, model = mod.shape
    seq = lax.axis_size("sx") * 2
    low = lambda i: jnp.minimum(i, 1)
    high = lambda i: jnp.clip(i - 2, 0, 1)
    once = lambda w: pl.BlockSpec((n, w), lambda i, c: (0, 0))
    shape = (seq, 5 * model // seq, model)
    return pl.pallas_call(
        outer_kernel,
        grid_spec=pltpu.PrefetchScalarGridSpec(
            num_scalar_prefetch=1,
            grid=(5,),
            in_specs=[
                once(model), pl.BlockSpec((n, model), lambda i, c: (0, high(i))),
                once(model // 2), once(model // 2),
                pl.BlockSpec((n, model), lambda i, c: (0, low(i))), once(model), once(model),
            ],
            out_specs=pl.BlockSpec(shape, lambda i, c: (0, 0, 0)),
        ),
        out_shape=jax.ShapeDtypeStruct(shape, BF),
        compiler_params=pltpu.CompilerParams(vmem_limit_bytes=60 * MIB),
        cost_estimate=QUICK,
        name="outer",
    )(core, mod, act, o_mine, o_other, d_hid, d_ff, d_br)


def qkv_outer_kernel(place, *refs, far):
    near_ref, dq_ref, dk_ref, dv_ref = refs[:4]
    far_refs = refs[4 : 4 + 3 * far]
    keep_ref, give_ref = refs[-2:]
    chips, _, rows, width = keep_ref.shape
    span = near_ref.shape[2]
    acc_q, acc = None, None
    add = lambda a, b: b if a is None else a + b
    for i in range(2):
        cut = slice(i * span, (i + 1) * span)
        both = jnp.concatenate([dk_ref[cut, :], dv_ref[cut, :]], axis=1)
        acc_q = add(acc_q, dot_nn(near_ref[i], dq_ref[cut, :]))
        acc = add(acc, dot_nn(near_ref[i], both))
    for f in range(far):
        mod_ref, dkf_ref, dvf_ref = far_refs[3 * f : 3 * f + 3]
        for i in range(2):
            cut = slice(i * span, (i + 1) * span)
            both = jnp.concatenate([dkf_ref[cut, :], dvf_ref[cut, :]], axis=1)
            acc = add(acc, dot_nn(mod_ref[i], both))
    parts = [acc_q.astype(BF), acc[:, :width].astype(BF), acc[:, width:].astype(BF)]
    for side in range(2):
        for out_ref, core in ((keep_ref, side), (give_ref, 1 - side)):
            @pl.when(place[1] == core)
            def _():
                for n in range(side, 2 * chips, 2):
                    chip = (n // 2 + chips - place[0]) % chips
                    for j, part in enumerate(parts):
                        out_ref[chip, j] = part[n * rows : (n + 1) * rows]


def qkv_outer(place, mod_near, dq, dk, dv, far):
    model = mod_near.shape[1]
    width = dq.shape[1]
    chips = lax.axis_size("sx")
    shape = (chips, 3, model // (2 * chips), width)
    args = [mod_near, dq, dk, dv]
    for item in far:
        args += list(item)
    return pl.pallas_call(
        functools.partial(qkv_outer_kernel, far=len(far)),
        grid_spec=pltpu.PrefetchScalarGridSpec(
            num_scalar_prefetch=1,
            grid=(1,),
            in_specs=[
                pl.BlockSpec(a.shape, lambda i, c, n=a.ndim: (0,) * n) for a in args
            ],
            out_specs=[pl.BlockSpec(shape, lambda i, c: (0,) * 4)] * 2,
        ),
        out_shape=[jax.ShapeDtypeStruct(shape, BF)] * 2,
        compiler_params=pltpu.CompilerParams(vmem_limit_bytes=60 * MIB),
        cost_estimate=QUICK,
        name="qkv_outer",
    )(place, *args)


def d_mod_kernel(core, *refs, parts):
    acc, at = None, 0
    for n, count in enumerate(parts):
        left = jnp.concatenate([ref[...] for ref in refs[at : at + count]], axis=1)
        part = dot_nt(left, refs[sum(parts) + n][...])
        acc = part if acc is None else acc + part
        at += count
    mine_ref, other_ref = refs[-2:]

    @pl.when(pl.program_id(1) % 2 == 0)
    def _():
        mine_ref[...] = acc.astype(BF)

    @pl.when(pl.program_id(1) % 2 == 1)
    def _():
        other_ref[...] = acc.astype(BF)


def d_mod(core, grads, w_qkv, span):
    arrays = [a for _, g in grads for a in g]
    rows, n = arrays[0].shape[:2]
    model = w_qkv.shape[0]
    half = model // 2
    specs = [pl.BlockSpec((None, span, a.shape[2]), lambda r, i, c: (r, i, 0)) for a in arrays]
    specs += [
        pl.BlockSpec((model, half), lambda r, i, c, j=j: (0, 2 * j + c[0])) for j, _ in grads
    ]
    out = pl.BlockSpec((None, span, model), lambda r, i, c: (r, 0, 0))
    return pl.pallas_call(
        functools.partial(d_mod_kernel, parts=tuple(len(g) for _, g in grads)),
        grid_spec=pltpu.PrefetchScalarGridSpec(
            num_scalar_prefetch=1,
            grid=(rows, n // span),
            in_specs=specs,
            out_specs=[out, out],
        ),
        out_shape=[jax.ShapeDtypeStruct((rows, span, model), BF)] * 2,
        compiler_params=pltpu.CompilerParams(vmem_limit_bytes=48 * MIB),
        cost_estimate=QUICK,
        name="d_mod",
    )(core, *arrays, *[w_qkv] * len(grads))


def tail_kernel(place, *refs, far, mel):
    x_ref, dres_ref, emb_ref, keep_ref, win_ref, bin_ref, near_ref, recv_ref = refs[:8]
    far_refs = refs[8 : 8 + far]
    noisy_ref, cond_ref, text_ref, keep_out, send_out, sums_ref, turned = refs[8 + far :]
    total = lambda v: jnp.sum(v, axis=0, keepdims=True)
    mean = lambda v: jnp.mean(v, axis=1, keepdims=True)
    width = win_ref.shape[0]
    resid = dot_nn(x_ref[:, :width], win_ref[...]) + bin_ref[...]
    center = resid - mean(resid)
    inv = lax.rsqrt(mean(center * center) + EPS)
    normed = center * inv
    d = near_ref[...].astype(F32) + recv_ref[...].astype(F32)
    for ref in far_refs:
        d = d + ref[...].astype(F32)
    sums_ref[0:1, :] = total(d)
    sums_ref[1:2, :] = total(d * normed)
    u = d * (1.0 + emb_ref[1:2, :])
    d_res = (dres_ref[...] + inv * (u - mean(u) - normed * mean(u * normed))).astype(BF)
    sums_ref[2:3, :] = total(d_res.astype(F32))
    turned[...] = d_res.T
    chips, rows = keep_out.shape[0], keep_out.shape[1]
    for t in range(chips):
        block = ((place[0] + t) % chips) * 2
        for out, core in ((send_out, 1 - place[1]), (keep_out, place[1])):
            at = pl.ds(pl.multiple_of((block + core) * rows, rows), rows)
            out[t] = dot_nn(turned[at, :], x_ref[...]).astype(BF)
    d_in = dot_nt(d_res, win_ref[...])
    noisy_ref[...] = d_in[:, :mel]
    cond_ref[...] = d_in[:, mel : 2 * mel] * keep_ref[:, 0:1]
    text_ref[...] = d_in[:, 2 * mel : width] * keep_ref[:, 1:2]


def tail(place, x, d_res, emb, keep, w_in, b_in, near, recv, far, mel):
    rows, span, width = x.shape
    model = w_in.shape[1]
    chips = lax.axis_size("sx")
    block = model // (2 * chips)
    frame = lambda w: pl.BlockSpec((None, span, w), lambda r, c: (r, 0, 0))
    whole = lambda a, b: pl.BlockSpec((a, b), lambda r, c: (0, 0))
    blocks = pl.BlockSpec((None, chips, block, width), lambda r, c: (r, 0, 0, 0))
    shape = lambda w: jax.ShapeDtypeStruct((rows, span, w), F32)
    return pl.pallas_call(
        functools.partial(tail_kernel, far=len(far), mel=mel),
        grid_spec=pltpu.PrefetchScalarGridSpec(
            num_scalar_prefetch=1,
            grid=(rows,),
            in_specs=[
                frame(width), frame(model), pl.BlockSpec((None, 6, model), lambda r, c: (r, 0, 0)),
                frame(2), whole(*w_in.shape), whole(1, model), frame(model), frame(model),
            ] + [frame(model)] * len(far),
            out_specs=[
                frame(mel), frame(mel), frame(w_in.shape[0] - 2 * mel), blocks, blocks,
                pl.BlockSpec((None, 8, model), lambda r, c: (r, 0, 0)),
            ],
            scratch_shapes=[pltpu.VMEM((model, span), BF)],
        ),
        out_shape=[
            shape(mel), shape(mel), shape(w_in.shape[0] - 2 * mel),
            jax.ShapeDtypeStruct((rows, chips, block, width), BF),
            jax.ShapeDtypeStruct((rows, chips, block, width), BF),
            jax.ShapeDtypeStruct((rows, 8, model), F32),
        ],
        compiler_params=pltpu.CompilerParams(vmem_limit_bytes=60 * MIB),
        cost_estimate=QUICK,
        name="tail",
    )(place, x, d_res, emb, keep, w_in, b_in, near, recv, *far)


def rows_of(refs, start, stop):
    parts, at = [], 0
    for ref in refs:
        size = ref.shape[0]
        lo, hi = max(start - at, 0), min(stop - at, size)
        if lo < hi:
            parts.append(ref[lo:hi, :])
        at += size
    return parts[0] if len(parts) == 1 else jnp.concatenate(parts, axis=0)


def attend_kernel(
    flag, q_ref, qx_ref, kf_ref, kn_ref, kxf_ref, kxn_ref, vf_ref, vn_ref,
    o_mine_ref, o_other_ref, l_ref, s_ref, m_ref, acc_ref,
):
    frames = s_ref.shape[1]
    span = o_mine_ref.shape[0]
    lane = lax.broadcasted_iota(jnp.int32, (1, 128), 1)
    zero = jnp.zeros((), BF)
    step = 256 if frames % 256 == 0 else frames
    apart = lambda n: pl.when(flag[0] >= -n)
    for h in range(2):
        mine = (lane // 64) == h

        @apart(2 * h)
        def _():
            q2 = jnp.concatenate([q_ref[...], qx_ref[...]], axis=1)
            top = None
            for c in range(0, frames, step):
                keys = jnp.where(mine, rows_of((kf_ref, kn_ref), c, c + step), zero)
                labels = rows_of((kxf_ref, kxn_ref), c, c + step)
                s = dot_nt(q2, jnp.concatenate([keys, labels], axis=1))
                s_ref[:, c : c + step] = s
                for t in range(0, step, 128):
                    part = s[:, t : t + 128]
                    top = part if top is None else jnp.maximum(top, part)
            m_ref[...] = jnp.broadcast_to(jnp.max(top, axis=1, keepdims=True), m_ref.shape)

        @apart(2 * h + 1)
        def _():
            top = m_ref[:, :1]
            ones = jnp.broadcast_to(jnp.where(mine, 1.0, 0.0).astype(BF), (step, 128))
            acc = None
            for c in range(0, frames, step):
                p = jnp.exp(s_ref[:, c : c + step] - top).astype(BF)
                values = jnp.where(mine, rows_of((vf_ref, vn_ref), c, c + step), zero)
                d = dot_nn(p, jnp.concatenate([values, ones], axis=1))
                acc = d if acc is None else acc + d
            if h == 0:
                acc_ref[...] = acc
                l_ref[...] = m_ref[...]
            if h == 1:
                both = acc + acc_ref[...]
                total = both[:, 128:]
                o = (both[:, :128] / total).astype(BF)
                o_mine_ref[...] = o[:span]
                o_other_ref[...] = o[span:]
                l_ref[...] = jnp.where(mine, m_ref[...], l_ref[...]) + jnp.log(total)


def attend(core, q, qx, k_far, k_near, kx_far, kx_near, v_far, v_near):
    rows, m, width = q.shape
    span = m // 2
    far, near = k_far.shape[1], k_near.shape[1]
    n = far + near
    pairs = width // 128
    at = lambda size: pl.BlockSpec((None, size, 128), lambda r, p, c: (r, 0, p))
    once = lambda size: pl.BlockSpec((None, size, 128), lambda r, p, c: (r, 0, 0))
    return pl.pallas_call(
        attend_kernel,
        grid_spec=pltpu.PrefetchScalarGridSpec(
            num_scalar_prefetch=1,
            grid=(rows, pairs),
            in_specs=[at(m), once(m), at(far), at(near), once(far), once(near), at(far), at(near)],
            out_specs=[at(span), at(span), at(m)],
            scratch_shapes=[
                pltpu.VMEM((m, n), F32),
                pltpu.VMEM((m, 128), F32),
                pltpu.VMEM((m, 256), F32),
            ],
        ),
        out_shape=[
            jax.ShapeDtypeStruct((rows, span, width), BF),
            jax.ShapeDtypeStruct((rows, span, width), BF),
            jax.ShapeDtypeStruct((rows, m, width), F32),
        ],
        compiler_params=pltpu.CompilerParams(vmem_limit_bytes=60 * MIB),
        cost_estimate=QUICK,
        name="attend",
    )(core, q, qx, k_far, k_near, kx_far, kx_near, v_far, v_near)


def split3(x, lane, rest):
    hi = x.astype(BF).astype(F32)
    mid = (x - hi).astype(BF).astype(F32)
    low = x - hi - mid
    place = lane % 64
    return jnp.where(
        place == 8, hi, jnp.where(place == 9, mid, jnp.where(place == 10, low, rest))
    ).astype(BF)


def attend_back_kernel(
    flag, q_ref, qx_ref, kf_ref, kn_ref, kxf_ref, kxn_ref, vf_ref, vn_ref,
    om_ref, oo_ref, dom_ref, doo_ref, l_ref, angf_ref, angn_ref,
    dq_ref, dkf_ref, dkn_ref, dvf_ref, dvn_ref,
    q2, d2, k2, v2, kk, qt, dt, p_s, s_s, dq_s, dk_s, dv_s,
):
    m, n = q_ref.shape[0], kk.shape[0]
    far = kf_ref.shape[0]
    span = om_ref.shape[0]
    lane = lax.broadcasted_iota(jnp.int32, (1, 128), 1)
    zero = jnp.zeros((), BF)
    steps = [(c, min(c + 256, n)) for c in range(0, n, 256)] if n % 128 == 0 else [(0, n)]
    apart = pl.when(flag[0] >= 0)

    @apart
    def _():
        q2[:, :128] = q_ref[...]
        q2[:, 128:] = split3(l_ref[...], lane, qx_ref[...].astype(F32))
        same = (
            lax.broadcasted_iota(jnp.int32, (128, 128), 0) // 64
            == lax.broadcasted_iota(jnp.int32, (128, 128), 1) // 64
        )
        same = jnp.where(same, 1.0, 0.0).astype(BF)
        same = jnp.concatenate([same, same], axis=0)
        for at, do_ref, o_ref in ((0, dom_ref, om_ref), (span, doo_ref, oo_ref)):
            cut = slice(at, at + span)
            prod = do_ref[...].astype(F32) * o_ref[...].astype(F32)
            hi = prod.astype(BF)
            low = (prod - hi.astype(F32)).astype(BF)
            delta = dot_nn(jnp.concatenate([hi, low], axis=1), same)
            d2[cut, :128] = do_ref[...]
            d2[cut, 128:] = split3(delta, lane, jnp.zeros((span, 128), F32))
        qt[...] = q_ref[...].T
        dt[...] = d2[:, :128].T

    for h in range(2):
        mine = (lane // 64) == h
        half = slice(h * 64, (h + 1) * 64)

        @apart
        def _():
            less = (lane - 64 * h >= 8) & (lane - 64 * h < 11)
            for at, k_ref, kx_ref, v_ref in (
                (0, kf_ref, kxf_ref, vf_ref), (far, kn_ref, kxn_ref, vn_ref)
            ):
                cut = slice(at, at + k_ref.shape[0])
                keys = jnp.where(mine, k_ref[...], zero)
                kk[cut, :] = keys
                k2[:128, cut] = keys.T
                k2[128:, cut] = jnp.where(less, -1.0, kx_ref[...].astype(F32)).astype(BF).T
                v2[:128, cut] = jnp.where(mine, v_ref[...], zero).T
            v2[128:, :] = jnp.broadcast_to(jnp.where(less, -1.0, 0.0), (n, 128)).astype(BF).T

        @apart
        def _():
            for c, e in steps:
                s = dot_nn(q2[...], k2[:, c:e])
                d = dot_nn(d2[...], v2[:, c:e])
                p = jnp.exp(s)
                p_s[:, c:e] = p.astype(BF)
                s_s[:, c:e] = (p * d).astype(BF)

        @apart
        def _():
            acc = dot_nn(s_s[...], kk[...])
            if h == 0:
                dq_s[...] = acc
            if h == 1:
                cos, sin = wide_tables(angn_ref)
                dq_ref[...] = turn((dq_s[...] + acc) * 0.125, cos, -sin, lane).astype(BF)

        @apart
        def _():
            for c, e in steps:
                dk_s[half, c:e] = dot_nn(qt[half, :], s_s[:, c:e])
                dv_s[half, c:e] = dot_nn(dt[half, :], p_s[:, c:e])

    @apart
    def _():
        for at, ang_ref, dk_ref, dv_ref in (
            (0, angf_ref, dkf_ref, dvf_ref), (far, angn_ref, dkn_ref, dvn_ref)
        ):
            cut = slice(at, at + dk_ref.shape[0])
            cos, sin = ang_ref[0], ang_ref[1]
            turned = []
            for h in range(2):
                a, b = dk_s[64 * h : 64 * h + 32, cut], dk_s[64 * h + 32 : 64 * h + 64, cut]
                turned += [a * cos + b * sin, b * cos - a * sin]
            dk_ref[...] = jnp.concatenate(turned, axis=0).astype(BF).T
            dv_ref[...] = dv_s[:, cut].astype(BF).T


def attend_back(
    core, q, qx, k_far, k_near, kx_far, kx_near, v_far, v_near, o_mine, o_other, d_mine, d_other,
    lse, ang_far, ang_near, first, pairs,
):
    rows, m, width = q.shape
    span = m // 2
    far, near = k_far.shape[1], k_near.shape[1]
    n = far + near
    at = lambda size: pl.BlockSpec((None, size, 128), lambda r, p, c: (r, 0, first + p))
    out = lambda size: pl.BlockSpec((None, size, 128), lambda r, p, c: (r, 0, p))
    once = lambda size: pl.BlockSpec((None, size, 128), lambda r, p, c: (r, 0, 0))
    angle = lambda size: pl.BlockSpec((None, 2, 32, size), lambda r, p, c: (r, 0, 0, 0))
    shape = lambda size: jax.ShapeDtypeStruct((rows, size, pairs * 128), BF)
    return pl.pallas_call(
        attend_back_kernel,
        grid_spec=pltpu.PrefetchScalarGridSpec(
            num_scalar_prefetch=1,
            grid=(rows, pairs),
            in_specs=[
                at(m), once(m), at(far), at(near), once(far), once(near), at(far), at(near),
                at(span), at(span), at(span), at(span), at(m), angle(far), angle(near),
            ],
            out_specs=[out(m), out(far), out(near), out(far), out(near)],
            scratch_shapes=[
                pltpu.VMEM((m, 256), BF),
                pltpu.VMEM((m, 256), BF),
                pltpu.VMEM((256, n), BF),
                pltpu.VMEM((256, n), BF),
                pltpu.VMEM((n, 128), BF),
                pltpu.VMEM((128, m), BF),
                pltpu.VMEM((128, m), BF),
                pltpu.VMEM((m, n), BF),
                pltpu.VMEM((m, n), BF),
                pltpu.VMEM((m, 128), F32),
                pltpu.VMEM((128, n), F32),
                pltpu.VMEM((128, n), F32),
            ],
        ),
        out_shape=[shape(m), shape(far), shape(near), shape(far), shape(near)],
        compiler_params=pltpu.CompilerParams(vmem_limit_bytes=60 * MIB),
        cost_estimate=QUICK,
        name="attend_back",
    )(
        core, q, qx, k_far, k_near, kx_far, kx_near, v_far, v_near, o_mine, o_other, d_mine,
        d_other, lse, ang_far, ang_near,
    )


def frame_table(seg_lengths, frames):
    ends = jnp.cumsum(seg_lengths, axis=1)
    starts = ends - seg_lengths
    at = frames[None, :, None]
    inside = (at >= starts[:, None, :]) & (at < ends[:, None, :])
    offsets = frames[None, :] - jnp.sum(jnp.where(inside, starts[:, None, :], 0), axis=2)
    return inside.astype(F32), offsets


def rotary_angles(offsets, head_dim):
    halves = head_dim // 2
    frequency = jnp.exp(-math.log(THETA) * 2.0 * jnp.arange(halves, dtype=F32) / head_dim)
    angles = offsets.astype(F32)[:, None, :] * frequency[:, None]
    return jnp.stack([jnp.cos(angles), jnp.sin(angles)], axis=1)


def shards(
    noisy_mel, cond_mel, text_feat, time_embed, seg_lengths, audio_drop, text_drop, w_in, b_in,
    ada_w, ada_b, w_qkv, b_qkv, w_out, b_out, w_up, b_up, w_down, b_down, cotangent,
):
    rows, span, mel = noisy_mel.shape
    model = w_qkv.shape[0]
    half = model // 2
    head_dim = model // HEADS
    core, sx = lax.axis_index("core"), lax.axis_index("sx")
    chips = lax.axis_size("sx")
    seq = chips * 2
    seq_index = sx * 2 + core
    place = jnp.stack([sx, core]).astype(jnp.int32)
    core_arg = place[1:]
    as_row = lambda v: v.astype(F32).reshape(1, -1)
    flat = lambda a: a.reshape(-1, a.shape[-1])

    ramp = jnp.arange(span, dtype=jnp.int32)

    def chip_frames(chip):
        return jnp.concatenate([(chip * 2 + core) * span + ramp, (chip * 2 + 1 - core) * span + ramp])

    member, _ = frame_table(seg_lengths, seq_index * span + ramp)
    keep_audio = 1.0 - jnp.einsum("rcs,rs->rc", member, audio_drop.astype(F32))
    keep_text = 1.0 - jnp.einsum("rcs,rs->rc", member, text_drop.astype(F32))
    keep = jnp.stack([keep_audio, keep_text], axis=2)
    frame_valid = 1.0 - member[:, :, -1:]
    width = w_in.shape[0]
    inputs = jnp.concatenate(
        [
            noisy_mel,
            cond_mel * keep_audio[..., None].astype(BF),
            text_feat * keep_text[..., None].astype(BF),
            jnp.zeros((rows, span, -width % 128), BF),
        ],
        axis=2,
    )
    inputs_other = flip(inputs, "core", 1)
    far_blocks = [shift(inputs, "sx", -t) for t in range(1, chips)]

    time_float = time_embed.astype(F32)
    time_act = jax.nn.silu(time_float).astype(BF)
    embedding = (dot_nn(time_act, ada_w) + ada_b.astype(F32)).reshape(rows, 6, model)

    def tables(frame_ids):
        inside, offsets = frame_table(seg_lengths, frame_ids)
        pad = jnp.zeros(inside.shape[:2] + (128 - inside.shape[2],), F32)
        angles = rotary_angles(offsets, head_dim)
        return jnp.concatenate([inside, pad], axis=2), angles

    def two_blocks(angles):
        return jnp.moveaxis(angles.reshape(rows, 2, 32, 2, span), 3, 1)

    inside_near, ang_near = tables(chip_frames(sx))
    qx = jnp.where(jnp.arange(128) < seg_lengths.shape[1], 1.0 - inside_near, 0.0).astype(BF)
    kx_near = (MASKED * inside_near).astype(BF)
    bq, bi = as_row(b_qkv), as_row(b_in)
    mod_near, q, k_near, v_near = front(
        core_arg, inputs, inputs_other, w_in, bi, embedding, w_qkv, bq, two_blocks(ang_near),
        ("q", "k", "v"),
    )
    q, far_blocks = lax.optimization_barrier((q, far_blocks))
    far = []
    for t in range(1, chips):
        block = far_blocks[t - 1]
        inside, angles = tables(chip_frames((sx + t) % chips))
        made = front(
            core_arg, block, flip(block, "core", 1), w_in, bi, embedding, w_qkv, bq,
            two_blocks(angles), ("k", "v"),
        )
        far.append((*made, (MASKED * inside).astype(BF), angles))
    join = lambda n, axis: far[0][n] if chips == 2 else jnp.concatenate([f[n] for f in far], axis=axis)
    k_far, v_far, kx_far, ang_far = join(1, 1), join(2, 1), join(3, 1), join(4, 3)
    o_mine, o_give, lse = attend(
        core_arg, q, qx, k_far, k_near, kx_far, kx_near, v_far, v_near
    )

    o_other = flip(o_give, "core", 1)
    result, d_resid, d_o_mine, d_o_give, mod_two, act, d_hid, d_ff, d_br, sums, up_sums = mid(
        core_arg, inputs, o_mine, o_other, cotangent, frame_valid, embedding, w_in, bi,
        w_out, as_row(b_out), w_up, as_row(b_up), w_down, as_row(b_down),
    )
    d_o_other = flip(d_o_give, "core", 1)

    early = outer(
        core_arg, *[flat(a) for a in (mod_two, act, o_mine, o_other, d_hid, d_ff, d_br)]
    )
    early = lax.psum_scatter(early, ("sx", "core"), scatter_dimension=0, tiled=False)

    pairs = half // 128
    shared = [q, qx, k_far, k_near, kx_far, kx_near, v_far, v_near, o_mine, o_give, d_o_mine]
    shared += [d_o_other, lse, ang_far, ang_near]
    def far_part(far_grads):
        made = []
        for t in range(chips - 1):
            cut = slice(2 * span * t, 2 * span * (t + 1))
            grads = [(j, [a[:, cut] if chips > 2 else a for a in g]) for j, g in far_grads]
            mine, other = d_mod(core_arg, grads, w_qkv, span)
            made.append((mine, flip(other, "core", 1)))
        return made

    def outers(dq, dk_far, dk, dv_far, dv):
        pieces = []
        for r in range(rows):
            block = lambda a, t: a[r, 2 * span * t : 2 * span * (t + 1)]
            pieces.append(
                qkv_outer(
                    place, mod_near[r], dq[r], dk[r], dv[r],
                    [(far[t][0][r], block(dk_far, t), block(dv_far, t)) for t in range(chips - 1)],
                )
            )
        return pieces[0] if rows == 1 else [total(p) for p in zip(*pieces)]

    def by_chip(kept, given):
        return [
            jnp.stack([kept[t], given[t]], axis=0).reshape(-1, kept.shape[-1]) for t in range(chips)
        ]

    def send(blocks):
        return [blocks[0]] + [shift(b, "sx", t + 1) for t, b in enumerate(blocks[1:])]

    tie = lambda *trees: lax.optimization_barrier(trees)

    first_made = attend_back(core_arg, *shared, 0, pairs - 1)
    first_kept, first_given = outers(*first_made)
    first_blocks = by_chip(first_kept, flip(first_given, "core", 1))
    give = rows_give([early])
    shared, give, first_blocks = tie(shared, give, first_blocks)
    early_recv = flip(give, "ry", 1)
    first_late = send(first_blocks)
    last_made = attend_back(core_arg, *shared, pairs - 1, 1)
    last_made, early_recv, first_late = tie(last_made, early_recv, first_late)

    near_grads = [(0, [m[0] for m in (first_made, last_made)])]
    near_grads += [(j, [m[2 * j] for m in (first_made, last_made)]) for j in (1, 2)]
    far_grads = [(j, [m[2 * j - 1] for m in (first_made, last_made)]) for j in (1, 2)]
    far_parts = far_part(far_grads)
    first_late = total(first_late)
    late_give = rows_give([first_late])
    far_parts, late_give = tie(far_parts, late_give)
    far_parts = [total(p) for p in far_parts]
    early_mine = rows_mine([early], early_recv)
    last_made, far_parts, late_give, early_mine = tie(last_made, far_parts, late_give, early_mine)
    far_got = [shift(p, "sx", t + 1) for t, p in enumerate(far_parts)]
    late_recv = flip(late_give, "ry", 1)
    early = rows_turn(early_mine)
    last_kept, last_given = outers(*last_made)
    near_mine, near_give = d_mod(core_arg, near_grads, w_qkv, span)
    last_kept, last_given, near_give, far_got, early, late_recv = tie(
        last_kept, last_given, near_give, far_got, early, late_recv
    )
    near_recv = flip(near_give, "core", 1)
    last_given = flip(last_given, "core", 1)
    early = total(early)
    first_late = rows_turn(rows_mine([first_late], late_recv))
    last_blocks = by_chip(last_kept, last_given)
    near_recv, early, first_late, last_blocks = tie(near_recv, early, first_late, last_blocks)
    early = rows_spread(early)
    last_late = send(last_blocks)
    noisy_grad, cond_grad, text_grad, in_kept, in_given, in_sums = tail(
        place, inputs, d_resid, embedding, keep, w_in, bi, near_mine, near_recv, far_got, mel
    )
    in_kept, in_given, in_sums, early, first_late, last_late = tie(
        in_kept, in_given, in_sums, early, first_late, last_late
    )
    if rows > 1:
        in_kept, in_given = [jnp.sum(a.astype(F32), axis=0).astype(BF) for a in (in_kept, in_given)]
    else:
        in_kept, in_given = in_kept[0], in_given[0]

    emb_partial = jnp.stack(
        [in_sums[:, 0], in_sums[:, 1], sums[:, 4], sums[:, 2], sums[:, 3], sums[:, 0]], axis=1
    )
    over = lambda a: jnp.sum(a, axis=0)
    columns = lambda *a: sum(jnp.sum(flat(b).astype(F32), axis=0) for b in a)
    bias_mine = jnp.stack(
        [
            jnp.concatenate([columns(m[0]) for m in (first_made, last_made)]),
            jnp.concatenate([columns(m[1], m[2]) for m in (first_made, last_made)]),
            jnp.concatenate([columns(m[3], m[4]) for m in (first_made, last_made)]),
        ]
    )
    gap = jnp.zeros_like(bias_mine)
    b_qkv_grad = jnp.stack(
        [jnp.where(core == 0, bias_mine, gap), jnp.where(core == 0, gap, bias_mine)], axis=1
    )
    bias_sizes = [model, 3 * model, model, w_up.shape[1], model]
    biases = jnp.concatenate(
        [over(in_sums[:, 2]), b_qkv_grad.reshape(-1), over(sums[:, 5]), over(up_sums[:, 0]), over(sums[:, 1])]
    )
    vector = jnp.concatenate([emb_partial.reshape(-1), biases])

    in_given = flip(in_given, "core", 1)
    other = flip(vector, "core", 1)
    early = rows_half(early)
    early_other = flip(early, "ry", 1)
    first_late = rows_spread(total(first_late))
    last_late = total(last_late)
    last_give = rows_give([last_late])
    in_given, other, early, first_late[-1], last_give = tie(
        in_given, other, early, first_late[-1], last_give
    )
    in_late = sum_chips([(in_kept[t], in_given[t]) for t in range(chips)])
    vector = sum_small(vector + other, "sx")
    last_recv = flip(last_give, "ry", 1)
    first_late, last_recv = tie(first_late, last_recv)
    last_mine = rows_mine([last_late], last_recv)
    first_late = rows_half(first_late)
    in_late, vector, last_mine, first_late = tie(in_late, vector, last_mine, first_late)
    last_late = rows_turn(last_mine)
    first_other = flip(first_late, "ry", 1)
    in_late = total(in_late)
    in_recv = flip(rows_give([in_late]), "ry", 1)
    emb_size = rows * 6 * model
    d_embedding = vector[:emb_size].reshape(rows, 6 * model).astype(BF)
    biases = vector[emb_size:]
    shares, at = [], 0
    for size in bias_sizes:
        share = size // seq
        shares.append(lax.dynamic_slice_in_dim(biases, at + seq_index * share, share, 0))
        at += size
    width_share = model // seq
    act_share = lax.dynamic_slice_in_dim(time_act, seq_index * width_share, width_share, 1)
    shares = jnp.concatenate(shares)
    bias_share = shares.shape[0]
    shares = jnp.concatenate([shares[None], jnp.zeros((rows - 1, bias_share), F32)], axis=0)
    joined = jnp.concatenate([shares, act_share.astype(F32), d_embedding.astype(F32)], axis=1)
    joined = gather_small(joined, "ry")
    _, silu_pull = jax.vjp(jax.nn.silu, time_float)
    time_grad = silu_pull(dot_nt(d_embedding, ada_w))[0]
    in_recv, joined, last_late, time_grad = tie(in_recv, joined, last_late, time_grad)
    in_late = rows_turn(rows_mine([in_late], in_recv))
    joined = gather_small(joined, "rz")
    last_late = rows_spread(total(last_late))
    in_late, joined, last_late, early_other, first_other = tie(
        in_late, joined, last_late, early_other, first_other
    )
    in_late = rows_spread(total(in_late))
    last_late = rows_half(last_late)
    last_other = flip(last_late, "ry", 1)
    by_row = lambda a, b: jnp.concatenate(
        [jnp.where(lax.axis_index("ry") == 0, a, b), jnp.where(lax.axis_index("ry") == 0, b, a)],
        axis=0,
    )
    early = by_row(early, early_other)
    in_late, last_other, early = tie(in_late, last_other, early)
    late = jnp.concatenate([by_row(first_late, first_other), by_row(last_late, last_other)], axis=1)
    late = late.reshape(2, 3, model // seq, half)
    in_low, in_high = rows_join(rows_half(in_late))
    w_in_grad = jnp.concatenate([in_low, in_high], axis=0)[:, :width].astype(F32).T

    block = model // seq
    early = early.astype(F32)
    w_up_grad = jnp.concatenate([early[:block], early[block : 2 * block]], axis=1)
    w_down_grad = early[2 * block : 4 * block]
    w_out_grad = early[4 * block :]
    late = [jnp.where(core == 0, late[0], late[1]), jnp.where(core == 0, late[1], late[0])]
    w_qkv_grad = jnp.concatenate(
        [late[c][j].astype(F32) for j in range(3) for c in range(2)], axis=1
    )
    shares = jnp.sum(joined[:, :bias_share], axis=0)
    all_act = joined[:, bias_share : bias_share + width_share].astype(BF)
    all_emb = joined[:, bias_share + width_share :]
    b_in_grad, b_qkv_grad, b_out_grad, b_up_grad, b_down_grad = jnp.split(
        shares, [sum(bias_sizes[:n]) // seq for n in range(1, 5)]
    )
    ada_w_grad = dot_tn(all_act, all_emb.astype(BF))
    emb_share = 6 * model // seq
    ada_b_grad = lax.dynamic_slice_in_dim(
        jnp.sum(all_emb, axis=0), seq_index * emb_share, emb_share, 0
    )
    return (
        result,
        noisy_grad,
        cond_grad,
        text_grad,
        time_grad,
        w_in_grad,
        b_in_grad,
        ada_w_grad,
        ada_b_grad,
        w_qkv_grad,
        b_qkv_grad,
        w_out_grad,
        b_out_grad,
        w_up_grad,
        b_up_grad,
        w_down_grad,
        b_down_grad,
    )


def solution(mesh):
    rows, seq = mesh.shape["rows"], mesh.shape["seq"]
    mesh = Mesh(mesh.devices.reshape(rows // 2, 2, seq // 2, 2), ("rz", "ry", "sx", "core"))
    r, s = ("rz", "ry"), ("sx", "core")
    in_specs = (
        (P(r, s, None),) * 3 + (P(r, None),) * 4 + (P(),) * 12 + (P(r, s, None),)
    )
    out_specs = (
        (P(r, s, None),) * 4
        + (P(r, None), P(None, s), P(s))
        + (P(s, None), P(s)) * 5
    )
    return jax.shard_map(shards, mesh=mesh, in_specs=in_specs, out_specs=out_specs, check_vma=False)
```

```python
import functools
import math

import jax
import jax.numpy as jnp
from jax import lax
from jax.experimental import pallas as pl
from jax.experimental.pallas import tpu as pltpu
from jax.sharding import Mesh, PartitionSpec as P

HEADS = 16
EPS = 1e-06
THETA = 10000.0
MASKED = -1e30
F32 = jnp.float32
BF = jnp.bfloat16
MIB = 2**20
QUICK = pl.CostEstimate(flops=1, bytes_accessed=1, transcendentals=0)


def dot_nn(a, b):
    return jnp.dot(a, b, preferred_element_type=F32)


def dot_tn(a, b):
    return lax.dot_general(a, b, (((0,), (0,)), ((), ())), preferred_element_type=F32)


def dot_nt(a, b):
    return lax.dot_general(a, b, (((1,), (1,)), ((), ())), preferred_element_type=F32)


def shift(v, axis, step):
    size = lax.axis_size(axis)
    return lax.ppermute(v, axis, [(i, (i + step) % size) for i in range(size)])


def flip(v, axis, bit):
    size = lax.axis_size(axis)
    return lax.ppermute(v, axis, [(i, i ^ bit) for i in range(size)])


def gray(i):
    return i ^ (i >> 1)


def near_flip(v, axis, bit):
    size = lax.axis_size(axis)
    place = {gray(i): i for i in range(size)}
    return lax.ppermute(v, axis, [(i, place[gray(i) ^ bit]) for i in range(size)])


def bits(axis):
    size = lax.axis_size(axis)
    assert size & (size - 1) == 0
    return [1 << b for b in range(size.bit_length() - 1)]


def sum_small(v, axis):
    for bit in bits(axis):
        v = v + flip(v, axis, bit)
    return v


def gather_small(v, axis):
    for bit in bits(axis):
        v = jnp.concatenate([v, flip(v, axis, bit)], axis=0)
    return v


def pick(v, index):
    return lax.dynamic_index_in_dim(v, index, 0, keepdims=False)


def part_of(v, index, count):
    size = v.shape[0] // count
    return lax.dynamic_slice_in_dim(v, index * size, size, 0)


def total(terms):
    acc = terms[0].astype(F32)
    for term in terms[1:]:
        acc = acc + term.astype(F32)
    return acc.astype(BF)


def rows_give(terms):
    return total([part_of(t, 1 - lax.axis_index("ry"), 2) for t in terms])


def rows_mine(terms, recv):
    return total([part_of(t, lax.axis_index("ry"), 2) for t in terms] + [recv])


def side(axis, bit):
    return (gray(lax.axis_index(axis)) // bit) % 2


def give_half(v, axis, bit):
    return part_of(v, 1 - side(axis, bit), 2)


def keep_half(v, recv, axis, bit):
    return total([part_of(v, side(axis, bit), 2), recv])


def join_halves(mine, recv, axis, bit):
    low = side(axis, bit) == 0
    return jnp.concatenate([jnp.where(low, mine, recv), jnp.where(low, recv, mine)], axis=0)


def by_row(mine, recv):
    low = lax.axis_index("ry") == 0
    return jnp.concatenate([jnp.where(low, mine, recv), jnp.where(low, recv, mine)], axis=0)


def sum_chips(blocks):
    return list(blocks[0]) + [shift(total(blocks[t]), "sx", t) for t in range(1, len(blocks))]


def turn(x, cos, sin, lane):
    partner = jnp.where(lane % 64 < 32, pltpu.roll(x, 96, 1), pltpu.roll(x, 32, 1))
    return x * cos + partner * sin


def wide_tables(angles):
    cos, sin = angles[0], angles[1]
    return (
        jnp.concatenate([cos, cos, cos, cos], axis=0).T,
        jnp.concatenate([-sin, sin, -sin, sin], axis=0).T,
    )


def front_kernel(core, x0_ref, x1_ref, win_ref, bin_ref, emb_ref, *rest, parts):
    weights = rest[: 2 * len(parts)]
    angle_ref, mod_ref = rest[2 * len(parts) : 2 * len(parts) + 2]
    outs = rest[2 * len(parts) + 2 :]
    x = jnp.where(pl.program_id(1) == 0, x0_ref[...], x1_ref[...])[:, : win_ref.shape[0]]
    cos, sin = wide_tables(angle_ref)
    resid = dot_nn(x, win_ref[...]) + bin_ref[...]
    center = resid - jnp.mean(resid, axis=1, keepdims=True)
    inv = lax.rsqrt(jnp.mean(center * center, axis=1, keepdims=True) + EPS)
    mod = (center * inv * (1.0 + emb_ref[1:2, :]) + emb_ref[0:1, :]).astype(BF)
    mod_ref[...] = mod.T
    lane = lax.broadcasted_iota(jnp.int32, (1, 128), 1)
    for n, part in enumerate(parts):
        y = dot_nn(mod, weights[2 * n][...]) + weights[2 * n + 1][...]
        if part == "v":
            outs[n][...] = y.astype(BF)
            continue
        scale = 0.125 if part == "q" else 1.0
        for t in range(0, y.shape[1], 128):
            z = turn(y[:, t : t + 128], cos, sin, lane)
            outs[n][:, t : t + 128] = (z * scale).astype(BF)


def front(core, x0, x1, w_in, b_in, emb, w_qkv, b_qkv, angles, parts):
    rows, span, width = x0.shape
    n = 2 * span
    model = w_in.shape[1]
    half = model // 2
    place = {"q": 0, "k": 1, "v": 2}
    one = pl.BlockSpec((None, span, width), lambda r, i, c: (r, 0, 0))
    frame = lambda w: pl.BlockSpec((None, span, w), lambda r, i, c: (r, i, 0))
    whole = lambda a, b: pl.BlockSpec((a, b), lambda r, i, c: (0, 0))
    w_specs, w_args = [], []
    for part in parts:
        j = place[part]
        w_specs.append(pl.BlockSpec((model, half), lambda r, i, c, j=j: (0, 2 * j + c[0])))
        w_specs.append(pl.BlockSpec((1, half), lambda r, i, c, j=j: (0, 2 * j + c[0])))
        w_args += [w_qkv, b_qkv]
    return pl.pallas_call(
        functools.partial(front_kernel, parts=parts),
        grid_spec=pltpu.PrefetchScalarGridSpec(
            num_scalar_prefetch=1,
            grid=(rows, 2),
            in_specs=[one, one, whole(*w_in.shape), whole(1, model)]
            + [pl.BlockSpec((None, 6, model), lambda r, i, c: (r, 0, 0))]
            + w_specs
            + [pl.BlockSpec((None, None, 2, 32, span), lambda r, i, c: (r, i, 0, 0, 0))],
            out_specs=[pl.BlockSpec((None, None, model, span), lambda r, i, c: (r, i, 0, 0))]
            + [frame(half)] * len(parts),
        ),
        out_shape=[jax.ShapeDtypeStruct((rows, 2, model, span), BF)]
        + [jax.ShapeDtypeStruct((rows, n, half), BF)] * len(parts),
        compiler_params=pltpu.CompilerParams(vmem_limit_bytes=60 * MIB),
        cost_estimate=QUICK,
        name="front",
    )(core, x0, x1, w_in, b_in, emb, *w_args, angles)


def ada_kernel(t_ref, w_ref, out_ref, *, turned):
    out_ref[...] = (dot_nt if turned else dot_nn)(t_ref[...], w_ref[...])


def ada(t, w, turned):
    rows = t.shape[0]
    n = w.shape[0] if turned else w.shape[1]
    step = 256 if turned else 1024
    block = (step, w.shape[1]) if turned else (w.shape[0], step)
    return pl.pallas_call(
        functools.partial(ada_kernel, turned=turned),
        grid=(n // step,),
        in_specs=[
            pl.BlockSpec(t.shape, lambda i: (0, 0)),
            pl.BlockSpec(block, lambda i: (i, 0) if turned else (0, i)),
        ],
        out_specs=pl.BlockSpec((rows, step), lambda i: (0, i)),
        out_shape=jax.ShapeDtypeStruct((rows, n), F32),
        compiler_params=pltpu.CompilerParams(vmem_limit_bytes=60 * MIB),
        cost_estimate=QUICK,
        name="ada",
    )(t, w)


def mid_kernel(
    core, x_ref, om_ref, oo_ref, g_ref, valid_ref, emb_ref,
    win_ref, bin_ref, wom_ref, woo_ref, bout_ref, wup_ref, bup_ref, wdn_ref, bdn_ref,
    out_ref, dres_ref, dom_ref, doo_ref, mod_ref, act_ref, dhid_ref, dff_ref, dbr_ref,
    sums_ref, bupg_ref, slope_ref,
):
    hidden_width = wup_ref.shape[1]
    step = 512
    gate_one, shift_two = emb_ref[2:3, :], emb_ref[3:4, :]
    scale_two, gate_two = emb_ref[4:5, :], emb_ref[5:6, :]
    total = lambda v: jnp.sum(v, axis=0, keepdims=True)
    mean = lambda v: jnp.mean(v, axis=1, keepdims=True)
    resid = dot_nn(x_ref[:, : win_ref.shape[0]], win_ref[...]) + bin_ref[...]
    branch = dot_nn(om_ref[...], wom_ref[...]) + dot_nn(oo_ref[...], woo_ref[...]) + bout_ref[...]
    branch = branch * valid_ref[...]
    resid = resid + gate_one * branch
    center = resid - mean(resid)
    inv = lax.rsqrt(mean(center * center) + EPS)
    normed = center * inv
    mod = (normed * (1.0 + scale_two) + shift_two).astype(BF)
    mod_ref[...] = mod
    ff = None
    for j in range(0, hidden_width, step):
        h = dot_nn(mod, wup_ref[:, j : j + step]) + bup_ref[:, j : j + step]
        square = h * h
        t = jnp.tanh(h * (0.7978845608028654 + 0.035677408136300125 * square))
        up = 0.5 + 0.5 * t
        act = (h * up).astype(BF)
        act_ref[:, j : j + step] = act
        slope = up + h * (0.5 - 0.5 * t * t) * (0.7978845608028654 + 0.10703222440890037 * square)
        slope_ref[:, j : j + step] = slope.astype(BF)
        part = dot_nn(act, wdn_ref[j : j + step, :])
        ff = part if ff is None else ff + part
    ff = ff + bdn_ref[...]
    out_ref[...] = (resid + gate_two * ff).astype(BF)
    g = g_ref[...].astype(F32)
    sums_ref[0:1, :] = total(g * ff)
    d_ff = (g * gate_two).astype(BF)
    dff_ref[...] = d_ff
    sums_ref[1:2, :] = total(d_ff.astype(F32))
    d_mod = None
    for j in range(0, hidden_width, step):
        d_act = dot_nt(d_ff, wdn_ref[j : j + step, :])
        d_hid = (d_act * slope_ref[:, j : j + step].astype(F32)).astype(BF)
        dhid_ref[:, j : j + step] = d_hid
        bupg_ref[:, j : j + step] = total(d_hid.astype(F32))
        part = dot_nt(d_hid, wup_ref[:, j : j + step])
        d_mod = part if d_mod is None else d_mod + part
    sums_ref[2:3, :] = total(d_mod)
    sums_ref[3:4, :] = total(d_mod * normed)
    u = d_mod * (1.0 + scale_two)
    d_res = g + inv * (u - mean(u) - normed * mean(u * normed))
    dres_ref[...] = d_res
    sums_ref[4:5, :] = total(d_res * branch)
    d_branch = (d_res * gate_one * valid_ref[...]).astype(BF)
    dbr_ref[...] = d_branch
    sums_ref[5:6, :] = total(d_branch.astype(F32))
    dom_ref[...] = dot_nt(d_branch, wom_ref[...]).astype(BF)
    doo_ref[...] = dot_nt(d_branch, woo_ref[...]).astype(BF)


def mid(core, x, o_mine, o_other, g, valid, emb, w_in, b_in, w_out, b_out, w_up, b_up, w_down, b_down):
    rows, span, width = x.shape
    model, hidden = w_up.shape
    half = model // 2
    frame = lambda w: pl.BlockSpec((None, span, w), lambda r, c: (r, 0, 0))
    whole = lambda a, b: pl.BlockSpec(
        (a, b), lambda r, c: (0, 0), pipeline_mode=pl.Buffered(buffer_count=1)
    )
    out_half = lambda f: pl.BlockSpec(
        (half, model), lambda r, c: (f(c[0]), 0), pipeline_mode=pl.Buffered(buffer_count=1)
    )
    shape = lambda w, t: jax.ShapeDtypeStruct((rows, span, w), t)
    return pl.pallas_call(
        mid_kernel,
        grid_spec=pltpu.PrefetchScalarGridSpec(
            num_scalar_prefetch=1,
            grid=(rows,),
            in_specs=[
                frame(width), frame(half), frame(half), frame(model), frame(1),
                pl.BlockSpec((None, 6, model), lambda r, c: (r, 0, 0)),
                whole(*w_in.shape), whole(1, model),
                out_half(lambda c: c), out_half(lambda c: 1 - c), whole(1, model),
                whole(model, hidden), whole(1, hidden), whole(hidden, model), whole(1, model),
            ],
            out_specs=[
                frame(model), frame(model), frame(half), frame(half), frame(model),
                frame(hidden), frame(hidden), frame(model), frame(model),
                pl.BlockSpec((None, 8, model), lambda r, c: (r, 0, 0)),
                pl.BlockSpec((None, 1, hidden), lambda r, c: (r, 0, 0)),
            ],
            scratch_shapes=[pltpu.VMEM((span, hidden), BF)],
        ),
        out_shape=[
            shape(model, BF), shape(model, F32), shape(half, BF), shape(half, BF), shape(model, BF),
            shape(hidden, BF), shape(hidden, BF), shape(model, BF), shape(model, BF),
            jax.ShapeDtypeStruct((rows, 8, model), F32),
            jax.ShapeDtypeStruct((rows, 1, hidden), F32),
        ],
        compiler_params=pltpu.CompilerParams(vmem_limit_bytes=60 * MIB),
        cost_estimate=QUICK,
        name="mid",
    )(core, x, o_mine, o_other, g, valid, emb, w_in, b_in, w_out, w_out, b_out, w_up, b_up, w_down, b_down)


def outer_kernel(core, mod_ref, act_ref, om_ref, oo_ref, dhid_ref, dff_ref, dbr_ref, out_ref):
    step = pl.program_id(0)
    seq, model = out_ref.shape[0], out_ref.shape[2]
    r = model // seq

    def put(left, right, size, first, at):
        product = dot_nn(left.T, right).astype(BF)
        for n in range(model // size):
            out_ref[first + n, at : at + size, :] = product[n * size : (n + 1) * size]

    @pl.when(step < 2)
    def _():
        product = dot_nn(mod_ref[...].T, dhid_ref[...]).astype(BF)
        for j in range(2):
            @pl.when(step == j)
            def _():
                for n in range(seq):
                    out_ref[n, j * r : (j + 1) * r, :] = product[n * r : (n + 1) * r]

    @pl.when((step >= 2) & (step < 4))
    def _():
        product = dot_nn(act_ref[...].T, dff_ref[...]).astype(BF)
        for j in range(2):
            @pl.when(step == 2 + j)
            def _():
                for n in range(seq // 2):
                    out_ref[j * (seq // 2) + n, 2 * r : 4 * r, :] = product[
                        n * 2 * r : (n + 1) * 2 * r
                    ]

    @pl.when(step == 4)
    def _():
        mine, other = om_ref[...], oo_ref[...]
        low = core[0] == 0
        mixed = jnp.concatenate([jnp.where(low, mine, other), jnp.where(low, other, mine)], axis=1)
        product = dot_nn(mixed.T, dbr_ref[...]).astype(BF)
        for n in range(seq):
            out_ref[n, 4 * r :, :] = product[n * r : (n + 1) * r]


def outer(core, mod, act, o_mine, o_other, d_hid, d_ff, d_br):
    n, model = mod.shape
    seq = lax.axis_size("sx") * 2
    low = lambda i: jnp.minimum(i, 1)
    high = lambda i: jnp.clip(i - 2, 0, 1)
    once = lambda w: pl.BlockSpec((n, w), lambda i, c: (0, 0))
    shape = (seq, 5 * model // seq, model)
    return pl.pallas_call(
        outer_kernel,
        grid_spec=pltpu.PrefetchScalarGridSpec(
            num_scalar_prefetch=1,
            grid=(5,),
            in_specs=[
                once(model), pl.BlockSpec((n, model), lambda i, c: (0, high(i))),
                once(model // 2), once(model // 2),
                pl.BlockSpec((n, model), lambda i, c: (0, low(i))), once(model), once(model),
            ],
            out_specs=pl.BlockSpec(shape, lambda i, c: (0, 0, 0)),
        ),
        out_shape=jax.ShapeDtypeStruct(shape, BF),
        compiler_params=pltpu.CompilerParams(vmem_limit_bytes=60 * MIB),
        cost_estimate=QUICK,
        name="outer",
    )(core, mod, act, o_mine, o_other, d_hid, d_ff, d_br)


def qkv_outer_kernel(place, *refs, far):
    near_ref, dq_ref, dk_ref, dv_ref = refs[:4]
    far_refs = refs[4 : 4 + 3 * far]
    keep_ref, give_ref, sums_ref = refs[-3:]
    chips, rows, width = keep_ref.shape
    width //= 3
    span = near_ref.shape[2]
    acc_q, acc = None, None
    add = lambda a, b: b if a is None else a + b
    for i in range(2):
        cut = slice(i * span, (i + 1) * span)
        both = jnp.concatenate([dk_ref[cut, :], dv_ref[cut, :]], axis=1)
        acc_q = add(acc_q, dot_nn(near_ref[i], dq_ref[cut, :]))
        acc = add(acc, dot_nn(near_ref[i], both))
    for f in range(far):
        mod_ref, dkf_ref, dvf_ref = far_refs[3 * f : 3 * f + 3]
        for i in range(2):
            cut = slice(i * span, (i + 1) * span)
            both = jnp.concatenate([dkf_ref[cut, :], dvf_ref[cut, :]], axis=1)
            acc = add(acc, dot_nn(mod_ref[i], both))
    parts = [acc_q.astype(BF), acc[:, :width].astype(BF), acc[:, width:].astype(BF)]
    column = lambda ref: jnp.sum(ref[...].astype(F32), axis=0, keepdims=True)
    sums = [column(dq_ref), column(dk_ref), column(dv_ref)]
    for f in range(far):
        for j in (1, 2):
            sums[j] = sums[j] + column(far_refs[3 * f + j])
    for j in range(3):
        sums_ref[:, j * width : (j + 1) * width] = jnp.broadcast_to(sums[j], (8, width))
    for side in range(2):
        for out_ref, core in ((keep_ref, side), (give_ref, 1 - side)):
            @pl.when(place[1] == core)
            def _():
                for n in range(side, 2 * chips, 2):
                    chip = (n // 2 + chips - place[0]) % chips
                    for j, part in enumerate(parts):
                        out_ref[chip, :, j * width : (j + 1) * width] = part[
                            n * rows : (n + 1) * rows
                        ]


def qkv_outer(place, mod_near, dq, dk, dv, far):
    model = mod_near.shape[1]
    width = dq.shape[1]
    chips = lax.axis_size("sx")
    shape = (chips, model // (2 * chips), 3 * width)
    args = [mod_near, dq, dk, dv]
    whole = lambda a: pl.BlockSpec(a.shape, lambda i, c: (0,) * a.ndim)
    for item in far:
        args += list(item)
    specs = [whole(a) for a in args]
    return pl.pallas_call(
        functools.partial(qkv_outer_kernel, far=len(far)),
        grid_spec=pltpu.PrefetchScalarGridSpec(
            num_scalar_prefetch=1,
            grid=(1,),
            in_specs=specs,
            out_specs=[pl.BlockSpec(shape, lambda i, c: (0,) * 3)] * 2
            + [pl.BlockSpec((8, 3 * width), lambda i, c: (0, 0))],
        ),
        out_shape=[jax.ShapeDtypeStruct(shape, BF)] * 2
        + [jax.ShapeDtypeStruct((8, 3 * width), F32)],
        compiler_params=pltpu.CompilerParams(vmem_limit_bytes=60 * MIB),
        cost_estimate=QUICK,
        name="qkv_outer",
    )(place, *args)


def d_mod_kernel(core, *refs, parts):
    acc, at = None, 0
    for n, count in enumerate(parts):
        left = jnp.concatenate([ref[...] for ref in refs[at : at + count]], axis=1)
        part = dot_nt(left, refs[sum(parts) + n][...])
        acc = part if acc is None else acc + part
        at += count
    mine_ref, other_ref = refs[-2:]

    @pl.when(pl.program_id(1) % 2 == 0)
    def _():
        mine_ref[...] = acc.astype(BF)

    @pl.when(pl.program_id(1) % 2 == 1)
    def _():
        other_ref[...] = acc.astype(BF)


def d_mod(core, grads, w_qkv, span):
    arrays = [a for _, g in grads for a in g]
    rows, n = arrays[0].shape[:2]
    model = w_qkv.shape[0]
    half = model // 2
    specs = [pl.BlockSpec((None, span, a.shape[2]), lambda r, i, c: (r, i, 0)) for a in arrays]
    specs += [
        pl.BlockSpec((model, half), lambda r, i, c, j=j: (0, 2 * j + c[0])) for j, _ in grads
    ]
    out = pl.BlockSpec((None, span, model), lambda r, i, c: (r, 0, 0))
    return pl.pallas_call(
        functools.partial(d_mod_kernel, parts=tuple(len(g) for _, g in grads)),
        grid_spec=pltpu.PrefetchScalarGridSpec(
            num_scalar_prefetch=1,
            grid=(rows, n // span),
            in_specs=specs,
            out_specs=[out, out],
        ),
        out_shape=[jax.ShapeDtypeStruct((rows, span, model), BF)] * 2,
        compiler_params=pltpu.CompilerParams(vmem_limit_bytes=60 * MIB),
        cost_estimate=QUICK,
        name="d_mod",
    )(core, *arrays, *[w_qkv] * len(grads))


def norm_back(normed, inv, upstream):
    mean = lambda v: jnp.mean(v, axis=1, keepdims=True)
    return inv * (upstream - mean(upstream) - normed * mean(upstream * normed))


def first_norm(x_ref, win_ref, bin_ref):
    resid = dot_nn(x_ref[:, : win_ref.shape[0]], win_ref[...]) + bin_ref[...]
    center = resid - jnp.mean(resid, axis=1, keepdims=True)
    inv = lax.rsqrt(jnp.mean(center * center, axis=1, keepdims=True) + EPS)
    return center * inv, inv


def in_outer_kernel(place, dres_ref, emb_ref, win_ref, bin_ref, *refs, blocks):
    ins, refs = [refs[3 * n : 3 * n + 3] for n in range(blocks)], refs[3 * blocks :]
    keep_out, give_out, sums_ref = refs[:3]
    far_out, turned, joined = refs[3:-2], refs[-2], refs[-1]
    span = dres_ref.shape[0]
    total = lambda v: jnp.sum(v, axis=0, keepdims=True)
    sums_ref[...] = jnp.zeros(sums_ref.shape, F32)
    for n, (x_ref, mine_ref, recv_ref) in enumerate(ins):
        cut = slice(n * span, (n + 1) * span)
        normed, inv = first_norm(x_ref, win_ref, bin_ref)
        d = mine_ref[...].astype(F32) + recv_ref[...].astype(F32)
        if n:
            far_out[n - 1][...] = d.astype(BF)
        sums_ref[0:1, :] += total(d)
        sums_ref[1:2, :] += total(d * normed)
        d = norm_back(normed, inv, d * (1.0 + emb_ref[1:2, :]))
        d = (d if n else d + dres_ref[...]).astype(BF)
        sums_ref[2:3, :] += total(d.astype(F32))
        turned[:, cut] = d.T
        joined[cut, :] = x_ref[...]
    chips, rows = keep_out.shape[0], keep_out.shape[1]
    for t in range(chips):
        block = ((place[0] + t) % chips) * 2
        for out, core in ((give_out, 1 - place[1]), (keep_out, place[1])):
            at = pl.ds(pl.multiple_of((block + core) * rows, rows), rows)
            out[t] = dot_nn(turned[at, :], joined[...]).astype(BF)


def in_outer(place, blocks, d_res, emb, w_in, b_in):
    x = blocks[0][0]
    rows, span, width = x.shape
    model = w_in.shape[1]
    chips = lax.axis_size("sx")
    block = model // (2 * chips)
    frame = lambda w: pl.BlockSpec((None, span, w), lambda r, c: (r, 0, 0))
    whole = lambda a, b: pl.BlockSpec((a, b), lambda r, c: (0, 0))
    out = pl.BlockSpec((None, chips, block, width), lambda r, c: (r, 0, 0, 0))
    return pl.pallas_call(
        functools.partial(in_outer_kernel, blocks=len(blocks)),
        grid_spec=pltpu.PrefetchScalarGridSpec(
            num_scalar_prefetch=1,
            grid=(rows,),
            in_specs=[
                frame(model), pl.BlockSpec((None, 6, model), lambda r, c: (r, 0, 0)),
                whole(*w_in.shape), whole(1, model),
            ] + [frame(width), frame(model), frame(model)] * len(blocks),
            out_specs=[out, out, pl.BlockSpec((None, 8, model), lambda r, c: (r, 0, 0))]
            + [frame(model)] * (len(blocks) - 1),
            scratch_shapes=[
                pltpu.VMEM((model, len(blocks) * span), BF),
                pltpu.VMEM((len(blocks) * span, width), BF),
            ],
        ),
        out_shape=[
            jax.ShapeDtypeStruct((rows, chips, block, width), BF),
            jax.ShapeDtypeStruct((rows, chips, block, width), BF),
            jax.ShapeDtypeStruct((rows, 8, model), F32),
        ] + [jax.ShapeDtypeStruct((rows, span, model), BF)] * (len(blocks) - 1),
        compiler_params=pltpu.CompilerParams(vmem_limit_bytes=60 * MIB),
        cost_estimate=QUICK,
        name="in_outer",
    )(place, d_res, emb, w_in, b_in, *[a for b in blocks for a in b])


def d_in_kernel(*refs, parts, mel):
    x_ref, dres_ref, emb_ref, keep_ref, win_ref, bin_ref = refs[:6]
    noisy_ref, cond_ref, text_ref = refs[6 + parts :]
    normed, inv = first_norm(x_ref, win_ref, bin_ref)
    d = refs[6][...].astype(F32)
    for ref in refs[7 : 6 + parts]:
        d = d + ref[...].astype(F32)
    d = norm_back(normed, inv, d * (1.0 + emb_ref[1:2, :]))
    d_in = dot_nt((dres_ref[...] + d).astype(BF), win_ref[...])
    noisy_ref[...] = d_in[:, :mel]
    cond_ref[...] = d_in[:, mel : 2 * mel] * keep_ref[:, 0:1]
    text_ref[...] = d_in[:, 2 * mel :] * keep_ref[:, 1:2]


def d_in(x, d_res, emb, keep, w_in, b_in, parts, mel):
    rows, span, width = x.shape
    model = w_in.shape[1]
    frame = lambda w: pl.BlockSpec((None, span, w), lambda r: (r, 0, 0))
    whole = lambda a, b: pl.BlockSpec((a, b), lambda r: (0, 0))
    sizes = [mel, mel, w_in.shape[0] - 2 * mel]
    return pl.pallas_call(
        functools.partial(d_in_kernel, parts=len(parts), mel=mel),
        grid=(rows,),
        in_specs=[
            frame(width), frame(model), pl.BlockSpec((None, 6, model), lambda r: (r, 0, 0)),
            frame(2), whole(*w_in.shape), whole(1, model),
        ] + [frame(model)] * len(parts),
        out_specs=[frame(w) for w in sizes],
        out_shape=[jax.ShapeDtypeStruct((rows, span, w), F32) for w in sizes],
        compiler_params=pltpu.CompilerParams(vmem_limit_bytes=60 * MIB),
        cost_estimate=QUICK,
        name="d_in",
    )(x, d_res, emb, keep, w_in, b_in, *parts)


def rows_of(refs, start, stop):
    parts, at = [], 0
    for ref in refs:
        size = ref.shape[0]
        lo, hi = max(start - at, 0), min(stop - at, size)
        if lo < hi:
            parts.append(ref[lo:hi, :])
        at += size
    return parts[0] if len(parts) == 1 else jnp.concatenate(parts, axis=0)


def attend_kernel(
    flag, q_ref, qx_ref, kf_ref, kn_ref, kxf_ref, kxn_ref, vf_ref, vn_ref,
    o_mine_ref, o_other_ref, l_ref, s_ref, m_ref, acc_ref,
):
    frames = s_ref.shape[1]
    span = o_mine_ref.shape[0]
    lane = lax.broadcasted_iota(jnp.int32, (1, 128), 1)
    zero = jnp.zeros((), BF)
    step = 256 if frames % 256 == 0 else frames
    apart = lambda n: pl.when(flag[0] >= -n)
    for h in range(2):
        mine = (lane // 64) == h

        @apart(2 * h)
        def _():
            q2 = jnp.concatenate([q_ref[...], qx_ref[...]], axis=1)
            top = None
            for c in range(0, frames, step):
                keys = jnp.where(mine, rows_of((kf_ref, kn_ref), c, c + step), zero)
                labels = rows_of((kxf_ref, kxn_ref), c, c + step)
                s = dot_nt(q2, jnp.concatenate([keys, labels], axis=1))
                s_ref[:, c : c + step] = s
                for t in range(0, step, 128):
                    part = s[:, t : t + 128]
                    top = part if top is None else jnp.maximum(top, part)
            m_ref[...] = jnp.broadcast_to(jnp.max(top, axis=1, keepdims=True), m_ref.shape)

        @apart(2 * h + 1)
        def _():
            top = m_ref[:, :1]
            ones = jnp.broadcast_to(jnp.where(mine, 1.0, 0.0).astype(BF), (step, 128))
            acc = None
            for c in range(0, frames, step):
                p = jnp.exp(s_ref[:, c : c + step] - top).astype(BF)
                values = jnp.where(mine, rows_of((vf_ref, vn_ref), c, c + step), zero)
                d = dot_nn(p, jnp.concatenate([values, ones], axis=1))
                acc = d if acc is None else acc + d
            if h == 0:
                acc_ref[...] = acc
                l_ref[...] = m_ref[...]
            if h == 1:
                both = acc + acc_ref[...]
                total = both[:, 128:]
                o = (both[:, :128] / total).astype(BF)
                o_mine_ref[...] = o[:span]
                o_other_ref[...] = o[span:]
                l_ref[...] = jnp.where(mine, m_ref[...], l_ref[...]) + jnp.log(total)


def attend(core, q, qx, k_far, k_near, kx_far, kx_near, v_far, v_near):
    rows, m, width = q.shape
    span = m // 2
    far, near = k_far.shape[1], k_near.shape[1]
    n = far + near
    pairs = width // 128
    at = lambda size: pl.BlockSpec((None, size, 128), lambda r, p, c: (r, 0, p))
    once = lambda size: pl.BlockSpec((None, size, 128), lambda r, p, c: (r, 0, 0))
    return pl.pallas_call(
        attend_kernel,
        grid_spec=pltpu.PrefetchScalarGridSpec(
            num_scalar_prefetch=1,
            grid=(rows, pairs),
            in_specs=[at(m), once(m), at(far), at(near), once(far), once(near), at(far), at(near)],
            out_specs=[at(span), at(span), at(m)],
            scratch_shapes=[
                pltpu.VMEM((m, n), F32),
                pltpu.VMEM((m, 128), F32),
                pltpu.VMEM((m, 256), F32),
            ],
        ),
        out_shape=[
            jax.ShapeDtypeStruct((rows, span, width), BF),
            jax.ShapeDtypeStruct((rows, span, width), BF),
            jax.ShapeDtypeStruct((rows, m, width), F32),
        ],
        compiler_params=pltpu.CompilerParams(vmem_limit_bytes=60 * MIB),
        cost_estimate=QUICK,
        name="attend",
    )(core, q, qx, k_far, k_near, kx_far, kx_near, v_far, v_near)


def split3(x, lane, rest):
    hi = x.astype(BF).astype(F32)
    mid = (x - hi).astype(BF).astype(F32)
    low = x - hi - mid
    place = lane % 64
    return jnp.where(
        place == 8, hi, jnp.where(place == 9, mid, jnp.where(place == 10, low, rest))
    ).astype(BF)


def attend_back_kernel(flag, *refs, blocks, start, finish):
    q_ref, qx_ref, om_ref, oo_ref, dom_ref, doo_ref, l_ref = refs[:7]
    refs = refs[7:]
    keys_in, refs = [refs[4 * n : 4 * n + 4] for n in range(blocks)], refs[4 * blocks :]
    if finish:
        angle_ref, refs = refs[0], refs[1:]
    if not start:
        before_ref, refs = refs[0], refs[1:]
    dq_ref, refs = refs[0], refs[1:]
    keys_out, refs = [refs[2 * n : 2 * n + 2] for n in range(blocks)], refs[2 * blocks :]
    q2, d2, k2, v2, kk, qt, dt, p_s, s_s, dq_s, dk_s, dv_s = refs
    m, n = q_ref.shape[0], kk.shape[0]
    span = om_ref.shape[0]
    lane = lax.broadcasted_iota(jnp.int32, (1, 128), 1)
    zero = jnp.zeros((), BF)
    steps = [(c, min(c + 256, n)) for c in range(0, n, 256)] if n % 128 == 0 else [(0, n)]
    cuts, at = [], 0
    for k_ref, _, _, _ in keys_in:
        cuts.append(slice(at, at + k_ref.shape[0]))
        at += k_ref.shape[0]
    apart = pl.when(flag[0] >= 0)

    @apart
    def _():
        q2[:, :128] = q_ref[...]
        q2[:, 128:] = split3(l_ref[...], lane, qx_ref[...].astype(F32))
        same = (
            lax.broadcasted_iota(jnp.int32, (128, 128), 0) // 64
            == lax.broadcasted_iota(jnp.int32, (128, 128), 1) // 64
        )
        same = jnp.where(same, 1.0, 0.0).astype(BF)
        same = jnp.concatenate([same, same], axis=0)
        for at, do_ref, o_ref in ((0, dom_ref, om_ref), (span, doo_ref, oo_ref)):
            cut = slice(at, at + span)
            prod = do_ref[...].astype(F32) * o_ref[...].astype(F32)
            hi = prod.astype(BF)
            low = (prod - hi.astype(F32)).astype(BF)
            delta = dot_nn(jnp.concatenate([hi, low], axis=1), same)
            d2[cut, :128] = do_ref[...]
            d2[cut, 128:] = split3(delta, lane, jnp.zeros((span, 128), F32))
        qt[...] = q_ref[...].T
        dt[...] = d2[:, :128].T

    for h in range(2):
        mine = (lane // 64) == h
        half = slice(h * 64, (h + 1) * 64)

        @apart
        def _():
            less = (lane - 64 * h >= 8) & (lane - 64 * h < 11)
            for cut, (k_ref, kx_ref, v_ref, _) in zip(cuts, keys_in):
                keys = jnp.where(mine, k_ref[...], zero)
                kk[cut, :] = keys
                k2[:128, cut] = keys.T
                k2[128:, cut] = jnp.where(less, -1.0, kx_ref[...].astype(F32)).astype(BF).T
                v2[:128, cut] = jnp.where(mine, v_ref[...], zero).T
            v2[128:, :] = jnp.broadcast_to(jnp.where(less, -1.0, 0.0), (n, 128)).astype(BF).T

        @apart
        def _():
            for c, e in steps:
                s = dot_nn(q2[...], k2[:, c:e])
                d = dot_nn(d2[...], v2[:, c:e])
                p = jnp.exp(s)
                p_s[:, c:e] = p.astype(BF)
                s_s[:, c:e] = (p * d).astype(BF)

        @apart
        def _():
            acc = dot_nn(s_s[...], kk[...])
            if h == 0:
                dq_s[...] = acc if start else acc + before_ref[...]
            if h == 1:
                acc = dq_s[...] + acc
                if finish:
                    cos, sin = wide_tables(angle_ref)
                    acc = turn(acc * 0.125, cos, -sin, lane)
                dq_ref[...] = acc.astype(dq_ref.dtype)

        @apart
        def _():
            for c, e in steps:
                dk_s[half, c:e] = dot_nn(qt[half, :], s_s[:, c:e])
                dv_s[half, c:e] = dot_nn(dt[half, :], p_s[:, c:e])

    @apart
    def _():
        for cut, (_, _, _, ang_ref), (dk_ref, dv_ref) in zip(cuts, keys_in, keys_out):
            cos, sin = ang_ref[0], ang_ref[1]
            turned = []
            for h in range(2):
                a, b = dk_s[64 * h : 64 * h + 32, cut], dk_s[64 * h + 32 : 64 * h + 64, cut]
                turned += [a * cos + b * sin, b * cos - a * sin]
            dk_ref[...] = jnp.concatenate(turned, axis=0).astype(BF).T
            dv_ref[...] = dv_s[:, cut].astype(BF).T


def attend_back(core, queries, blocks, first, pairs, angles=None, before=None):
    q, qx, o_mine, o_other, d_mine, d_other, lse = queries
    rows, m, width = q.shape
    span = m // 2
    sizes = [k.shape[1] for k, _, _, _ in blocks]
    n = sum(sizes)
    at = lambda size: pl.BlockSpec((None, size, 128), lambda r, p, c: (r, 0, first + p))
    out = lambda size: pl.BlockSpec((None, size, 128), lambda r, p, c: (r, 0, p))
    once = lambda size: pl.BlockSpec((None, size, 128), lambda r, p, c: (r, 0, 0))
    angle = lambda size: pl.BlockSpec((None, 2, 32, size), lambda r, p, c: (r, 0, 0, 0))
    shape = lambda size, t: jax.ShapeDtypeStruct((rows, size, pairs * 128), t)
    in_specs = [at(m), once(m), at(span), at(span), at(span), at(span), at(m)]
    args = [q, qx, o_mine, o_other, d_mine, d_other, lse]
    for size, block in zip(sizes, blocks):
        in_specs += [at(size), once(size), at(size), angle(size)]
        args += list(block)
    if angles is not None:
        in_specs.append(angle(m))
        args.append(angles)
    if before is not None:
        in_specs.append(at(m))
        args.append(before)
    twice = [size for size in sizes for _ in range(2)]
    return pl.pallas_call(
        functools.partial(
            attend_back_kernel, blocks=len(blocks), start=before is None, finish=angles is not None
        ),
        grid_spec=pltpu.PrefetchScalarGridSpec(
            num_scalar_prefetch=1,
            grid=(rows, pairs),
            in_specs=in_specs,
            out_specs=[out(m)] + [out(size) for size in twice],
            scratch_shapes=[
                pltpu.VMEM((m, 256), BF),
                pltpu.VMEM((m, 256), BF),
                pltpu.VMEM((256, n), BF),
                pltpu.VMEM((256, n), BF),
                pltpu.VMEM((n, 128), BF),
                pltpu.VMEM((128, m), BF),
                pltpu.VMEM((128, m), BF),
                pltpu.VMEM((m, n), BF),
                pltpu.VMEM((m, n), BF),
                pltpu.VMEM((m, 128), F32),
                pltpu.VMEM((128, n), F32),
                pltpu.VMEM((128, n), F32),
            ],
        ),
        out_shape=[shape(m, F32 if angles is None else BF)] + [shape(size, BF) for size in twice],
        compiler_params=pltpu.CompilerParams(vmem_limit_bytes=60 * MIB),
        cost_estimate=QUICK,
        name="attend_back",
    )(core, *args)


def frame_table(seg_lengths, frames):
    ends = jnp.cumsum(seg_lengths, axis=1)
    starts = ends - seg_lengths
    at = frames[None, :, None]
    inside = (at >= starts[:, None, :]) & (at < ends[:, None, :])
    offsets = frames[None, :] - jnp.sum(jnp.where(inside, starts[:, None, :], 0), axis=2)
    return inside.astype(F32), offsets


def rotary_angles(offsets, head_dim):
    halves = head_dim // 2
    frequency = jnp.exp(-math.log(THETA) * 2.0 * jnp.arange(halves, dtype=F32) / head_dim)
    angles = offsets.astype(F32)[:, None, :] * frequency[:, None]
    return jnp.stack([jnp.cos(angles), jnp.sin(angles)], axis=1)


def shards(
    noisy_mel, cond_mel, text_feat, time_embed, seg_lengths, audio_drop, text_drop, w_in, b_in,
    ada_w, ada_b, w_qkv, b_qkv, w_out, b_out, w_up, b_up, w_down, b_down, cotangent,
):
    rows, span, mel = noisy_mel.shape
    model = w_qkv.shape[0]
    half = model // 2
    head_dim = model // HEADS
    core, sx = lax.axis_index("core"), lax.axis_index("sx")
    chips = lax.axis_size("sx")
    seq = chips * 2
    seq_index = sx * 2 + core
    place = jnp.stack([sx, core]).astype(jnp.int32)
    core_arg = place[1:]
    as_row = lambda v: v.astype(F32).reshape(1, -1)
    flat = lambda a: a.reshape(-1, a.shape[-1])

    ramp = jnp.arange(span, dtype=jnp.int32)

    def chip_frames(chip):
        return jnp.concatenate([(chip * 2 + core) * span + ramp, (chip * 2 + 1 - core) * span + ramp])

    member, _ = frame_table(seg_lengths, seq_index * span + ramp)
    keep_audio = 1.0 - jnp.einsum("rcs,rs->rc", member, audio_drop.astype(F32))
    keep_text = 1.0 - jnp.einsum("rcs,rs->rc", member, text_drop.astype(F32))
    keep = jnp.stack([keep_audio, keep_text], axis=2)
    frame_valid = 1.0 - member[:, :, -1:]
    width = w_in.shape[0]
    inputs = jnp.concatenate(
        [
            noisy_mel,
            cond_mel * keep_audio[..., None].astype(BF),
            text_feat * keep_text[..., None].astype(BF),
            jnp.zeros((rows, span, -width % 128), BF),
        ],
        axis=2,
    )
    inputs_other = flip(inputs, "core", 1)
    far_blocks = [shift(inputs, "sx", -t) for t in range(1, chips)]

    time_float = time_embed.astype(F32)
    time_act = jax.nn.silu(time_float).astype(BF)
    embedding = (ada(time_act, ada_w, False) + ada_b.astype(F32)).reshape(rows, 6, model)

    def tables(frame_ids):
        inside, offsets = frame_table(seg_lengths, frame_ids)
        pad = jnp.zeros(inside.shape[:2] + (128 - inside.shape[2],), F32)
        angles = rotary_angles(offsets, head_dim)
        return jnp.concatenate([inside, pad], axis=2), angles

    def two_blocks(angles):
        return jnp.moveaxis(angles.reshape(rows, 2, 32, 2, span), 3, 1)

    inside_near, ang_near = tables(chip_frames(sx))
    qx = jnp.where(jnp.arange(128) < seg_lengths.shape[1], 1.0 - inside_near, 0.0).astype(BF)
    kx_near = (MASKED * inside_near).astype(BF)
    bq, bi = as_row(b_qkv), as_row(b_in)
    mod_near, q, k_near, v_near = front(
        core_arg, inputs, inputs_other, w_in, bi, embedding, w_qkv, bq, two_blocks(ang_near),
        ("q", "k", "v"),
    )
    q, far_blocks = lax.optimization_barrier((q, far_blocks))
    far = []
    for t in range(1, chips):
        block = far_blocks[t - 1]
        inside, angles = tables(chip_frames((sx + t) % chips))
        made = front(
            core_arg, block, flip(block, "core", 1), w_in, bi, embedding, w_qkv, bq,
            two_blocks(angles), ("k", "v"),
        )
        far.append((*made, (MASKED * inside).astype(BF), angles))
    join = lambda n, axis: far[0][n] if chips == 2 else jnp.concatenate([f[n] for f in far], axis=axis)
    k_far, v_far, kx_far, ang_far = join(1, 1), join(2, 1), join(3, 1), join(4, 3)
    o_mine, o_give, lse = attend(
        core_arg, q, qx, k_far, k_near, kx_far, kx_near, v_far, v_near
    )

    o_other = flip(o_give, "core", 1)
    result, d_resid, d_o_mine, d_o_give, mod_two, act, d_hid, d_ff, d_br, sums, up_sums = mid(
        core_arg, inputs, o_mine, o_other, cotangent, frame_valid, embedding, w_in, bi,
        w_out, as_row(b_out), w_up, as_row(b_up), w_down, as_row(b_down),
    )
    d_o_other = flip(d_o_give, "core", 1)

    early = outer(
        core_arg, *[flat(a) for a in (mod_two, act, o_mine, o_other, d_hid, d_ff, d_br)]
    )
    early = lax.psum_scatter(early, ("sx", "core"), scatter_dimension=0, tiled=False)

    pairs = half // 128
    queries = (q, qx, o_mine, o_give, d_o_mine, d_o_other, lse)
    keys_far = (k_far, kx_far, v_far, ang_far)
    keys_near = (k_near, kx_near, v_near, ang_near)

    def far_part(far_grads):
        made = []
        for t in range(chips - 1):
            cut = slice(2 * span * t, 2 * span * (t + 1))
            grads = [(j, [a[:, cut] if chips > 2 else a for a in g]) for j, g in far_grads]
            made.append(d_mod(core_arg, grads, w_qkv, span))
        return made

    def outers(dq, dk_far, dk, dv_far, dv):
        pieces = []
        for r in range(rows):
            block = lambda a, t: a[r, 2 * span * t : 2 * span * (t + 1)]
            others = [
                (far[t][0][r], block(dk_far, t), block(dv_far, t)) for t in range(chips - 1)
            ]
            pieces.append(qkv_outer(place, mod_near[r], dq[r], dk[r], dv[r], others))
        if rows == 1:
            return pieces[0]
        kept, given, sums = zip(*pieces)
        return total(kept), total(given), sum(sums)

    def send(blocks):
        return [shift(b, "sx", t + 1) for t, b in enumerate(blocks)]

    tie = lambda *trees: lax.optimization_barrier(trees)

    order = (0, 1, 3, 2, 4)
    cut = 128 * (pairs - 1)
    made = attend_back(core_arg, queries, (keys_far, keys_near), 0, pairs - 1, angles=ang_near)
    first_made = [made[n] for n in order]
    first_made, early = tie(first_made, early)
    early_give = rows_give([early])
    first_made, early_give = tie(first_made, early_give)
    early_recv = flip(early_give, "ry", 1)
    first_kept, first_given, first_sums = outers(*first_made)
    first_given = flip(first_given, "core", 1)
    first_blocks = [
        jnp.concatenate([first_kept[t], first_given[t]], axis=0) for t in range(1, chips)
    ]
    queries, first_blocks = tie(queries, first_blocks)
    first_got = send(first_blocks)
    made = attend_back(core_arg, queries, (keys_far, keys_near), pairs - 1, 1, angles=ang_near)
    last_made = [made[n] for n in order]
    last_made, early_recv, first_got = tie(last_made, early_recv, first_got)

    def first_half(i):
        return total(
            [jnp.where(i == 0, first_kept[0], first_given[0])] + [part_of(g, i, 2) for g in first_got]
        )

    y = lax.axis_index("ry")
    zbits = bits("rz")
    early = rows_mine([early], early_recv)
    early_give = give_half(early, "rz", zbits[0])
    first_give = first_half(1 - y)
    last_made, early_give, first_give = tie(last_made, early_give, first_give)
    early_got = near_flip(early_give, "rz", zbits[0])
    first_recv = flip(first_give, "ry", 1)
    last_kept, last_given, last_sums = outers(*last_made)
    last_made, last_given = tie(last_made, last_given)
    far_parts = far_part([(j, [m[2 * j - 1] for m in (first_made, last_made)]) for j in (1, 2)])
    near_grads = [(0, [m[0] for m in (first_made, last_made)])]
    near_grads += [(j, [m[2 * j] for m in (first_made, last_made)]) for j in (1, 2)]
    near_mine, near_give = d_mod(core_arg, near_grads, w_qkv, span)
    far_parts, near_mine, near_give, last_given, early_got, first_recv = tie(
        far_parts, near_mine, near_give, last_given, early_got, first_recv
    )
    near_recv = flip(near_give, "core", 1)
    far_parts = [(mine, flip(give, "core", 1)) for mine, give in far_parts]
    last_given = flip(last_given, "core", 1)
    early = keep_half(early, early_got, "rz", zbits[0])
    for bit in zbits[1:-1]:
        early = keep_half(early, near_flip(give_half(early, "rz", bit), "rz", bit), "rz", bit)
    early_give = give_half(early, "rz", zbits[-1])
    first_late = total([first_half(y), first_recv])
    first_give = give_half(first_late, "rz", zbits[0])
    last_blocks = [jnp.concatenate([last_kept[t], last_given[t]], axis=1) for t in range(1, chips)]
    far_parts, near_recv, early_give, last_blocks, first_give = tie(
        far_parts, near_recv, early_give, last_blocks, first_give
    )
    early_got = near_flip(early_give, "rz", zbits[-1])
    first_recv = near_flip(first_give, "rz", zbits[0])
    last_got = send(last_blocks)
    d_blocks = [(inputs, near_mine, near_recv)]
    d_blocks += [(far_blocks[t], *far_parts[t]) for t in range(chips - 1)]
    in_kept, in_given, in_sums, *far_sums = in_outer(place, d_blocks, d_resid, embedding, w_in, bi)
    in_kept, in_given, in_sums, far_sums, last_got, early_got, first_recv = tie(
        in_kept, in_given, in_sums, far_sums, last_got, early_got, first_recv
    )
    if rows > 1:
        in_kept, in_given = [jnp.sum(a.astype(F32), axis=0).astype(BF) for a in (in_kept, in_given)]
    else:
        in_kept, in_given = in_kept[0], in_given[0]

    emb_partial = jnp.stack(
        [in_sums[:, 0], in_sums[:, 1], sums[:, 4], sums[:, 2], sums[:, 3], sums[:, 0]], axis=1
    )
    over = lambda a: jnp.sum(a, axis=0)
    bias_mine = jnp.concatenate(
        [first_sums[0].reshape(3, -1), last_sums[0].reshape(3, -1)], axis=1
    )
    gap = jnp.zeros_like(bias_mine)
    b_qkv_grad = jnp.stack(
        [jnp.where(core == 0, bias_mine, gap), jnp.where(core == 0, gap, bias_mine)], axis=1
    )
    bias_sizes = [model, 3 * model, model, w_up.shape[1], model]
    biases = jnp.concatenate(
        [over(in_sums[:, 2]), b_qkv_grad.reshape(-1), over(sums[:, 5]), over(up_sums[:, 0]), over(sums[:, 1])]
    )
    vector = jnp.concatenate([emb_partial.reshape(-1), biases])

    in_given = flip(in_given, "core", 1)
    other = flip(vector, "core", 1)
    first_late = keep_half(first_late, first_recv, "rz", zbits[0])
    for bit in zbits[1:-1]:
        first_give = give_half(first_late, "rz", bit)
        first_late = keep_half(first_late, near_flip(first_give, "rz", bit), "rz", bit)
    early = keep_half(early, early_got, "rz", zbits[-1])
    early_got = near_flip(early, "rz", zbits[-1])
    in_given, other, first_late, early_got = tie(in_given, other, first_late, early_got)
    in_blocks = [total([in_kept[t], in_given[t]]) for t in range(1, chips)]
    vector = vector + other
    early = join_halves(early, early_got, "rz", zbits[-1])
    for bit in zbits[-2:0:-1]:
        early = join_halves(early, near_flip(early, "rz", bit), "rz", bit)
    in_blocks, vector, far_sums, first_late, early = tie(
        in_blocks, vector, far_sums, first_late, early
    )
    in_got = send(in_blocks)
    vector = sum_small(vector, "sx")
    early_got = near_flip(early, "rz", zbits[0])
    first_got = near_flip(give_half(first_late, "rz", zbits[-1]), "rz", zbits[-1])
    in_got, vector, first_got = tie(in_got, vector, first_got)
    far_got = [shift(p, "sx", t + 1) for t, p in enumerate(far_sums)]
    in_terms = [in_kept[0], in_given[0]] + in_got
    last_terms = [jnp.concatenate([last_kept[0], last_given[0]], axis=1)] + last_got
    in_give = jnp.concatenate([rows_give(in_terms), rows_give(last_terms)], axis=0)
    emb_size = rows * 6 * model
    d_embedding = vector[:emb_size].reshape(rows, 6 * model).astype(BF)
    biases = vector[emb_size:]
    shares, at = [], 0
    for size in bias_sizes:
        share = size // seq
        shares.append(lax.dynamic_slice_in_dim(biases, at + seq_index * share, share, 0))
        at += size
    width_share = model // seq
    act_share = lax.dynamic_slice_in_dim(time_act, seq_index * width_share, width_share, 1)
    shares = jnp.concatenate(shares)
    bias_share = shares.shape[0]
    shares = jnp.concatenate([shares[None], jnp.zeros((rows - 1, bias_share), F32)], axis=0)
    joined = jnp.concatenate([shares, act_share.astype(F32), d_embedding.astype(F32)], axis=1)
    first_late = keep_half(first_late, first_got, "rz", zbits[-1])
    time_float, in_give, joined, first_late = tie(time_float, in_give, joined, first_late)
    in_recv = flip(in_give, "ry", 1)
    joined = gather_small(joined, "ry")
    for bit in zbits[:0:-1]:
        first_late = join_halves(first_late, near_flip(first_late, "rz", bit), "rz", bit)
    _, silu_pull = jax.vjp(jax.nn.silu, time_float)
    time_grad = ada(d_embedding, ada_w, True)
    in_mine = [total([part_of(t, y, 2) for t in terms]) for terms in (in_terms, last_terms)]
    in_mine = jnp.concatenate(in_mine, axis=0)
    joined, in_recv, time_grad, in_mine, early_got, first_late = tie(
        joined, in_recv, time_grad, in_mine, early_got, first_late
    )
    time_grad = silu_pull(time_grad)[0]
    in_mine = total([in_mine, in_recv])
    early = join_halves(early, early_got, "rz", zbits[0])
    in_mine, first_late, early = tie(in_mine, first_late, early)
    early_other = flip(early, "ry", 1)
    for n, bit in enumerate(bits("rz")):
        in_got = near_flip(in_mine, "rz", bit)
        far_bit = bits("rz")[::-1][n]
        joined = jnp.concatenate([joined, near_flip(joined, "rz", far_bit)], axis=0)
        if n == 1:
            noisy_grad, cond_grad, text_grad = d_in(
                inputs, d_resid, embedding, keep, w_in, bi, [near_mine, near_recv] + far_got, mel
            )
            in_got, joined, noisy_grad = tie(in_got, joined, noisy_grad)
        in_mine = total([in_mine, in_got])
        if n == 0:
            first_got = near_flip(first_late, "rz", zbits[0])
            in_mine, joined, first_got = tie(in_mine, joined, first_got)
            first_late = join_halves(first_late, first_got, "rz", zbits[0])
            first_other = flip(first_late, "ry", 1)
        else:
            in_mine, joined = tie(in_mine, joined)
    in_mine, noisy_grad = tie(in_mine, noisy_grad)
    in_recv = flip(in_mine, "ry", 1)
    all_act = joined[:, bias_share : bias_share + width_share].astype(BF)
    all_emb = joined[:, bias_share + width_share :]
    ada_w_grad = dot_tn(all_act, all_emb.astype(BF))
    early = by_row(early, early_other).astype(F32)
    block = model // seq
    w_up_grad = jnp.concatenate([early[:block], early[block : 2 * block]], axis=1)
    w_down_grad = early[2 * block : 4 * block]
    w_out_grad = early[4 * block :]
    in_recv, ada_w_grad, first_other, w_up_grad, w_down_grad, w_out_grad = tie(
        in_recv, ada_w_grad, first_other, w_up_grad, w_down_grad, w_out_grad
    )
    share = in_mine.shape[0] // 2
    w_in_grad = by_row(in_mine[:share], in_recv[:share])[:, :width].astype(F32).T
    last_late = by_row(in_mine[share:], in_recv[share:])

    low, high = jnp.where(y == 0, first_late, first_other), jnp.where(y == 0, first_other, first_late)
    first_late = [jnp.where(core == 0, low, high), jnp.where(core == 0, high, low)]
    low, high = last_late[:, : 3 * 128], last_late[:, 3 * 128 :]
    last_late = [jnp.where(core == 0, low, high), jnp.where(core == 0, high, low)]
    w_qkv_grad = jnp.concatenate(
        [
            part[c][:, j * size : (j + 1) * size].astype(F32)
            for j in range(3)
            for c in range(2)
            for part, size in ((first_late, cut), (last_late, 128))
        ],
        axis=1,
    )
    shares = jnp.sum(joined[:, :bias_share], axis=0)
    b_in_grad, b_qkv_grad, b_out_grad, b_up_grad, b_down_grad = jnp.split(
        shares, [sum(bias_sizes[:n]) // seq for n in range(1, 5)]
    )
    emb_share = 6 * model // seq
    ada_b_grad = lax.dynamic_slice_in_dim(
        jnp.sum(all_emb, axis=0), seq_index * emb_share, emb_share, 0
    )
    return (
        result,
        noisy_grad,
        cond_grad,
        text_grad,
        time_grad,
        w_in_grad,
        b_in_grad,
        ada_w_grad,
        ada_b_grad,
        w_qkv_grad,
        b_qkv_grad,
        w_out_grad,
        b_out_grad,
        w_up_grad,
        b_up_grad,
        w_down_grad,
        b_down_grad,
    )


def solution(mesh):
    rows, seq = mesh.shape["rows"], mesh.shape["seq"]
    mesh = Mesh(mesh.devices.reshape(rows // 2, 2, seq // 2, 2), ("rz", "ry", "sx", "core"))
    r, s = ("rz", "ry"), ("sx", "core")
    in_specs = (
        (P(r, s, None),) * 3 + (P(r, None),) * 4 + (P(),) * 12 + (P(r, s, None),)
    )
    out_specs = (
        (P(r, s, None),) * 4
        + (P(r, None), P(None, s), P(s))
        + (P(s, None), P(s)) * 5
    )
    return jax.shard_map(shards, mesh=mesh, in_specs=in_specs, out_specs=out_specs, check_vma=False)
```

```python
import functools
import math

import jax
import jax.numpy as jnp
from jax import lax
from jax.experimental import pallas as pl
from jax.experimental.pallas import tpu as pltpu
from jax.sharding import Mesh, PartitionSpec as P

HEADS = 16
EPS = 1e-06
THETA = 10000.0
MASKED = -1e30
F32 = jnp.float32
BF = jnp.bfloat16
MIB = 2**20
QUICK = pl.CostEstimate(flops=1, bytes_accessed=1, transcendentals=0)


def dot_nn(a, b):
    return jnp.dot(a, b, preferred_element_type=F32)


def dot_tn(a, b):
    return lax.dot_general(a, b, (((0,), (0,)), ((), ())), preferred_element_type=F32)


def dot_nt(a, b):
    return lax.dot_general(a, b, (((1,), (1,)), ((), ())), preferred_element_type=F32)


def shift(v, axis, step):
    size = lax.axis_size(axis)
    return lax.ppermute(v, axis, [(i, (i + step) % size) for i in range(size)])


def flip(v, axis, bit):
    size = lax.axis_size(axis)
    return lax.ppermute(v, axis, [(i, i ^ bit) for i in range(size)])


def gray(i):
    return i ^ (i >> 1)


def near_flip(v, axis, bit):
    size = lax.axis_size(axis)
    place = {gray(i): i for i in range(size)}
    return lax.ppermute(v, axis, [(i, place[gray(i) ^ bit]) for i in range(size)])


def bits(axis):
    size = lax.axis_size(axis)
    assert size & (size - 1) == 0
    return [1 << b for b in range(size.bit_length() - 1)]


def sum_small(v, axis):
    for bit in bits(axis):
        v = v + flip(v, axis, bit)
    return v


def gather_small(v, axis):
    for bit in bits(axis):
        v = jnp.concatenate([v, flip(v, axis, bit)], axis=0)
    return v


def pick(v, index):
    return lax.dynamic_index_in_dim(v, index, 0, keepdims=False)


def part_of(v, index, count):
    size = v.shape[0] // count
    return lax.dynamic_slice_in_dim(v, index * size, size, 0)


def total(terms):
    acc = terms[0].astype(F32)
    for term in terms[1:]:
        acc = acc + term.astype(F32)
    return acc.astype(BF)


def rows_give(terms):
    return total([part_of(t, 1 - lax.axis_index("ry"), 2) for t in terms])


def rows_mine(terms, recv):
    return total([part_of(t, lax.axis_index("ry"), 2) for t in terms] + [recv])


def side(axis, bit):
    return (gray(lax.axis_index(axis)) // bit) % 2


def give_half(v, axis, bit):
    return part_of(v, 1 - side(axis, bit), 2)


def keep_half(v, recv, axis, bit):
    return total([part_of(v, side(axis, bit), 2), recv])


def join_halves(mine, recv, axis, bit):
    low = side(axis, bit) == 0
    return jnp.concatenate([jnp.where(low, mine, recv), jnp.where(low, recv, mine)], axis=0)


def by_row(mine, recv):
    low = lax.axis_index("ry") == 0
    return jnp.concatenate([jnp.where(low, mine, recv), jnp.where(low, recv, mine)], axis=0)


def sum_chips(blocks):
    return list(blocks[0]) + [shift(total(blocks[t]), "sx", t) for t in range(1, len(blocks))]


def turn(x, cos, sin, lane):
    partner = jnp.where(lane % 64 < 32, pltpu.roll(x, 96, 1), pltpu.roll(x, 32, 1))
    return x * cos + partner * sin


def wide_tables(angles):
    cos, sin = angles[0], angles[1]
    return (
        jnp.concatenate([cos, cos, cos, cos], axis=0).T,
        jnp.concatenate([-sin, sin, -sin, sin], axis=0).T,
    )


def front_kernel(core, x0_ref, x1_ref, win_ref, bin_ref, emb_ref, *rest, parts):
    weights = rest[: 2 * len(parts)]
    angle_ref, mod_ref = rest[2 * len(parts) : 2 * len(parts) + 2]
    outs = rest[2 * len(parts) + 2 :]
    x = jnp.where(pl.program_id(1) == 0, x0_ref[...], x1_ref[...])[:, : win_ref.shape[0]]
    cos, sin = wide_tables(angle_ref)
    resid = dot_nn(x, win_ref[...]) + bin_ref[...]
    center = resid - jnp.mean(resid, axis=1, keepdims=True)
    inv = lax.rsqrt(jnp.mean(center * center, axis=1, keepdims=True) + EPS)
    mod = (center * inv * (1.0 + emb_ref[1:2, :]) + emb_ref[0:1, :]).astype(BF)
    mod_ref[...] = mod.T
    lane = lax.broadcasted_iota(jnp.int32, (1, 128), 1)
    for n, part in enumerate(parts):
        y = dot_nn(mod, weights[2 * n][...]) + weights[2 * n + 1][...]
        if part == "v":
            outs[n][...] = y.astype(BF)
            continue
        scale = 0.125 if part == "q" else 1.0
        for t in range(0, y.shape[1], 128):
            z = turn(y[:, t : t + 128], cos, sin, lane)
            outs[n][:, t : t + 128] = (z * scale).astype(BF)


def front(core, x0, x1, w_in, b_in, emb, w_qkv, b_qkv, angles, parts):
    rows, span, width = x0.shape
    n = 2 * span
    model = w_in.shape[1]
    half = model // 2
    place = {"q": 0, "k": 1, "v": 2}
    one = pl.BlockSpec((None, span, width), lambda r, i, c: (r, 0, 0))
    frame = lambda w: pl.BlockSpec((None, span, w), lambda r, i, c: (r, i, 0))
    whole = lambda a, b: pl.BlockSpec((a, b), lambda r, i, c: (0, 0))
    w_specs, w_args = [], []
    for part in parts:
        j = place[part]
        w_specs.append(pl.BlockSpec((model, half), lambda r, i, c, j=j: (0, 2 * j + c[0])))
        w_specs.append(pl.BlockSpec((1, half), lambda r, i, c, j=j: (0, 2 * j + c[0])))
        w_args += [w_qkv, b_qkv]
    return pl.pallas_call(
        functools.partial(front_kernel, parts=parts),
        grid_spec=pltpu.PrefetchScalarGridSpec(
            num_scalar_prefetch=1,
            grid=(rows, 2),
            in_specs=[one, one, whole(*w_in.shape), whole(1, model)]
            + [pl.BlockSpec((None, 6, model), lambda r, i, c: (r, 0, 0))]
            + w_specs
            + [pl.BlockSpec((None, None, 2, 32, span), lambda r, i, c: (r, i, 0, 0, 0))],
            out_specs=[pl.BlockSpec((None, None, model, span), lambda r, i, c: (r, i, 0, 0))]
            + [frame(half)] * len(parts),
        ),
        out_shape=[jax.ShapeDtypeStruct((rows, 2, model, span), BF)]
        + [jax.ShapeDtypeStruct((rows, n, half), BF)] * len(parts),
        compiler_params=pltpu.CompilerParams(vmem_limit_bytes=60 * MIB),
        cost_estimate=QUICK,
        name="front",
    )(core, x0, x1, w_in, b_in, emb, *w_args, angles)


def ada_kernel(t_ref, w_ref, out_ref, *, turned):
    out_ref[...] = (dot_nt if turned else dot_nn)(t_ref[...], w_ref[...])


def ada(t, w, turned):
    rows = t.shape[0]
    n = w.shape[0] if turned else w.shape[1]
    step = 256 if turned else 1024
    block = (step, w.shape[1]) if turned else (w.shape[0], step)
    return pl.pallas_call(
        functools.partial(ada_kernel, turned=turned),
        grid=(n // step,),
        in_specs=[
            pl.BlockSpec(t.shape, lambda i: (0, 0)),
            pl.BlockSpec(block, lambda i: (i, 0) if turned else (0, i)),
        ],
        out_specs=pl.BlockSpec((rows, step), lambda i: (0, i)),
        out_shape=jax.ShapeDtypeStruct((rows, n), F32),
        compiler_params=pltpu.CompilerParams(vmem_limit_bytes=60 * MIB),
        cost_estimate=QUICK,
        name="ada",
    )(t, w)


def mid_kernel(
    core, x_ref, om_ref, oo_ref, g_ref, valid_ref, emb_ref,
    win_ref, bin_ref, wom_ref, woo_ref, bout_ref, wup_hbm, bup_ref, wdn_hbm, bdn_ref,
    dres_ref, dom_ref, doo_ref, dbr_ref, sums_ref, bupg_ref,
    out_hbm, mod_hbm, act_hbm, dhid_hbm, dff_hbm,
    slope_ref, wup_ref, wdn_ref, out_ref, mod_ref, act_ref, dhid_ref, dff_ref, come, go,
):
    hidden_width = wup_ref.shape[1]
    step = 512
    row = pl.program_id(0)
    fetch_up = pltpu.make_async_copy(wup_hbm, wup_ref, come.at[0])
    fetch_down = pltpu.make_async_copy(wdn_hbm, wdn_ref, come.at[1])
    fetch_up.start()
    fetch_down.start()
    gone = []

    def leave(ref, hbm):
        copy = pltpu.make_async_copy(ref, hbm.at[row], go.at[len(gone)])
        copy.start()
        gone.append(copy)

    gate_one, shift_two = emb_ref[2:3, :], emb_ref[3:4, :]
    scale_two, gate_two = emb_ref[4:5, :], emb_ref[5:6, :]
    total = lambda v: jnp.sum(v, axis=0, keepdims=True)
    mean = lambda v: jnp.mean(v, axis=1, keepdims=True)
    resid = dot_nn(x_ref[:, : win_ref.shape[0]], win_ref[...]) + bin_ref[...]
    branch = dot_nn(om_ref[...], wom_ref[...]) + dot_nn(oo_ref[...], woo_ref[...]) + bout_ref[...]
    branch = branch * valid_ref[...]
    resid = resid + gate_one * branch
    center = resid - mean(resid)
    inv = lax.rsqrt(mean(center * center) + EPS)
    normed = center * inv
    mod = (normed * (1.0 + scale_two) + shift_two).astype(BF)
    mod_ref[...] = mod
    leave(mod_ref, mod_hbm)
    fetch_up.wait()
    fetch_down.wait()
    ff = None
    for j in range(0, hidden_width, step):
        h = dot_nn(mod, wup_ref[:, j : j + step]) + bup_ref[:, j : j + step]
        square = h * h
        t = jnp.tanh(h * (0.7978845608028654 + 0.035677408136300125 * square))
        up = 0.5 + 0.5 * t
        act = (h * up).astype(BF)
        act_ref[:, j : j + step] = act
        slope = up + h * (0.5 - 0.5 * t * t) * (0.7978845608028654 + 0.10703222440890037 * square)
        slope_ref[:, j : j + step] = slope.astype(BF)
        part = dot_nn(act, wdn_ref[j : j + step, :])
        ff = part if ff is None else ff + part
    leave(act_ref, act_hbm)
    ff = ff + bdn_ref[...]
    out_ref[...] = (resid + gate_two * ff).astype(BF)
    leave(out_ref, out_hbm)
    g = g_ref[...].astype(F32)
    sums_ref[0:1, :] = total(g * ff)
    d_ff = (g * gate_two).astype(BF)
    dff_ref[...] = d_ff
    leave(dff_ref, dff_hbm)
    sums_ref[1:2, :] = total(d_ff.astype(F32))
    d_mod = None
    for j in range(0, hidden_width, step):
        d_act = dot_nt(d_ff, wdn_ref[j : j + step, :])
        d_hid = (d_act * slope_ref[:, j : j + step].astype(F32)).astype(BF)
        dhid_ref[:, j : j + step] = d_hid
        bupg_ref[:, j : j + step] = total(d_hid.astype(F32))
        part = dot_nt(d_hid, wup_ref[:, j : j + step])
        d_mod = part if d_mod is None else d_mod + part
    leave(dhid_ref, dhid_hbm)
    sums_ref[2:3, :] = total(d_mod)
    sums_ref[3:4, :] = total(d_mod * normed)
    u = d_mod * (1.0 + scale_two)
    d_res = g + inv * (u - mean(u) - normed * mean(u * normed))
    dres_ref[...] = d_res
    sums_ref[4:5, :] = total(d_res * branch)
    d_branch = (d_res * gate_one * valid_ref[...]).astype(BF)
    dbr_ref[...] = d_branch
    sums_ref[5:6, :] = total(d_branch.astype(F32))
    dom_ref[...] = dot_nt(d_branch, wom_ref[...]).astype(BF)
    doo_ref[...] = dot_nt(d_branch, woo_ref[...]).astype(BF)
    for copy in gone:
        copy.wait()


def mid(core, x, o_mine, o_other, g, valid, emb, w_in, b_in, w_out, b_out, w_up, b_up, w_down, b_down):
    rows, span, width = x.shape
    model, hidden = w_up.shape
    half = model // 2
    frame = lambda w: pl.BlockSpec((None, span, w), lambda r, c: (r, 0, 0))
    whole = lambda a, b: pl.BlockSpec(
        (a, b), lambda r, c: (0, 0), pipeline_mode=pl.Buffered(buffer_count=1)
    )
    out_half = lambda f: pl.BlockSpec(
        (half, model), lambda r, c: (f(c[0]), 0), pipeline_mode=pl.Buffered(buffer_count=1)
    )
    anywhere = pl.BlockSpec(memory_space=pl.ANY)
    shape = lambda w, t: jax.ShapeDtypeStruct((rows, span, w), t)
    return pl.pallas_call(
        mid_kernel,
        grid_spec=pltpu.PrefetchScalarGridSpec(
            num_scalar_prefetch=1,
            grid=(rows,),
            in_specs=[
                frame(width), frame(half), frame(half), frame(model), frame(1),
                pl.BlockSpec((None, 6, model), lambda r, c: (r, 0, 0)),
                whole(*w_in.shape), whole(1, model),
                out_half(lambda c: c), out_half(lambda c: 1 - c), whole(1, model),
                anywhere, whole(1, hidden), anywhere, whole(1, model),
            ],
            out_specs=[
                frame(model), frame(half), frame(half), frame(model),
                pl.BlockSpec((None, 8, model), lambda r, c: (r, 0, 0)),
                pl.BlockSpec((None, 1, hidden), lambda r, c: (r, 0, 0)),
            ] + [anywhere] * 5,
            scratch_shapes=[
                pltpu.VMEM((span, hidden), BF),
                pltpu.VMEM((model, hidden), BF),
                pltpu.VMEM((hidden, model), BF),
                pltpu.VMEM((span, model), BF),
                pltpu.VMEM((span, model), BF),
                pltpu.VMEM((span, hidden), BF),
                pltpu.VMEM((span, hidden), BF),
                pltpu.VMEM((span, model), BF),
                pltpu.SemaphoreType.DMA((2,)),
                pltpu.SemaphoreType.DMA((5,)),
            ],
        ),
        out_shape=[
            shape(model, F32), shape(half, BF), shape(half, BF), shape(model, BF),
            jax.ShapeDtypeStruct((rows, 8, model), F32),
            jax.ShapeDtypeStruct((rows, 1, hidden), F32),
            shape(model, BF), shape(model, BF), shape(hidden, BF), shape(hidden, BF),
            shape(model, BF),
        ],
        compiler_params=pltpu.CompilerParams(vmem_limit_bytes=60 * MIB),
        cost_estimate=QUICK,
        name="mid",
    )(core, x, o_mine, o_other, g, valid, emb, w_in, b_in, w_out, w_out, b_out, w_up, b_up, w_down, b_down)


def outer_kernel(core, mod_ref, act_ref, om_ref, oo_ref, dhid_ref, dff_ref, dbr_ref, out_ref, left):
    step = pl.program_id(0)
    seq, r, model = out_ref.shape

    def put(rows, right):
        product = dot_nn(rows, right).astype(BF)
        for n in range(seq):
            out_ref[n] = product[n * r : (n + 1) * r]

    @pl.when(step == 0)
    def _():
        left[:model, :] = mod_ref[...].T

    @pl.when(step == 2)
    def _():
        left[...] = act_ref[...].T

    @pl.when(step == 4)
    def _():
        mine, other = om_ref[...], oo_ref[...]
        low = core[0] == 0
        half = model // 2
        left[:half, :] = jnp.where(low, mine, other).T
        left[half:model, :] = jnp.where(low, other, mine).T

    @pl.when(step < 2)
    def _():
        put(left[:model, :], dhid_ref[...])

    for j in range(2):

        @pl.when(step == 2 + j)
        def _():
            at = [(2 * n + j) * r for n in range(seq)]
            put(jnp.concatenate([left[a : a + r, :] for a in at], axis=0), dff_ref[...])

    @pl.when(step == 4)
    def _():
        put(left[:model, :], dbr_ref[...])


def outer(core, mod, act, o_mine, o_other, d_hid, d_ff, d_br):
    n, model = mod.shape
    seq = lax.axis_size("sx") * 2
    rows = model // seq
    once = lambda w: pl.BlockSpec((n, w), lambda i, c: (0, 0))
    return pl.pallas_call(
        outer_kernel,
        grid_spec=pltpu.PrefetchScalarGridSpec(
            num_scalar_prefetch=1,
            grid=(5,),
            in_specs=[
                once(model), once(act.shape[1]), once(model // 2), once(model // 2),
                pl.BlockSpec((n, model), lambda i, c: (0, jnp.minimum(i, 1))),
                once(model), once(model),
            ],
            out_specs=pl.BlockSpec((seq, rows, model), lambda i, c: (0, i, 0)),
            scratch_shapes=[pltpu.VMEM((act.shape[1], n), BF)],
        ),
        out_shape=jax.ShapeDtypeStruct((seq, 5 * rows, model), BF),
        compiler_params=pltpu.CompilerParams(vmem_limit_bytes=60 * MIB),
        cost_estimate=QUICK,
        name="outer",
    )(core, mod, act, o_mine, o_other, d_hid, d_ff, d_br)


def qkv_outer_kernel(place, *refs, far):
    near_ref, dq_ref, dk_ref, dv_ref = refs[:4]
    far_refs = refs[4 : 4 + 3 * far]
    keep_ref, give_ref, sums_ref = refs[-3:]
    chips, rows, width = keep_ref.shape
    width //= 3
    span = near_ref.shape[2]
    acc_q, acc = None, None
    add = lambda a, b: b if a is None else a + b
    for i in range(2):
        cut = slice(i * span, (i + 1) * span)
        both = jnp.concatenate([dk_ref[cut, :], dv_ref[cut, :]], axis=1)
        acc_q = add(acc_q, dot_nn(near_ref[i], dq_ref[cut, :]))
        acc = add(acc, dot_nn(near_ref[i], both))
    for f in range(far):
        mod_ref, dkf_ref, dvf_ref = far_refs[3 * f : 3 * f + 3]
        for i in range(2):
            cut = slice(i * span, (i + 1) * span)
            both = jnp.concatenate([dkf_ref[cut, :], dvf_ref[cut, :]], axis=1)
            acc = add(acc, dot_nn(mod_ref[i], both))
    parts = [acc_q.astype(BF), acc[:, :width].astype(BF), acc[:, width:].astype(BF)]
    column = lambda ref: jnp.sum(ref[...].astype(F32), axis=0, keepdims=True)
    sums = [column(dq_ref), column(dk_ref), column(dv_ref)]
    for f in range(far):
        for j in (1, 2):
            sums[j] = sums[j] + column(far_refs[3 * f + j])
    for j in range(3):
        sums_ref[:, j * width : (j + 1) * width] = jnp.broadcast_to(sums[j], (8, width))
    for side in range(2):
        for out_ref, core in ((keep_ref, side), (give_ref, 1 - side)):
            @pl.when(place[1] == core)
            def _():
                for n in range(side, 2 * chips, 2):
                    chip = (n // 2 + chips - place[0]) % chips
                    for j, part in enumerate(parts):
                        out_ref[chip, :, j * width : (j + 1) * width] = part[
                            n * rows : (n + 1) * rows
                        ]


def qkv_outer(place, mod_near, dq, dk, dv, far):
    model = mod_near.shape[1]
    width = dq.shape[1]
    chips = lax.axis_size("sx")
    shape = (chips, model // (2 * chips), 3 * width)
    args = [mod_near, dq, dk, dv]
    whole = lambda a: pl.BlockSpec(a.shape, lambda i, c: (0,) * a.ndim)
    for item in far:
        args += list(item)
    specs = [whole(a) for a in args]
    return pl.pallas_call(
        functools.partial(qkv_outer_kernel, far=len(far)),
        grid_spec=pltpu.PrefetchScalarGridSpec(
            num_scalar_prefetch=1,
            grid=(1,),
            in_specs=specs,
            out_specs=[pl.BlockSpec(shape, lambda i, c: (0,) * 3)] * 2
            + [pl.BlockSpec((8, 3 * width), lambda i, c: (0, 0))],
        ),
        out_shape=[jax.ShapeDtypeStruct(shape, BF)] * 2
        + [jax.ShapeDtypeStruct((8, 3 * width), F32)],
        compiler_params=pltpu.CompilerParams(vmem_limit_bytes=60 * MIB),
        cost_estimate=QUICK,
        name="qkv_outer",
    )(place, *args)


def d_mod_kernel(core, *refs, parts):
    acc, at = None, 0
    for n, count in enumerate(parts):
        left = jnp.concatenate([ref[...] for ref in refs[at : at + count]], axis=1)
        part = dot_nt(left, refs[sum(parts) + n][...])
        acc = part if acc is None else acc + part
        at += count
    mine_ref, other_ref = refs[-2:]

    @pl.when(pl.program_id(1) % 2 == 0)
    def _():
        mine_ref[...] = acc.astype(BF)

    @pl.when(pl.program_id(1) % 2 == 1)
    def _():
        other_ref[...] = acc.astype(BF)


def d_mod(core, grads, w_qkv, span):
    arrays = [a for _, g in grads for a in g]
    rows, n = arrays[0].shape[:2]
    model = w_qkv.shape[0]
    half = model // 2
    specs = [pl.BlockSpec((None, span, a.shape[2]), lambda r, i, c: (r, i, 0)) for a in arrays]
    specs += [
        pl.BlockSpec((model, half), lambda r, i, c, j=j: (0, 2 * j + c[0])) for j, _ in grads
    ]
    out = pl.BlockSpec((None, span, model), lambda r, i, c: (r, 0, 0))
    return pl.pallas_call(
        functools.partial(d_mod_kernel, parts=tuple(len(g) for _, g in grads)),
        grid_spec=pltpu.PrefetchScalarGridSpec(
            num_scalar_prefetch=1,
            grid=(rows, n // span),
            in_specs=specs,
            out_specs=[out, out],
        ),
        out_shape=[jax.ShapeDtypeStruct((rows, span, model), BF)] * 2,
        compiler_params=pltpu.CompilerParams(vmem_limit_bytes=60 * MIB),
        cost_estimate=QUICK,
        name="d_mod",
    )(core, *arrays, *[w_qkv] * len(grads))


def norm_back(normed, inv, upstream):
    mean = lambda v: jnp.mean(v, axis=1, keepdims=True)
    return inv * (upstream - mean(upstream) - normed * mean(upstream * normed))


def first_norm(x_ref, win_ref, bin_ref):
    resid = dot_nn(x_ref[:, : win_ref.shape[0]], win_ref[...]) + bin_ref[...]
    center = resid - jnp.mean(resid, axis=1, keepdims=True)
    inv = lax.rsqrt(jnp.mean(center * center, axis=1, keepdims=True) + EPS)
    return center * inv, inv


def in_outer_kernel(place, dres_hbm, emb_ref, win_ref, bin_ref, *refs, blocks):
    ins, refs = [refs[3 * n : 3 * n + 3] for n in range(blocks)], refs[3 * blocks :]
    keep_out, give_out, sums_ref = refs[:3]
    far_out, refs = refs[3 : 2 + blocks], refs[2 + blocks :]
    turned, joined, sems, dres_ref, *later = refs
    row = pl.program_id(0)
    come = [pltpu.make_async_copy(dres_hbm.at[row], dres_ref, sems.at[0])]
    far_hbm = [ref for block in ins[1:] for ref in block]
    for n, (src, dst) in enumerate(zip(far_hbm, later)):
        come.append(pltpu.make_async_copy(src.at[row], dst, sems.at[n + 1]))
    for copy in come:
        copy.start()
    ins = [ins[0]] + [later[3 * n : 3 * n + 3] for n in range(blocks - 1)]
    span = ins[0][0].shape[0]
    total = lambda v: jnp.sum(v, axis=0, keepdims=True)
    sums_ref[...] = jnp.zeros(sums_ref.shape, F32)
    for n, (x_ref, mine_ref, recv_ref) in enumerate(ins):
        cut = slice(n * span, (n + 1) * span)
        if n:
            for copy in come[3 * n - 2 : 3 * n + 1]:
                copy.wait()
        normed, inv = first_norm(x_ref, win_ref, bin_ref)
        d = mine_ref[...].astype(F32) + recv_ref[...].astype(F32)
        if n:
            far_out[n - 1][...] = d.astype(BF)
        sums_ref[0:1, :] += total(d)
        sums_ref[1:2, :] += total(d * normed)
        d = norm_back(normed, inv, d * (1.0 + emb_ref[1:2, :]))
        if n == 0:
            come[0].wait()
        d = (d if n else d + dres_ref[...]).astype(BF)
        sums_ref[2:3, :] += total(d.astype(F32))
        turned[:, cut] = d.T
        joined[cut, :] = x_ref[...]
    chips, rows = keep_out.shape[0], keep_out.shape[1]
    for t in range(chips):
        block = ((place[0] + t) % chips) * 2
        for out, core in ((give_out, 1 - place[1]), (keep_out, place[1])):
            at = pl.ds(pl.multiple_of((block + core) * rows, rows), rows)
            out[t] = dot_nn(turned[at, :], joined[...]).astype(BF)


def in_outer(place, blocks, d_res, emb, w_in, b_in):
    x = blocks[0][0]
    rows, span, width = x.shape
    model = w_in.shape[1]
    chips = lax.axis_size("sx")
    block = model // (2 * chips)
    frame = lambda w: pl.BlockSpec((None, span, w), lambda r, c: (r, 0, 0))
    whole = lambda a, b: pl.BlockSpec((a, b), lambda r, c: (0, 0))
    out = pl.BlockSpec((None, chips, block, width), lambda r, c: (r, 0, 0, 0))
    anywhere = pl.BlockSpec(memory_space=pl.ANY)
    return pl.pallas_call(
        functools.partial(in_outer_kernel, blocks=len(blocks)),
        grid_spec=pltpu.PrefetchScalarGridSpec(
            num_scalar_prefetch=1,
            grid=(rows,),
            in_specs=[
                anywhere, pl.BlockSpec((None, 6, model), lambda r, c: (r, 0, 0)),
                whole(*w_in.shape), whole(1, model), frame(width), frame(model), frame(model),
            ] + [anywhere] * (3 * len(blocks) - 3),
            out_specs=[out, out, pl.BlockSpec((None, 8, model), lambda r, c: (r, 0, 0))]
            + [frame(model)] * (len(blocks) - 1),
            scratch_shapes=[
                pltpu.VMEM((model, len(blocks) * span), BF),
                pltpu.VMEM((len(blocks) * span, width), BF),
                pltpu.SemaphoreType.DMA((3 * len(blocks) - 2,)),
                pltpu.VMEM((span, model), F32),
            ] + [pltpu.VMEM((span, w), BF) for w in (width, model, model)] * (len(blocks) - 1),
        ),
        out_shape=[
            jax.ShapeDtypeStruct((rows, chips, block, width), BF),
            jax.ShapeDtypeStruct((rows, chips, block, width), BF),
            jax.ShapeDtypeStruct((rows, 8, model), F32),
        ] + [jax.ShapeDtypeStruct((rows, span, model), BF)] * (len(blocks) - 1),
        compiler_params=pltpu.CompilerParams(vmem_limit_bytes=60 * MIB),
        cost_estimate=QUICK,
        name="in_outer",
    )(place, d_res, emb, w_in, b_in, *[a for b in blocks for a in b])


def d_in_kernel(*refs, parts, mel):
    x_ref, dres_ref, emb_ref, keep_ref, win_ref, bin_ref = refs[:6]
    noisy_ref, cond_ref, text_ref = refs[6 + parts :]
    normed, inv = first_norm(x_ref, win_ref, bin_ref)
    d = refs[6][...].astype(F32)
    for ref in refs[7 : 6 + parts]:
        d = d + ref[...].astype(F32)
    d = norm_back(normed, inv, d * (1.0 + emb_ref[1:2, :]))
    d_in = dot_nt((dres_ref[...] + d).astype(BF), win_ref[...])
    noisy_ref[...] = d_in[:, :mel]
    cond_ref[...] = d_in[:, mel : 2 * mel] * keep_ref[:, 0:1]
    text_ref[...] = d_in[:, 2 * mel :] * keep_ref[:, 1:2]


def d_in(x, d_res, emb, keep, w_in, b_in, parts, mel):
    rows, span, width = x.shape
    model = w_in.shape[1]
    frame = lambda w: pl.BlockSpec((None, span, w), lambda r: (r, 0, 0))
    whole = lambda a, b: pl.BlockSpec((a, b), lambda r: (0, 0))
    sizes = [mel, mel, w_in.shape[0] - 2 * mel]
    return pl.pallas_call(
        functools.partial(d_in_kernel, parts=len(parts), mel=mel),
        grid=(rows,),
        in_specs=[
            frame(width), frame(model), pl.BlockSpec((None, 6, model), lambda r: (r, 0, 0)),
            frame(2), whole(*w_in.shape), whole(1, model),
        ] + [frame(model)] * len(parts),
        out_specs=[frame(w) for w in sizes],
        out_shape=[jax.ShapeDtypeStruct((rows, span, w), F32) for w in sizes],
        compiler_params=pltpu.CompilerParams(vmem_limit_bytes=60 * MIB),
        cost_estimate=QUICK,
        name="d_in",
    )(x, d_res, emb, keep, w_in, b_in, *parts)


def rows_of(refs, start, stop):
    parts, at = [], 0
    for ref in refs:
        size = ref.shape[0]
        lo, hi = max(start - at, 0), min(stop - at, size)
        if lo < hi:
            parts.append(ref[lo:hi, :])
        at += size
    return parts[0] if len(parts) == 1 else jnp.concatenate(parts, axis=0)


def attend_kernel(
    flag, q_ref, qx_ref, kf_ref, kn_ref, kxf_ref, kxn_ref, vf_ref, vn_ref,
    o_mine_ref, o_other_ref, l_ref, s_ref, m_ref, acc_ref,
):
    frames = s_ref.shape[1]
    span = o_mine_ref.shape[0]
    lane = lax.broadcasted_iota(jnp.int32, (1, 128), 1)
    zero = jnp.zeros((), BF)
    step = 256 if frames % 256 == 0 else frames
    apart = lambda n: pl.when(flag[0] >= -n)
    for h in range(2):
        mine = (lane // 64) == h

        @apart(2 * h)
        def _():
            q2 = jnp.concatenate([q_ref[...], qx_ref[...]], axis=1)
            top = None
            for c in range(0, frames, step):
                keys = jnp.where(mine, rows_of((kf_ref, kn_ref), c, c + step), zero)
                labels = rows_of((kxf_ref, kxn_ref), c, c + step)
                s = dot_nt(q2, jnp.concatenate([keys, labels], axis=1))
                s_ref[:, c : c + step] = s
                for t in range(0, step, 128):
                    part = s[:, t : t + 128]
                    top = part if top is None else jnp.maximum(top, part)
            m_ref[...] = jnp.broadcast_to(jnp.max(top, axis=1, keepdims=True), m_ref.shape)

        @apart(2 * h + 1)
        def _():
            top = m_ref[:, :1]
            ones = jnp.broadcast_to(jnp.where(mine, 1.0, 0.0).astype(BF), (step, 128))
            acc = None
            for c in range(0, frames, step):
                p = jnp.exp(s_ref[:, c : c + step] - top).astype(BF)
                values = jnp.where(mine, rows_of((vf_ref, vn_ref), c, c + step), zero)
                d = dot_nn(p, jnp.concatenate([values, ones], axis=1))
                acc = d if acc is None else acc + d
            if h == 0:
                acc_ref[...] = acc
                l_ref[...] = m_ref[...]
            if h == 1:
                both = acc + acc_ref[...]
                total = both[:, 128:]
                o = (both[:, :128] / total).astype(BF)
                o_mine_ref[...] = o[:span]
                o_other_ref[...] = o[span:]
                l_ref[...] = jnp.where(mine, m_ref[...], l_ref[...]) + jnp.log(total)


def attend(core, q, qx, k_far, k_near, kx_far, kx_near, v_far, v_near):
    rows, m, width = q.shape
    span = m // 2
    far, near = k_far.shape[1], k_near.shape[1]
    n = far + near
    pairs = width // 128
    at = lambda size: pl.BlockSpec((None, size, 128), lambda r, p, c: (r, 0, p))
    once = lambda size: pl.BlockSpec((None, size, 128), lambda r, p, c: (r, 0, 0))
    return pl.pallas_call(
        attend_kernel,
        grid_spec=pltpu.PrefetchScalarGridSpec(
            num_scalar_prefetch=1,
            grid=(rows, pairs),
            in_specs=[at(m), once(m), at(far), at(near), once(far), once(near), at(far), at(near)],
            out_specs=[at(span), at(span), at(m)],
            scratch_shapes=[
                pltpu.VMEM((m, n), F32),
                pltpu.VMEM((m, 128), F32),
                pltpu.VMEM((m, 256), F32),
            ],
        ),
        out_shape=[
            jax.ShapeDtypeStruct((rows, span, width), BF),
            jax.ShapeDtypeStruct((rows, span, width), BF),
            jax.ShapeDtypeStruct((rows, m, width), F32),
        ],
        compiler_params=pltpu.CompilerParams(vmem_limit_bytes=60 * MIB),
        cost_estimate=QUICK,
        name="attend",
    )(core, q, qx, k_far, k_near, kx_far, kx_near, v_far, v_near)


def split3(x, lane, rest):
    hi = x.astype(BF).astype(F32)
    mid = (x - hi).astype(BF).astype(F32)
    low = x - hi - mid
    place = lane % 64
    return jnp.where(
        place == 8, hi, jnp.where(place == 9, mid, jnp.where(place == 10, low, rest))
    ).astype(BF)


def attend_back_kernel(flag, *refs, blocks, start, finish):
    q_ref, qx_ref, om_ref, oo_ref, dom_ref, doo_ref, l_ref = refs[:7]
    refs = refs[7:]
    keys_in, refs = [refs[4 * n : 4 * n + 4] for n in range(blocks)], refs[4 * blocks :]
    if finish:
        angle_ref, refs = refs[0], refs[1:]
    if not start:
        before_ref, refs = refs[0], refs[1:]
    dq_ref, refs = refs[0], refs[1:]
    keys_out, refs = [refs[2 * n : 2 * n + 2] for n in range(blocks)], refs[2 * blocks :]
    q2, d2, k2, v2, kk, qt, dt, p_s, s_s, dq_s, dk_s, dv_s = refs
    m, n = q_ref.shape[0], kk.shape[0]
    span = om_ref.shape[0]
    lane = lax.broadcasted_iota(jnp.int32, (1, 128), 1)
    zero = jnp.zeros((), BF)
    steps = [(c, min(c + 256, n)) for c in range(0, n, 256)] if n % 128 == 0 else [(0, n)]
    cuts, at = [], 0
    for k_ref, _, _, _ in keys_in:
        cuts.append(slice(at, at + k_ref.shape[0]))
        at += k_ref.shape[0]
    apart = pl.when(flag[0] >= 0)

    @apart
    def _():
        q2[:, :128] = q_ref[...]
        q2[:, 128:] = split3(l_ref[...], lane, qx_ref[...].astype(F32))
        same = (
            lax.broadcasted_iota(jnp.int32, (128, 128), 0) // 64
            == lax.broadcasted_iota(jnp.int32, (128, 128), 1) // 64
        )
        same = jnp.where(same, 1.0, 0.0).astype(BF)
        same = jnp.concatenate([same, same], axis=0)
        for at, do_ref, o_ref in ((0, dom_ref, om_ref), (span, doo_ref, oo_ref)):
            cut = slice(at, at + span)
            prod = do_ref[...].astype(F32) * o_ref[...].astype(F32)
            hi = prod.astype(BF)
            low = (prod - hi.astype(F32)).astype(BF)
            delta = dot_nn(jnp.concatenate([hi, low], axis=1), same)
            d2[cut, :128] = do_ref[...]
            d2[cut, 128:] = split3(delta, lane, jnp.zeros((span, 128), F32))
        qt[...] = q_ref[...].T
        dt[...] = d2[:, :128].T

    for h in range(2):
        mine = (lane // 64) == h
        half = slice(h * 64, (h + 1) * 64)

        @apart
        def _():
            less = (lane - 64 * h >= 8) & (lane - 64 * h < 11)
            for cut, (k_ref, kx_ref, v_ref, _) in zip(cuts, keys_in):
                keys = jnp.where(mine, k_ref[...], zero)
                kk[cut, :] = keys
                k2[:128, cut] = keys.T
                k2[128:, cut] = jnp.where(less, -1.0, kx_ref[...].astype(F32)).astype(BF).T
                v2[:128, cut] = jnp.where(mine, v_ref[...], zero).T
            v2[128:, :] = jnp.broadcast_to(jnp.where(less, -1.0, 0.0), (n, 128)).astype(BF).T

        @apart
        def _():
            for c, e in steps:
                s = dot_nn(q2[...], k2[:, c:e])
                d = dot_nn(d2[...], v2[:, c:e])
                p = jnp.exp(s)
                p_s[:, c:e] = p.astype(BF)
                s_s[:, c:e] = (p * d).astype(BF)

        @apart
        def _():
            acc = dot_nn(s_s[...], kk[...])
            if h == 0:
                dq_s[...] = acc if start else acc + before_ref[...]
            if h == 1:
                acc = dq_s[...] + acc
                if finish:
                    cos, sin = wide_tables(angle_ref)
                    acc = turn(acc * 0.125, cos, -sin, lane)
                dq_ref[...] = acc.astype(dq_ref.dtype)

        @apart
        def _():
            for c, e in steps:
                dk_s[half, c:e] = dot_nn(qt[half, :], s_s[:, c:e])
                dv_s[half, c:e] = dot_nn(dt[half, :], p_s[:, c:e])

    @apart
    def _():
        for cut, (_, _, _, ang_ref), (dk_ref, dv_ref) in zip(cuts, keys_in, keys_out):
            cos, sin = ang_ref[0], ang_ref[1]
            turned = []
            for h in range(2):
                a, b = dk_s[64 * h : 64 * h + 32, cut], dk_s[64 * h + 32 : 64 * h + 64, cut]
                turned += [a * cos + b * sin, b * cos - a * sin]
            dk_ref[...] = jnp.concatenate(turned, axis=0).astype(BF).T
            dv_ref[...] = dv_s[:, cut].astype(BF).T


def attend_back(core, queries, blocks, first, pairs, angles=None, before=None):
    q, qx, o_mine, o_other, d_mine, d_other, lse = queries
    rows, m, width = q.shape
    span = m // 2
    sizes = [k.shape[1] for k, _, _, _ in blocks]
    n = sum(sizes)
    at = lambda size: pl.BlockSpec((None, size, 128), lambda r, p, c: (r, 0, first + p))
    out = lambda size: pl.BlockSpec((None, size, 128), lambda r, p, c: (r, 0, p))
    once = lambda size: pl.BlockSpec((None, size, 128), lambda r, p, c: (r, 0, 0))
    angle = lambda size: pl.BlockSpec((None, 2, 32, size), lambda r, p, c: (r, 0, 0, 0))
    shape = lambda size, t: jax.ShapeDtypeStruct((rows, size, pairs * 128), t)
    in_specs = [at(m), once(m), at(span), at(span), at(span), at(span), at(m)]
    args = [q, qx, o_mine, o_other, d_mine, d_other, lse]
    for size, block in zip(sizes, blocks):
        in_specs += [at(size), once(size), at(size), angle(size)]
        args += list(block)
    if angles is not None:
        in_specs.append(angle(m))
        args.append(angles)
    if before is not None:
        in_specs.append(at(m))
        args.append(before)
    twice = [size for size in sizes for _ in range(2)]
    return pl.pallas_call(
        functools.partial(
            attend_back_kernel, blocks=len(blocks), start=before is None, finish=angles is not None
        ),
        grid_spec=pltpu.PrefetchScalarGridSpec(
            num_scalar_prefetch=1,
            grid=(rows, pairs),
            in_specs=in_specs,
            out_specs=[out(m)] + [out(size) for size in twice],
            scratch_shapes=[
                pltpu.VMEM((m, 256), BF),
                pltpu.VMEM((m, 256), BF),
                pltpu.VMEM((256, n), BF),
                pltpu.VMEM((256, n), BF),
                pltpu.VMEM((n, 128), BF),
                pltpu.VMEM((128, m), BF),
                pltpu.VMEM((128, m), BF),
                pltpu.VMEM((m, n), BF),
                pltpu.VMEM((m, n), BF),
                pltpu.VMEM((m, 128), F32),
                pltpu.VMEM((128, n), F32),
                pltpu.VMEM((128, n), F32),
            ],
        ),
        out_shape=[shape(m, F32 if angles is None else BF)] + [shape(size, BF) for size in twice],
        compiler_params=pltpu.CompilerParams(vmem_limit_bytes=60 * MIB),
        cost_estimate=QUICK,
        name="attend_back",
    )(core, *args)


def frame_table(seg_lengths, frames):
    ends = jnp.cumsum(seg_lengths, axis=1)
    starts = ends - seg_lengths
    at = frames[None, :, None]
    inside = (at >= starts[:, None, :]) & (at < ends[:, None, :])
    offsets = frames[None, :] - jnp.sum(jnp.where(inside, starts[:, None, :], 0), axis=2)
    return inside.astype(F32), offsets


def rotary_angles(offsets, head_dim):
    halves = head_dim // 2
    frequency = jnp.exp(-math.log(THETA) * 2.0 * jnp.arange(halves, dtype=F32) / head_dim)
    angles = offsets.astype(F32)[:, None, :] * frequency[:, None]
    return jnp.stack([jnp.cos(angles), jnp.sin(angles)], axis=1)


def shards(
    noisy_mel, cond_mel, text_feat, time_embed, seg_lengths, audio_drop, text_drop, w_in, b_in,
    ada_w, ada_b, w_qkv, b_qkv, w_out, b_out, w_up, b_up, w_down, b_down, cotangent,
):
    rows, span, mel = noisy_mel.shape
    model = w_qkv.shape[0]
    half = model // 2
    head_dim = model // HEADS
    core, sx = lax.axis_index("core"), lax.axis_index("sx")
    chips = lax.axis_size("sx")
    seq = chips * 2
    seq_index = sx * 2 + core
    place = jnp.stack([sx, core]).astype(jnp.int32)
    core_arg = place[1:]
    as_row = lambda v: v.astype(F32).reshape(1, -1)
    flat = lambda a: a.reshape(-1, a.shape[-1])

    ramp = jnp.arange(span, dtype=jnp.int32)

    def chip_frames(chip):
        return jnp.concatenate([(chip * 2 + core) * span + ramp, (chip * 2 + 1 - core) * span + ramp])

    member, _ = frame_table(seg_lengths, seq_index * span + ramp)
    keep_audio = 1.0 - jnp.einsum("rcs,rs->rc", member, audio_drop.astype(F32))
    keep_text = 1.0 - jnp.einsum("rcs,rs->rc", member, text_drop.astype(F32))
    keep = jnp.stack([keep_audio, keep_text], axis=2)
    frame_valid = 1.0 - member[:, :, -1:]
    width = w_in.shape[0]
    inputs = jnp.concatenate(
        [
            noisy_mel,
            cond_mel * keep_audio[..., None].astype(BF),
            text_feat * keep_text[..., None].astype(BF),
            jnp.zeros((rows, span, -width % 128), BF),
        ],
        axis=2,
    )
    inputs_other = flip(inputs, "core", 1)
    far_blocks = [shift(inputs, "sx", -t) for t in range(1, chips)]

    time_float = time_embed.astype(F32)
    time_act = jax.nn.silu(time_float).astype(BF)
    embedding = (dot_nn(time_act, ada_w) + ada_b.astype(F32)).reshape(rows, 6, model)

    def tables(frame_ids):
        inside, offsets = frame_table(seg_lengths, frame_ids)
        pad = jnp.zeros(inside.shape[:2] + (128 - inside.shape[2],), F32)
        angles = rotary_angles(offsets, head_dim)
        return jnp.concatenate([inside, pad], axis=2), angles

    def two_blocks(angles):
        return jnp.moveaxis(angles.reshape(rows, 2, 32, 2, span), 3, 1)

    inside_near, ang_near = tables(chip_frames(sx))
    qx = jnp.where(jnp.arange(128) < seg_lengths.shape[1], 1.0 - inside_near, 0.0).astype(BF)
    kx_near = (MASKED * inside_near).astype(BF)
    bq, bi = as_row(b_qkv), as_row(b_in)
    mod_near, q, k_near, v_near = front(
        core_arg, inputs, inputs_other, w_in, bi, embedding, w_qkv, bq, two_blocks(ang_near),
        ("q", "k", "v"),
    )
    q, far_blocks = lax.optimization_barrier((q, far_blocks))
    far = []
    for t in range(1, chips):
        block = far_blocks[t - 1]
        inside, angles = tables(chip_frames((sx + t) % chips))
        made = front(
            core_arg, block, flip(block, "core", 1), w_in, bi, embedding, w_qkv, bq,
            two_blocks(angles), ("k", "v"),
        )
        far.append((*made, (MASKED * inside).astype(BF), angles))
    join = lambda n, axis: far[0][n] if chips == 2 else jnp.concatenate([f[n] for f in far], axis=axis)
    k_far, v_far, kx_far, ang_far = join(1, 1), join(2, 1), join(3, 1), join(4, 3)
    o_mine, o_give, lse = attend(
        core_arg, q, qx, k_far, k_near, kx_far, kx_near, v_far, v_near
    )

    o_other = flip(o_give, "core", 1)
    d_resid, d_o_mine, d_o_give, d_br, sums, up_sums, result, mod_two, act, d_hid, d_ff = mid(
        core_arg, inputs, o_mine, o_other, cotangent, frame_valid, embedding, w_in, bi,
        w_out, as_row(b_out), w_up, as_row(b_up), w_down, as_row(b_down),
    )
    d_o_other = flip(d_o_give, "core", 1)

    early = outer(
        core_arg, *[flat(a) for a in (mod_two, act, o_mine, o_other, d_hid, d_ff, d_br)]
    )
    early, d_o_other = lax.optimization_barrier((early, d_o_other))
    early = lax.psum_scatter(early, ("sx", "core"), scatter_dimension=0, tiled=False)

    pairs = half // 128
    queries = (q, qx, o_mine, o_give, d_o_mine, d_o_other, lse)
    keys_far = (k_far, kx_far, v_far, ang_far)
    keys_near = (k_near, kx_near, v_near, ang_near)

    def far_part(far_grads):
        made = []
        for t in range(chips - 1):
            cut = slice(2 * span * t, 2 * span * (t + 1))
            grads = [(j, [a[:, cut] if chips > 2 else a for a in g]) for j, g in far_grads]
            made.append(d_mod(core_arg, grads, w_qkv, span))
        return made

    def outers(dq, dk_far, dk, dv_far, dv):
        pieces = []
        for r in range(rows):
            block = lambda a, t: a[r, 2 * span * t : 2 * span * (t + 1)]
            others = [
                (far[t][0][r], block(dk_far, t), block(dv_far, t)) for t in range(chips - 1)
            ]
            pieces.append(qkv_outer(place, mod_near[r], dq[r], dk[r], dv[r], others))
        if rows == 1:
            return pieces[0]
        kept, given, sums = zip(*pieces)
        return total(kept), total(given), sum(sums)

    def send(blocks):
        return [shift(b, "sx", t + 1) for t, b in enumerate(blocks)]

    tie = lambda *trees: lax.optimization_barrier(trees)

    order = (0, 1, 3, 2, 4)
    cut = 128 * (pairs - 1)
    made = attend_back(core_arg, queries, (keys_far, keys_near), 0, pairs - 1, angles=ang_near)
    first_made = [made[n] for n in order]
    first_made, early = tie(first_made, early)
    early_give = rows_give([early])
    first_made, early_give = tie(first_made, early_give)
    early_recv = flip(early_give, "ry", 1)
    first_kept, first_given, first_sums = outers(*first_made)
    first_given = flip(first_given, "core", 1)
    first_blocks = [
        jnp.concatenate([first_kept[t], first_given[t]], axis=0) for t in range(1, chips)
    ]
    queries, first_blocks = tie(queries, first_blocks)
    first_got = send(first_blocks)
    made = attend_back(core_arg, queries, (keys_far, keys_near), pairs - 1, 1, angles=ang_near)
    last_made = [made[n] for n in order]
    last_made, early_recv, first_got = tie(last_made, early_recv, first_got)

    def first_half(i):
        return total(
            [jnp.where(i == 0, first_kept[0], first_given[0])] + [part_of(g, i, 2) for g in first_got]
        )

    y = lax.axis_index("ry")
    zbits = bits("rz")
    early = rows_mine([early], early_recv)
    early_give = give_half(early, "rz", zbits[0])
    first_give = first_half(1 - y)
    last_made, early_give, first_give = tie(last_made, early_give, first_give)
    early_got = near_flip(early_give, "rz", zbits[0])
    first_recv = flip(first_give, "ry", 1)
    last_kept, last_given, last_sums = outers(*last_made)
    last_made, last_given = tie(last_made, last_given)
    far_parts = far_part([(j, [m[2 * j - 1] for m in (first_made, last_made)]) for j in (1, 2)])
    near_grads = [(0, [m[0] for m in (first_made, last_made)])]
    near_grads += [(j, [m[2 * j] for m in (first_made, last_made)]) for j in (1, 2)]
    far_parts, early_got = tie(far_parts, early_got)
    early = keep_half(early, early_got, "rz", zbits[0])
    for bit in zbits[1:-1]:
        early = keep_half(early, near_flip(give_half(early, "rz", bit), "rz", bit), "rz", bit)
    early_give = give_half(early, "rz", zbits[-1])
    near_arrays, early_give = tie([g for _, g in near_grads], early_give)
    early_got = near_flip(early_give, "rz", zbits[-1])
    near_mine, near_give = d_mod(core_arg, list(enumerate(near_arrays)), w_qkv, span)
    far_parts, near_mine, near_give, last_given, first_recv, early_got = tie(
        far_parts, near_mine, near_give, last_given, first_recv, early_got
    )
    near_recv = flip(near_give, "core", 1)
    far_parts = [(mine, flip(give, "core", 1)) for mine, give in far_parts]
    last_given = flip(last_given, "core", 1)
    first_late = total([first_half(y), first_recv])
    first_give = give_half(first_late, "rz", zbits[0])
    last_blocks = [jnp.concatenate([last_kept[t], last_given[t]], axis=1) for t in range(1, chips)]
    early = keep_half(early, early_got, "rz", zbits[-1])
    far_parts, near_recv, early, last_blocks, first_give = tie(
        far_parts, near_recv, early, last_blocks, first_give
    )
    early_got = near_flip(early, "rz", zbits[-1])
    first_recv = near_flip(first_give, "rz", zbits[0])
    last_got = send(last_blocks)
    d_blocks = [(inputs, near_mine, near_recv)]
    d_blocks += [(far_blocks[t], *far_parts[t]) for t in range(chips - 1)]
    in_kept, in_given, in_sums, *far_sums = in_outer(place, d_blocks, d_resid, embedding, w_in, bi)
    in_kept, in_given, in_sums, far_sums, last_got, early_got, first_recv = tie(
        in_kept, in_given, in_sums, far_sums, last_got, early_got, first_recv
    )
    if rows > 1:
        in_kept, in_given = [jnp.sum(a.astype(F32), axis=0).astype(BF) for a in (in_kept, in_given)]
    else:
        in_kept, in_given = in_kept[0], in_given[0]

    emb_partial = jnp.stack(
        [in_sums[:, 0], in_sums[:, 1], sums[:, 4], sums[:, 2], sums[:, 3], sums[:, 0]], axis=1
    )
    over = lambda a: jnp.sum(a, axis=0)
    bias_mine = jnp.concatenate(
        [first_sums[0].reshape(3, -1), last_sums[0].reshape(3, -1)], axis=1
    )
    gap = jnp.zeros_like(bias_mine)
    b_qkv_grad = jnp.stack(
        [jnp.where(core == 0, bias_mine, gap), jnp.where(core == 0, gap, bias_mine)], axis=1
    )
    bias_sizes = [model, 3 * model, model, w_up.shape[1], model]
    biases = jnp.concatenate(
        [over(in_sums[:, 2]), b_qkv_grad.reshape(-1), over(sums[:, 5]), over(up_sums[:, 0]), over(sums[:, 1])]
    )
    vector = jnp.concatenate([emb_partial.reshape(-1), biases])

    in_given = flip(in_given, "core", 1)
    other = flip(vector, "core", 1)
    first_late = keep_half(first_late, first_recv, "rz", zbits[0])
    for bit in zbits[1:-1]:
        first_give = give_half(first_late, "rz", bit)
        first_late = keep_half(first_late, near_flip(first_give, "rz", bit), "rz", bit)
    early = join_halves(early, early_got, "rz", zbits[-1])
    for bit in zbits[-2:0:-1]:
        early = join_halves(early, near_flip(early, "rz", bit), "rz", bit)
    early_got = near_flip(early, "rz", zbits[0])
    in_given, other, first_late = tie(in_given, other, first_late)
    in_blocks = [total([in_kept[t], in_given[t]]) for t in range(1, chips)]
    vector = vector + other
    in_blocks, vector, far_sums, first_late = tie(in_blocks, vector, far_sums, first_late)
    in_got = send(in_blocks)
    vector = sum_small(vector, "sx")
    first_got = near_flip(give_half(first_late, "rz", zbits[-1]), "rz", zbits[-1])
    in_got, vector, first_got = tie(in_got, vector, first_got)
    far_got = [shift(p, "sx", t + 1) for t, p in enumerate(far_sums)]
    in_terms = [in_kept[0], in_given[0]] + in_got
    last_terms = [jnp.concatenate([last_kept[0], last_given[0]], axis=1)] + last_got
    in_give = jnp.concatenate([rows_give(in_terms), rows_give(last_terms)], axis=0)
    emb_size = rows * 6 * model
    d_embedding = vector[:emb_size].reshape(rows, 6 * model).astype(BF)
    biases = vector[emb_size:]
    shares, at = [], 0
    for size in bias_sizes:
        share = size // seq
        shares.append(lax.dynamic_slice_in_dim(biases, at + seq_index * share, share, 0))
        at += size
    width_share = model // seq
    act_share = lax.dynamic_slice_in_dim(time_act, seq_index * width_share, width_share, 1)
    shares = jnp.concatenate(shares)
    bias_share = shares.shape[0]
    shares = jnp.concatenate([shares[None], jnp.zeros((rows - 1, bias_share), F32)], axis=0)
    joined = jnp.concatenate([shares, act_share.astype(F32), d_embedding.astype(F32)], axis=1)
    first_late = keep_half(first_late, first_got, "rz", zbits[-1])
    time_float, in_give, joined, first_late = tie(time_float, in_give, joined, first_late)
    in_recv = flip(in_give, "ry", 1)
    joined = gather_small(joined, "ry")
    for bit in zbits[:0:-1]:
        first_late = join_halves(first_late, near_flip(first_late, "rz", bit), "rz", bit)
    _, silu_pull = jax.vjp(jax.nn.silu, time_float)
    time_grad = ada(d_embedding, ada_w, True)
    in_mine = [total([part_of(t, y, 2) for t in terms]) for terms in (in_terms, last_terms)]
    in_mine = jnp.concatenate(in_mine, axis=0)
    joined, in_recv, time_grad, in_mine, early_got, first_late = tie(
        joined, in_recv, time_grad, in_mine, early_got, first_late
    )
    time_grad = silu_pull(time_grad)[0]
    in_mine = total([in_mine, in_recv])
    early = join_halves(early, early_got, "rz", zbits[0])
    in_mine, first_late, early = tie(in_mine, first_late, early)
    early_other = flip(early, "ry", 1)
    for n, bit in enumerate(bits("rz")):
        in_got = near_flip(in_mine, "rz", bit)
        far_bit = bits("rz")[::-1][n]
        joined = jnp.concatenate([joined, near_flip(joined, "rz", far_bit)], axis=0)
        if n == 1:
            noisy_grad, cond_grad, text_grad = d_in(
                inputs, d_resid, embedding, keep, w_in, bi, [near_mine, near_recv] + far_got, mel
            )
            in_got, joined, noisy_grad = tie(in_got, joined, noisy_grad)
        in_mine = total([in_mine, in_got])
        if n == 0:
            first_got = near_flip(first_late, "rz", zbits[0])
            in_mine, joined, first_got = tie(in_mine, joined, first_got)
            first_late = join_halves(first_late, first_got, "rz", zbits[0])
            first_other = flip(first_late, "ry", 1)
        else:
            in_mine, joined = tie(in_mine, joined)
    in_mine, noisy_grad = tie(in_mine, noisy_grad)
    in_recv = flip(in_mine, "ry", 1)
    all_act = joined[:, bias_share : bias_share + width_share].astype(BF)
    all_emb = joined[:, bias_share + width_share :]
    ada_w_grad = dot_tn(all_act, all_emb.astype(BF))
    early = by_row(early, early_other).astype(F32)
    block = model // seq
    w_up_grad = jnp.concatenate([early[:block], early[block : 2 * block]], axis=1)
    w_down_grad = early[2 * block : 4 * block]
    w_out_grad = early[4 * block :]
    in_recv, ada_w_grad, first_other, w_up_grad, w_down_grad, w_out_grad = tie(
        in_recv, ada_w_grad, first_other, w_up_grad, w_down_grad, w_out_grad
    )
    share = in_mine.shape[0] // 2
    w_in_grad = by_row(in_mine[:share], in_recv[:share])[:, :width].astype(F32).T
    last_late = by_row(in_mine[share:], in_recv[share:])

    low, high = jnp.where(y == 0, first_late, first_other), jnp.where(y == 0, first_other, first_late)
    first_late = [jnp.where(core == 0, low, high), jnp.where(core == 0, high, low)]
    low, high = last_late[:, : 3 * 128], last_late[:, 3 * 128 :]
    last_late = [jnp.where(core == 0, low, high), jnp.where(core == 0, high, low)]
    w_qkv_grad = jnp.concatenate(
        [
            part[c][:, j * size : (j + 1) * size].astype(F32)
            for j in range(3)
            for c in range(2)
            for part, size in ((first_late, cut), (last_late, 128))
        ],
        axis=1,
    )
    shares = jnp.sum(joined[:, :bias_share], axis=0)
    b_in_grad, b_qkv_grad, b_out_grad, b_up_grad, b_down_grad = jnp.split(
        shares, [sum(bias_sizes[:n]) // seq for n in range(1, 5)]
    )
    emb_share = 6 * model // seq
    ada_b_grad = lax.dynamic_slice_in_dim(
        jnp.sum(all_emb, axis=0), seq_index * emb_share, emb_share, 0
    )
    return (
        result,
        noisy_grad,
        cond_grad,
        text_grad,
        time_grad,
        w_in_grad,
        b_in_grad,
        ada_w_grad,
        ada_b_grad,
        w_qkv_grad,
        b_qkv_grad,
        w_out_grad,
        b_out_grad,
        w_up_grad,
        b_up_grad,
        w_down_grad,
        b_down_grad,
    )


def solution(mesh):
    rows, seq = mesh.shape["rows"], mesh.shape["seq"]
    mesh = Mesh(mesh.devices.reshape(rows // 2, 2, seq // 2, 2), ("rz", "ry", "sx", "core"))
    r, s = ("rz", "ry"), ("sx", "core")
    in_specs = (
        (P(r, s, None),) * 3 + (P(r, None),) * 4 + (P(),) * 12 + (P(r, s, None),)
    )
    out_specs = (
        (P(r, s, None),) * 4
        + (P(r, None), P(None, s), P(s))
        + (P(s, None), P(s)) * 5
    )
    return jax.shard_map(shards, mesh=mesh, in_specs=in_specs, out_specs=out_specs, check_vma=False)
```

```python
import functools
import math

import jax
import jax.numpy as jnp
from jax import lax
from jax.experimental import pallas as pl
from jax.experimental.pallas import tpu as pltpu
from jax.sharding import Mesh, PartitionSpec as P

HEADS = 16
EPS = 1e-06
THETA = 10000.0
MASKED = -1e30
F32 = jnp.float32
BF = jnp.bfloat16
MIB = 2**20
QUICK = pl.CostEstimate(flops=1, bytes_accessed=1, transcendentals=0)


def dot_nn(a, b):
    return jnp.dot(a, b, preferred_element_type=F32)


def dot_tn(a, b):
    return lax.dot_general(a, b, (((0,), (0,)), ((), ())), preferred_element_type=F32)


def dot_nt(a, b):
    return lax.dot_general(a, b, (((1,), (1,)), ((), ())), preferred_element_type=F32)


def shift(v, axis, step):
    size = lax.axis_size(axis)
    return lax.ppermute(v, axis, [(i, (i + step) % size) for i in range(size)])


def flip(v, axis, bit):
    size = lax.axis_size(axis)
    return lax.ppermute(v, axis, [(i, i ^ bit) for i in range(size)])


def gray(i):
    return i ^ (i >> 1)


def near_flip(v, axis, bit):
    size = lax.axis_size(axis)
    place = {gray(i): i for i in range(size)}
    return lax.ppermute(v, axis, [(i, place[gray(i) ^ bit]) for i in range(size)])


def bits(axis):
    size = lax.axis_size(axis)
    assert size & (size - 1) == 0
    return [1 << b for b in range(size.bit_length() - 1)]


def sum_small(v, axis):
    for bit in bits(axis):
        v = v + flip(v, axis, bit)
    return v


def gather_small(v, axis):
    for bit in bits(axis):
        v = jnp.concatenate([v, flip(v, axis, bit)], axis=0)
    return v


def pick(v, index):
    return lax.dynamic_index_in_dim(v, index, 0, keepdims=False)


def part_of(v, index, count):
    size = v.shape[0] // count
    return lax.dynamic_slice_in_dim(v, index * size, size, 0)


def total(terms):
    acc = terms[0].astype(F32)
    for term in terms[1:]:
        acc = acc + term.astype(F32)
    return acc.astype(BF)


def rows_give(terms):
    return total([part_of(t, 1 - lax.axis_index("ry"), 2) for t in terms])


def rows_mine(terms, recv):
    return total([part_of(t, lax.axis_index("ry"), 2) for t in terms] + [recv])


def side(axis, bit):
    return (gray(lax.axis_index(axis)) // bit) % 2


def give_half(v, axis, bit):
    return part_of(v, 1 - side(axis, bit), 2)


def keep_half(v, recv, axis, bit):
    return total([part_of(v, side(axis, bit), 2), recv])


def join_halves(mine, recv, axis, bit):
    low = side(axis, bit) == 0
    return jnp.concatenate([jnp.where(low, mine, recv), jnp.where(low, recv, mine)], axis=0)


def by_row(mine, recv):
    low = lax.axis_index("ry") == 0
    return jnp.concatenate([jnp.where(low, mine, recv), jnp.where(low, recv, mine)], axis=0)


def sum_chips(blocks):
    return list(blocks[0]) + [shift(total(blocks[t]), "sx", t) for t in range(1, len(blocks))]


def turn(x, cos, sin, lane):
    partner = jnp.where(lane % 64 < 32, pltpu.roll(x, 96, 1), pltpu.roll(x, 32, 1))
    return x * cos + partner * sin


def wide_tables(angles):
    cos, sin = angles[0], angles[1]
    return (
        jnp.concatenate([cos, cos, cos, cos], axis=0).T,
        jnp.concatenate([-sin, sin, -sin, sin], axis=0).T,
    )


def front_kernel(core, x0_ref, x1_ref, win_ref, bin_ref, emb_ref, *rest, parts):
    weights = rest[: 2 * len(parts)]
    angle_ref, mod_ref = rest[2 * len(parts) : 2 * len(parts) + 2]
    outs = rest[2 * len(parts) + 2 :]
    x = jnp.where(pl.program_id(1) == 0, x0_ref[...], x1_ref[...])[:, : win_ref.shape[0]]
    angles = angle_ref[...]
    span = x0_ref.shape[0]
    angles = jnp.where(pl.program_id(1) == 0, angles[:, :, :span], angles[:, :, span:])
    cos, sin = wide_tables(angles)
    resid = dot_nn(x, win_ref[...]) + bin_ref[...]
    center = resid - jnp.mean(resid, axis=1, keepdims=True)
    inv = lax.rsqrt(jnp.mean(center * center, axis=1, keepdims=True) + EPS)
    mod = (center * inv * (1.0 + emb_ref[1:2, :]) + emb_ref[0:1, :]).astype(BF)
    mod_ref[...] = mod.T
    lane = lax.broadcasted_iota(jnp.int32, (1, 128), 1)
    for n, part in enumerate(parts):
        y = dot_nn(mod, weights[2 * n][...]) + weights[2 * n + 1][...]
        if part == "v":
            outs[n][...] = y.astype(BF)
            continue
        scale = 0.125 if part == "q" else 1.0
        for t in range(0, y.shape[1], 128):
            z = turn(y[:, t : t + 128], cos, sin, lane)
            outs[n][:, t : t + 128] = (z * scale).astype(BF)


def front(core, x0, x1, w_in, b_in, emb, w_qkv, b_qkv, angles, parts):
    rows, span, width = x0.shape
    n = 2 * span
    model = w_in.shape[1]
    half = model // 2
    place = {"q": 0, "k": 1, "v": 2}
    one = pl.BlockSpec((None, span, width), lambda r, i, c: (r, 0, 0))
    frame = lambda w: pl.BlockSpec((None, span, w), lambda r, i, c: (r, i, 0))
    whole = lambda a, b: pl.BlockSpec((a, b), lambda r, i, c: (0, 0))
    w_specs, w_args = [], []
    for part in parts:
        j = place[part]
        w_specs.append(pl.BlockSpec((model, half), lambda r, i, c, j=j: (0, 2 * j + c[0])))
        w_specs.append(pl.BlockSpec((1, half), lambda r, i, c, j=j: (0, 2 * j + c[0])))
        w_args += [w_qkv, b_qkv]
    return pl.pallas_call(
        functools.partial(front_kernel, parts=parts),
        grid_spec=pltpu.PrefetchScalarGridSpec(
            num_scalar_prefetch=1,
            grid=(rows, 2),
            in_specs=[one, one, whole(*w_in.shape), whole(1, model)]
            + [pl.BlockSpec((None, 6, model), lambda r, i, c: (r, 0, 0))]
            + w_specs
            + [pl.BlockSpec((None, 2, 32, n), lambda r, i, c: (r, 0, 0, 0))],
            out_specs=[pl.BlockSpec((None, None, model, span), lambda r, i, c: (r, i, 0, 0))]
            + [frame(half)] * len(parts),
        ),
        out_shape=[jax.ShapeDtypeStruct((rows, 2, model, span), BF)]
        + [jax.ShapeDtypeStruct((rows, n, half), BF)] * len(parts),
        compiler_params=pltpu.CompilerParams(vmem_limit_bytes=60 * MIB),
        cost_estimate=QUICK,
        name="front",
    )(core, x0, x1, w_in, b_in, emb, *w_args, angles)


def ada_kernel(t_ref, w_ref, out_ref, *, turned):
    out_ref[...] = (dot_nt if turned else dot_nn)(t_ref[...], w_ref[...])


def ada(t, w, turned):
    rows = t.shape[0]
    n = w.shape[0] if turned else w.shape[1]
    step = 256 if turned else 1024
    block = (step, w.shape[1]) if turned else (w.shape[0], step)
    return pl.pallas_call(
        functools.partial(ada_kernel, turned=turned),
        grid=(n // step,),
        in_specs=[
            pl.BlockSpec(t.shape, lambda i: (0, 0)),
            pl.BlockSpec(block, lambda i: (i, 0) if turned else (0, i)),
        ],
        out_specs=pl.BlockSpec((rows, step), lambda i: (0, i)),
        out_shape=jax.ShapeDtypeStruct((rows, n), F32),
        compiler_params=pltpu.CompilerParams(vmem_limit_bytes=60 * MIB),
        cost_estimate=QUICK,
        name="ada",
    )(t, w)


def mid_kernel(
    core, x_ref, om_ref, oo_ref, g_ref, valid_ref, emb_ref,
    win_ref, bin_ref, wom_ref, woo_ref, bout_ref, wup_hbm, bup_ref, wdn_hbm, bdn_ref,
    dres_ref, dom_ref, doo_ref, dbr_ref, sums_ref, bupg_ref,
    out_hbm, mod_hbm, act_hbm, dhid_hbm, dff_hbm,
    slope_ref, wup_ref, wdn_ref, out_ref, mod_ref, act_ref, dhid_ref, dff_ref, come, go,
):
    hidden_width = wup_ref.shape[1]
    step = 512
    row = pl.program_id(0)
    fetch_up = pltpu.make_async_copy(wup_hbm, wup_ref, come.at[0])
    fetch_down = pltpu.make_async_copy(wdn_hbm, wdn_ref, come.at[1])
    fetch_up.start()
    fetch_down.start()
    gone = []

    def leave(ref, hbm):
        copy = pltpu.make_async_copy(ref, hbm.at[row], go.at[len(gone)])
        copy.start()
        gone.append(copy)

    gate_one, shift_two = emb_ref[2:3, :], emb_ref[3:4, :]
    scale_two, gate_two = emb_ref[4:5, :], emb_ref[5:6, :]
    total = lambda v: jnp.sum(v, axis=0, keepdims=True)
    mean = lambda v: jnp.mean(v, axis=1, keepdims=True)
    resid = dot_nn(x_ref[:, : win_ref.shape[0]], win_ref[...]) + bin_ref[...]
    branch = dot_nn(om_ref[...], wom_ref[...]) + dot_nn(oo_ref[...], woo_ref[...]) + bout_ref[...]
    branch = branch * valid_ref[...]
    resid = resid + gate_one * branch
    center = resid - mean(resid)
    inv = lax.rsqrt(mean(center * center) + EPS)
    normed = center * inv
    mod = (normed * (1.0 + scale_two) + shift_two).astype(BF)
    mod_ref[...] = mod
    leave(mod_ref, mod_hbm)
    fetch_up.wait()
    fetch_down.wait()
    ff = None
    for j in range(0, hidden_width, step):
        h = dot_nn(mod, wup_ref[:, j : j + step]) + bup_ref[:, j : j + step]
        square = h * h
        t = jnp.tanh(h * (0.7978845608028654 + 0.035677408136300125 * square))
        up = 0.5 + 0.5 * t
        act = (h * up).astype(BF)
        act_ref[:, j : j + step] = act
        slope = up + h * (0.5 - 0.5 * t * t) * (0.7978845608028654 + 0.10703222440890037 * square)
        slope_ref[:, j : j + step] = slope.astype(BF)
        part = dot_nn(act, wdn_ref[j : j + step, :])
        ff = part if ff is None else ff + part
    leave(act_ref, act_hbm)
    ff = ff + bdn_ref[...]
    out_ref[...] = (resid + gate_two * ff).astype(BF)
    leave(out_ref, out_hbm)
    g = g_ref[...].astype(F32)
    sums_ref[0:1, :] = total(g * ff)
    d_ff = (g * gate_two).astype(BF)
    dff_ref[...] = d_ff
    leave(dff_ref, dff_hbm)
    sums_ref[1:2, :] = total(d_ff.astype(F32))
    d_mod = None
    for j in range(0, hidden_width, step):
        d_act = dot_nt(d_ff, wdn_ref[j : j + step, :])
        d_hid = (d_act * slope_ref[:, j : j + step].astype(F32)).astype(BF)
        dhid_ref[:, j : j + step] = d_hid
        bupg_ref[:, j : j + step] = total(d_hid.astype(F32))
        part = dot_nt(d_hid, wup_ref[:, j : j + step])
        d_mod = part if d_mod is None else d_mod + part
    leave(dhid_ref, dhid_hbm)
    sums_ref[2:3, :] = total(d_mod)
    sums_ref[3:4, :] = total(d_mod * normed)
    u = d_mod * (1.0 + scale_two)
    d_res = g + inv * (u - mean(u) - normed * mean(u * normed))
    dres_ref[...] = d_res
    sums_ref[4:5, :] = total(d_res * branch)
    d_branch = (d_res * gate_one * valid_ref[...]).astype(BF)
    dbr_ref[...] = d_branch
    sums_ref[5:6, :] = total(d_branch.astype(F32))
    dom_ref[...] = dot_nt(d_branch, wom_ref[...]).astype(BF)
    doo_ref[...] = dot_nt(d_branch, woo_ref[...]).astype(BF)
    for copy in gone:
        copy.wait()


def mid(core, x, o_mine, o_other, g, valid, emb, w_in, b_in, w_out, b_out, w_up, b_up, w_down, b_down):
    rows, span, width = x.shape
    model, hidden = w_up.shape
    half = model // 2
    frame = lambda w: pl.BlockSpec((None, span, w), lambda r, c: (r, 0, 0))
    whole = lambda a, b: pl.BlockSpec(
        (a, b), lambda r, c: (0, 0), pipeline_mode=pl.Buffered(buffer_count=1)
    )
    out_half = lambda f: pl.BlockSpec(
        (half, model), lambda r, c: (f(c[0]), 0), pipeline_mode=pl.Buffered(buffer_count=1)
    )
    anywhere = pl.BlockSpec(memory_space=pl.ANY)
    shape = lambda w, t: jax.ShapeDtypeStruct((rows, span, w), t)
    return pl.pallas_call(
        mid_kernel,
        grid_spec=pltpu.PrefetchScalarGridSpec(
            num_scalar_prefetch=1,
            grid=(rows,),
            in_specs=[
                frame(width), frame(half), frame(half), frame(model), frame(1),
                pl.BlockSpec((None, 6, model), lambda r, c: (r, 0, 0)),
                whole(*w_in.shape), whole(1, model),
                out_half(lambda c: c), out_half(lambda c: 1 - c), whole(1, model),
                anywhere, whole(1, hidden), anywhere, whole(1, model),
            ],
            out_specs=[
                frame(model), frame(half), frame(half), frame(model),
                pl.BlockSpec((None, 8, model), lambda r, c: (r, 0, 0)),
                pl.BlockSpec((None, 1, hidden), lambda r, c: (r, 0, 0)),
            ] + [anywhere] * 5,
            scratch_shapes=[
                pltpu.VMEM((span, hidden), BF),
                pltpu.VMEM((model, hidden), BF),
                pltpu.VMEM((hidden, model), BF),
                pltpu.VMEM((span, model), BF),
                pltpu.VMEM((span, model), BF),
                pltpu.VMEM((span, hidden), BF),
                pltpu.VMEM((span, hidden), BF),
                pltpu.VMEM((span, model), BF),
                pltpu.SemaphoreType.DMA((2,)),
                pltpu.SemaphoreType.DMA((5,)),
            ],
        ),
        out_shape=[
            shape(model, F32), shape(half, BF), shape(half, BF), shape(model, BF),
            jax.ShapeDtypeStruct((rows, 8, model), F32),
            jax.ShapeDtypeStruct((rows, 1, hidden), F32),
            shape(model, BF), shape(model, BF), shape(hidden, BF), shape(hidden, BF),
            shape(model, BF),
        ],
        compiler_params=pltpu.CompilerParams(vmem_limit_bytes=60 * MIB),
        cost_estimate=QUICK,
        name="mid",
    )(core, x, o_mine, o_other, g, valid, emb, w_in, b_in, w_out, w_out, b_out, w_up, b_up, w_down, b_down)


def outer_kernel(core, mod_ref, act_ref, om_ref, oo_ref, dhid_ref, dff_ref, dbr_ref, out_ref, left):
    step = pl.program_id(0)
    seq, r, model = out_ref.shape

    def put(rows, right):
        product = dot_nn(rows, right).astype(BF)
        for n in range(seq):
            out_ref[n] = product[n * r : (n + 1) * r]

    @pl.when(step == 0)
    def _():
        left[:model, :] = mod_ref[...].T

    @pl.when(step == 2)
    def _():
        left[...] = act_ref[...].T

    @pl.when(step == 4)
    def _():
        mine, other = om_ref[...], oo_ref[...]
        low = core[0] == 0
        half = model // 2
        left[:half, :] = jnp.where(low, mine, other).T
        left[half:model, :] = jnp.where(low, other, mine).T

    @pl.when(step < 2)
    def _():
        put(left[:model, :], dhid_ref[...])

    for j in range(2):

        @pl.when(step == 2 + j)
        def _():
            at = [(2 * n + j) * r for n in range(seq)]
            put(jnp.concatenate([left[a : a + r, :] for a in at], axis=0), dff_ref[...])

    @pl.when(step == 4)
    def _():
        put(left[:model, :], dbr_ref[...])


def outer(core, mod, act, o_mine, o_other, d_hid, d_ff, d_br):
    n, model = mod.shape
    seq = lax.axis_size("sx") * 2
    rows = model // seq
    once = lambda w: pl.BlockSpec((n, w), lambda i, c: (0, 0))
    return pl.pallas_call(
        outer_kernel,
        grid_spec=pltpu.PrefetchScalarGridSpec(
            num_scalar_prefetch=1,
            grid=(5,),
            in_specs=[
                once(model), once(act.shape[1]), once(model // 2), once(model // 2),
                pl.BlockSpec((n, model), lambda i, c: (0, jnp.minimum(i, 1))),
                once(model), once(model),
            ],
            out_specs=pl.BlockSpec((seq, rows, model), lambda i, c: (0, i, 0)),
            scratch_shapes=[pltpu.VMEM((act.shape[1], n), BF)],
        ),
        out_shape=jax.ShapeDtypeStruct((seq, 5 * rows, model), BF),
        compiler_params=pltpu.CompilerParams(vmem_limit_bytes=60 * MIB),
        cost_estimate=QUICK,
        name="outer",
    )(core, mod, act, o_mine, o_other, d_hid, d_ff, d_br)


def qkv_outer_kernel(place, *refs, far):
    near_ref, dq_ref, dk_ref, dv_ref = refs[:4]
    far_refs = refs[4 : 4 + 3 * far]
    keep_ref, give_ref, sums_ref = refs[-3:]
    chips, rows, width = keep_ref.shape
    width //= 3
    span = near_ref.shape[2]
    acc_q, acc = None, None
    add = lambda a, b: b if a is None else a + b
    for i in range(2):
        cut = slice(i * span, (i + 1) * span)
        both = jnp.concatenate([dk_ref[cut, :], dv_ref[cut, :]], axis=1)
        acc_q = add(acc_q, dot_nn(near_ref[i], dq_ref[cut, :]))
        acc = add(acc, dot_nn(near_ref[i], both))
    for f in range(far):
        mod_ref, dkf_ref, dvf_ref = far_refs[3 * f : 3 * f + 3]
        for i in range(2):
            cut = slice(i * span, (i + 1) * span)
            both = jnp.concatenate([dkf_ref[cut, :], dvf_ref[cut, :]], axis=1)
            acc = add(acc, dot_nn(mod_ref[i], both))
    parts = [acc_q.astype(BF), acc[:, :width].astype(BF), acc[:, width:].astype(BF)]
    column = lambda ref: jnp.sum(ref[...].astype(F32), axis=0, keepdims=True)
    sums = [column(dq_ref), column(dk_ref), column(dv_ref)]
    for f in range(far):
        for j in (1, 2):
            sums[j] = sums[j] + column(far_refs[3 * f + j])
    for j in range(3):
        sums_ref[:, j * width : (j + 1) * width] = jnp.broadcast_to(sums[j], (8, width))
    for side in range(2):
        for out_ref, core in ((keep_ref, side), (give_ref, 1 - side)):
            @pl.when(place[1] == core)
            def _():
                for n in range(side, 2 * chips, 2):
                    chip = (n // 2 + chips - place[0]) % chips
                    for j, part in enumerate(parts):
                        out_ref[chip, :, j * width : (j + 1) * width] = part[
                            n * rows : (n + 1) * rows
                        ]


def qkv_outer(place, mod_near, dq, dk, dv, far):
    model = mod_near.shape[1]
    width = dq.shape[1]
    chips = lax.axis_size("sx")
    shape = (chips, model // (2 * chips), 3 * width)
    args = [mod_near, dq, dk, dv]
    whole = lambda a: pl.BlockSpec(a.shape, lambda i, c: (0,) * a.ndim)
    for item in far:
        args += list(item)
    specs = [whole(a) for a in args]
    return pl.pallas_call(
        functools.partial(qkv_outer_kernel, far=len(far)),
        grid_spec=pltpu.PrefetchScalarGridSpec(
            num_scalar_prefetch=1,
            grid=(1,),
            in_specs=specs,
            out_specs=[pl.BlockSpec(shape, lambda i, c: (0,) * 3)] * 2
            + [pl.BlockSpec((8, 3 * width), lambda i, c: (0, 0))],
        ),
        out_shape=[jax.ShapeDtypeStruct(shape, BF)] * 2
        + [jax.ShapeDtypeStruct((8, 3 * width), F32)],
        compiler_params=pltpu.CompilerParams(vmem_limit_bytes=60 * MIB),
        cost_estimate=QUICK,
        name="qkv_outer",
    )(place, *args)


def d_mod_kernel(core, *refs, parts):
    acc, at = None, 0
    for n, count in enumerate(parts):
        left = jnp.concatenate([ref[...] for ref in refs[at : at + count]], axis=1)
        part = dot_nt(left, refs[sum(parts) + n][...])
        acc = part if acc is None else acc + part
        at += count
    mine_ref, other_ref = refs[-2:]

    @pl.when(pl.program_id(1) % 2 == 0)
    def _():
        mine_ref[...] = acc.astype(BF)

    @pl.when(pl.program_id(1) % 2 == 1)
    def _():
        other_ref[...] = acc.astype(BF)


def d_mod(core, grads, w_qkv, span):
    arrays = [a for _, g in grads for a in g]
    rows, n = arrays[0].shape[:2]
    model = w_qkv.shape[0]
    half = model // 2
    specs = [pl.BlockSpec((None, span, a.shape[2]), lambda r, i, c: (r, i, 0)) for a in arrays]
    specs += [
        pl.BlockSpec((model, half), lambda r, i, c, j=j: (0, 2 * j + c[0])) for j, _ in grads
    ]
    out = pl.BlockSpec((None, span, model), lambda r, i, c: (r, 0, 0))
    return pl.pallas_call(
        functools.partial(d_mod_kernel, parts=tuple(len(g) for _, g in grads)),
        grid_spec=pltpu.PrefetchScalarGridSpec(
            num_scalar_prefetch=1,
            grid=(rows, n // span),
            in_specs=specs,
            out_specs=[out, out],
        ),
        out_shape=[jax.ShapeDtypeStruct((rows, span, model), BF)] * 2,
        compiler_params=pltpu.CompilerParams(vmem_limit_bytes=60 * MIB),
        cost_estimate=QUICK,
        name="d_mod",
    )(core, *arrays, *[w_qkv] * len(grads))


def norm_back(normed, inv, upstream):
    mean = lambda v: jnp.mean(v, axis=1, keepdims=True)
    return inv * (upstream - mean(upstream) - normed * mean(upstream * normed))


def first_norm(x_ref, win_ref, bin_ref):
    resid = dot_nn(x_ref[:, : win_ref.shape[0]], win_ref[...]) + bin_ref[...]
    center = resid - jnp.mean(resid, axis=1, keepdims=True)
    inv = lax.rsqrt(jnp.mean(center * center, axis=1, keepdims=True) + EPS)
    return center * inv, inv


def in_outer_kernel(place, dres_hbm, emb_ref, win_ref, bin_ref, *refs, blocks):
    ins, refs = [refs[3 * n : 3 * n + 3] for n in range(blocks)], refs[3 * blocks :]
    keep_out, give_out, sums_ref = refs[:3]
    far_out, refs = refs[3 : 2 + blocks], refs[2 + blocks :]
    turned, joined, sems, dres_ref, *later = refs
    row = pl.program_id(0)
    come = [pltpu.make_async_copy(dres_hbm.at[row], dres_ref, sems.at[0])]
    far_hbm = [ref for block in ins[1:] for ref in block]
    for n, (src, dst) in enumerate(zip(far_hbm, later)):
        come.append(pltpu.make_async_copy(src.at[row], dst, sems.at[n + 1]))
    for copy in come:
        copy.start()
    ins = [ins[0]] + [later[3 * n : 3 * n + 3] for n in range(blocks - 1)]
    span = ins[0][0].shape[0]
    total = lambda v: jnp.sum(v, axis=0, keepdims=True)
    sums_ref[...] = jnp.zeros(sums_ref.shape, F32)
    for n, (x_ref, mine_ref, recv_ref) in enumerate(ins):
        cut = slice(n * span, (n + 1) * span)
        if n:
            for copy in come[3 * n - 2 : 3 * n + 1]:
                copy.wait()
        normed, inv = first_norm(x_ref, win_ref, bin_ref)
        d = mine_ref[...].astype(F32) + recv_ref[...].astype(F32)
        if n:
            far_out[n - 1][...] = d.astype(BF)
        sums_ref[0:1, :] += total(d)
        sums_ref[1:2, :] += total(d * normed)
        d = norm_back(normed, inv, d * (1.0 + emb_ref[1:2, :]))
        if n == 0:
            come[0].wait()
        d = (d if n else d + dres_ref[...]).astype(BF)
        sums_ref[2:3, :] += total(d.astype(F32))
        turned[:, cut] = d.T
        joined[cut, :] = x_ref[...]
    chips, rows = keep_out.shape[0], keep_out.shape[1]
    for t in range(chips):
        block = ((place[0] + t) % chips) * 2
        for out, core in ((give_out, 1 - place[1]), (keep_out, place[1])):
            at = pl.ds(pl.multiple_of((block + core) * rows, rows), rows)
            out[t] = dot_nn(turned[at, :], joined[...]).astype(BF)


def in_outer(place, blocks, d_res, emb, w_in, b_in):
    x = blocks[0][0]
    rows, span, width = x.shape
    model = w_in.shape[1]
    chips = lax.axis_size("sx")
    block = model // (2 * chips)
    frame = lambda w: pl.BlockSpec((None, span, w), lambda r, c: (r, 0, 0))
    whole = lambda a, b: pl.BlockSpec((a, b), lambda r, c: (0, 0))
    out = pl.BlockSpec((None, chips, block, width), lambda r, c: (r, 0, 0, 0))
    anywhere = pl.BlockSpec(memory_space=pl.ANY)
    return pl.pallas_call(
        functools.partial(in_outer_kernel, blocks=len(blocks)),
        grid_spec=pltpu.PrefetchScalarGridSpec(
            num_scalar_prefetch=1,
            grid=(rows,),
            in_specs=[
                anywhere, pl.BlockSpec((None, 6, model), lambda r, c: (r, 0, 0)),
                whole(*w_in.shape), whole(1, model), frame(width), frame(model), frame(model),
            ] + [anywhere] * (3 * len(blocks) - 3),
            out_specs=[out, out, pl.BlockSpec((None, 8, model), lambda r, c: (r, 0, 0))]
            + [frame(model)] * (len(blocks) - 1),
            scratch_shapes=[
                pltpu.VMEM((model, len(blocks) * span), BF),
                pltpu.VMEM((len(blocks) * span, width), BF),
                pltpu.SemaphoreType.DMA((3 * len(blocks) - 2,)),
                pltpu.VMEM((span, model), F32),
            ] + [pltpu.VMEM((span, w), BF) for w in (width, model, model)] * (len(blocks) - 1),
        ),
        out_shape=[
            jax.ShapeDtypeStruct((rows, chips, block, width), BF),
            jax.ShapeDtypeStruct((rows, chips, block, width), BF),
            jax.ShapeDtypeStruct((rows, 8, model), F32),
        ] + [jax.ShapeDtypeStruct((rows, span, model), BF)] * (len(blocks) - 1),
        compiler_params=pltpu.CompilerParams(vmem_limit_bytes=60 * MIB),
        cost_estimate=QUICK,
        name="in_outer",
    )(place, d_res, emb, w_in, b_in, *[a for b in blocks for a in b])


def d_in_kernel(*refs, parts, mel):
    x_ref, dres_ref, emb_ref, keep_ref, win_ref, bin_ref = refs[:6]
    noisy_ref, cond_ref, text_ref = refs[6 + parts :]
    normed, inv = first_norm(x_ref, win_ref, bin_ref)
    d = refs[6][...].astype(F32)
    for ref in refs[7 : 6 + parts]:
        d = d + ref[...].astype(F32)
    d = norm_back(normed, inv, d * (1.0 + emb_ref[1:2, :]))
    d_in = dot_nt((dres_ref[...] + d).astype(BF), win_ref[...])
    noisy_ref[...] = d_in[:, :mel]
    cond_ref[...] = d_in[:, mel : 2 * mel] * keep_ref[:, 0:1]
    text_ref[...] = d_in[:, 2 * mel :] * keep_ref[:, 1:2]


def d_in(x, d_res, emb, keep, w_in, b_in, parts, mel):
    rows, span, width = x.shape
    model = w_in.shape[1]
    frame = lambda w: pl.BlockSpec((None, span, w), lambda r: (r, 0, 0))
    whole = lambda a, b: pl.BlockSpec((a, b), lambda r: (0, 0))
    sizes = [mel, mel, w_in.shape[0] - 2 * mel]
    return pl.pallas_call(
        functools.partial(d_in_kernel, parts=len(parts), mel=mel),
        grid=(rows,),
        in_specs=[
            frame(width), frame(model), pl.BlockSpec((None, 6, model), lambda r: (r, 0, 0)),
            frame(2), whole(*w_in.shape), whole(1, model),
        ] + [frame(model)] * len(parts),
        out_specs=[frame(w) for w in sizes],
        out_shape=[jax.ShapeDtypeStruct((rows, span, w), F32) for w in sizes],
        compiler_params=pltpu.CompilerParams(vmem_limit_bytes=60 * MIB),
        cost_estimate=QUICK,
        name="d_in",
    )(x, d_res, emb, keep, w_in, b_in, *parts)


def rows_of(refs, start, stop):
    parts, at = [], 0
    for ref in refs:
        size = ref.shape[0]
        lo, hi = max(start - at, 0), min(stop - at, size)
        if lo < hi:
            parts.append(ref[lo:hi, :])
        at += size
    return parts[0] if len(parts) == 1 else jnp.concatenate(parts, axis=0)


def attend_kernel(
    flag, q_ref, qx_ref, kf_ref, kn_ref, kxf_ref, kxn_ref, vf_ref, vn_ref,
    o_mine_ref, o_other_ref, l_ref, s_ref, m_ref, acc_ref,
):
    frames = s_ref.shape[1]
    span = o_mine_ref.shape[0]
    lane = lax.broadcasted_iota(jnp.int32, (1, 128), 1)
    zero = jnp.zeros((), BF)
    step = 256 if frames % 256 == 0 else frames
    apart = lambda n: pl.when(flag[0] >= -n)
    for h in range(2):
        mine = (lane // 64) == h

        @apart(2 * h)
        def _():
            q2 = jnp.concatenate([q_ref[...], qx_ref[...]], axis=1)
            top = None
            for c in range(0, frames, step):
                keys = jnp.where(mine, rows_of((kf_ref, kn_ref), c, c + step), zero)
                labels = rows_of((kxf_ref, kxn_ref), c, c + step)
                s = dot_nt(q2, jnp.concatenate([keys, labels], axis=1))
                s_ref[:, c : c + step] = s
                for t in range(0, step, 128):
                    part = s[:, t : t + 128]
                    top = part if top is None else jnp.maximum(top, part)
            m_ref[...] = jnp.broadcast_to(jnp.max(top, axis=1, keepdims=True), m_ref.shape)

        @apart(2 * h + 1)
        def _():
            top = m_ref[:, :1]
            ones = jnp.broadcast_to(jnp.where(mine, 1.0, 0.0).astype(BF), (step, 128))
            acc = None
            for c in range(0, frames, step):
                p = jnp.exp(s_ref[:, c : c + step] - top).astype(BF)
                values = jnp.where(mine, rows_of((vf_ref, vn_ref), c, c + step), zero)
                d = dot_nn(p, jnp.concatenate([values, ones], axis=1))
                acc = d if acc is None else acc + d
            if h == 0:
                acc_ref[...] = acc
                l_ref[...] = m_ref[...]
            if h == 1:
                both = acc + acc_ref[...]
                total = both[:, 128:]
                o = (both[:, :128] / total).astype(BF)
                o_mine_ref[...] = o[:span]
                o_other_ref[...] = o[span:]
                l_ref[...] = jnp.where(mine, m_ref[...], l_ref[...]) + jnp.log(total)


def attend(core, q, qx, k_far, k_near, kx_far, kx_near, v_far, v_near):
    rows, m, width = q.shape
    span = m // 2
    far, near = k_far.shape[1], k_near.shape[1]
    n = far + near
    pairs = width // 128
    at = lambda size: pl.BlockSpec((None, size, 128), lambda r, p, c: (r, 0, p))
    once = lambda size: pl.BlockSpec((None, size, 128), lambda r, p, c: (r, 0, 0))
    return pl.pallas_call(
        attend_kernel,
        grid_spec=pltpu.PrefetchScalarGridSpec(
            num_scalar_prefetch=1,
            grid=(rows, pairs),
            in_specs=[at(m), once(m), at(far), at(near), once(far), once(near), at(far), at(near)],
            out_specs=[at(span), at(span), at(m)],
            scratch_shapes=[
                pltpu.VMEM((m, n), F32),
                pltpu.VMEM((m, 128), F32),
                pltpu.VMEM((m, 256), F32),
            ],
        ),
        out_shape=[
            jax.ShapeDtypeStruct((rows, span, width), BF),
            jax.ShapeDtypeStruct((rows, span, width), BF),
            jax.ShapeDtypeStruct((rows, m, width), F32),
        ],
        compiler_params=pltpu.CompilerParams(vmem_limit_bytes=60 * MIB),
        cost_estimate=QUICK,
        name="attend",
    )(core, q, qx, k_far, k_near, kx_far, kx_near, v_far, v_near)


def split3(x, lane, rest):
    hi = x.astype(BF).astype(F32)
    mid = (x - hi).astype(BF).astype(F32)
    low = x - hi - mid
    place = lane % 64
    return jnp.where(
        place == 8, hi, jnp.where(place == 9, mid, jnp.where(place == 10, low, rest))
    ).astype(BF)


def attend_back_kernel(flag, *refs, blocks, start, finish):
    q_ref, qx_ref, om_ref, oo_ref, dom_ref, doo_ref, l_ref = refs[:7]
    refs = refs[7:]
    keys_in, refs = [refs[4 * n : 4 * n + 4] for n in range(blocks)], refs[4 * blocks :]
    if finish:
        angle_ref, refs = refs[0], refs[1:]
    if not start:
        before_ref, refs = refs[0], refs[1:]
    dq_ref, refs = refs[0], refs[1:]
    keys_out, refs = [refs[2 * n : 2 * n + 2] for n in range(blocks)], refs[2 * blocks :]
    q2, d2, k2, v2, kk, qt, dt, p_s, s_s, dq_s, dk_s, dv_s = refs
    m, n = q_ref.shape[0], kk.shape[0]
    span = om_ref.shape[0]
    lane = lax.broadcasted_iota(jnp.int32, (1, 128), 1)
    zero = jnp.zeros((), BF)
    steps = [(c, min(c + 256, n)) for c in range(0, n, 256)] if n % 128 == 0 else [(0, n)]
    cuts, at = [], 0
    for k_ref, _, _, _ in keys_in:
        cuts.append(slice(at, at + k_ref.shape[0]))
        at += k_ref.shape[0]
    apart = pl.when(flag[0] >= 0)

    @apart
    def _():
        q2[:, :128] = q_ref[...]
        q2[:, 128:] = split3(l_ref[...], lane, qx_ref[...].astype(F32))
        same = (
            lax.broadcasted_iota(jnp.int32, (128, 128), 0) // 64
            == lax.broadcasted_iota(jnp.int32, (128, 128), 1) // 64
        )
        same = jnp.where(same, 1.0, 0.0).astype(BF)
        same = jnp.concatenate([same, same], axis=0)
        for at, do_ref, o_ref in ((0, dom_ref, om_ref), (span, doo_ref, oo_ref)):
            cut = slice(at, at + span)
            prod = do_ref[...].astype(F32) * o_ref[...].astype(F32)
            hi = prod.astype(BF)
            low = (prod - hi.astype(F32)).astype(BF)
            delta = dot_nn(jnp.concatenate([hi, low], axis=1), same)
            d2[cut, :128] = do_ref[...]
            d2[cut, 128:] = split3(delta, lane, jnp.zeros((span, 128), F32))
        qt[...] = q_ref[...].T
        dt[...] = d2[:, :128].T

    for h in range(2):
        mine = (lane // 64) == h
        half = slice(h * 64, (h + 1) * 64)

        @apart
        def _():
            less = (lane - 64 * h >= 8) & (lane - 64 * h < 11)
            for cut, (k_ref, kx_ref, v_ref, _) in zip(cuts, keys_in):
                keys = jnp.where(mine, k_ref[...], zero)
                kk[cut, :] = keys
                k2[:128, cut] = keys.T
                k2[128:, cut] = jnp.where(less, -1.0, kx_ref[...].astype(F32)).astype(BF).T
                v2[:128, cut] = jnp.where(mine, v_ref[...], zero).T
            v2[128:, :] = jnp.broadcast_to(jnp.where(less, -1.0, 0.0), (n, 128)).astype(BF).T

        @apart
        def _():
            for c, e in steps:
                s = dot_nn(q2[...], k2[:, c:e])
                d = dot_nn(d2[...], v2[:, c:e])
                p = jnp.exp(s)
                p_s[:, c:e] = p.astype(BF)
                s_s[:, c:e] = (p * d).astype(BF)

        @apart
        def _():
            acc = dot_nn(s_s[...], kk[...])
            if h == 0:
                dq_s[...] = acc if start else acc + before_ref[...]
            if h == 1:
                acc = dq_s[...] + acc
                if finish:
                    cos, sin = wide_tables(angle_ref)
                    acc = turn(acc * 0.125, cos, -sin, lane)
                dq_ref[...] = acc.astype(dq_ref.dtype)

        @apart
        def _():
            for c, e in steps:
                dk_s[half, c:e] = dot_nn(qt[half, :], s_s[:, c:e])
                dv_s[half, c:e] = dot_nn(dt[half, :], p_s[:, c:e])

    @apart
    def _():
        for cut, (_, _, _, ang_ref), (dk_ref, dv_ref) in zip(cuts, keys_in, keys_out):
            cos, sin = ang_ref[0], ang_ref[1]
            turned = []
            for h in range(2):
                a, b = dk_s[64 * h : 64 * h + 32, cut], dk_s[64 * h + 32 : 64 * h + 64, cut]
                turned += [a * cos + b * sin, b * cos - a * sin]
            dk_ref[...] = jnp.concatenate(turned, axis=0).astype(BF).T
            dv_ref[...] = dv_s[:, cut].astype(BF).T


def attend_back(core, queries, blocks, first, pairs, angles=None, before=None):
    q, qx, o_mine, o_other, d_mine, d_other, lse = queries
    rows, m, width = q.shape
    span = m // 2
    sizes = [k.shape[1] for k, _, _, _ in blocks]
    n = sum(sizes)
    at = lambda size: pl.BlockSpec((None, size, 128), lambda r, p, c: (r, 0, first + p))
    out = lambda size: pl.BlockSpec((None, size, 128), lambda r, p, c: (r, 0, p))
    once = lambda size: pl.BlockSpec((None, size, 128), lambda r, p, c: (r, 0, 0))
    angle = lambda size: pl.BlockSpec((None, 2, 32, size), lambda r, p, c: (r, 0, 0, 0))
    shape = lambda size, t: jax.ShapeDtypeStruct((rows, size, pairs * 128), t)
    in_specs = [at(m), once(m), at(span), at(span), at(span), at(span), at(m)]
    args = [q, qx, o_mine, o_other, d_mine, d_other, lse]
    for size, block in zip(sizes, blocks):
        in_specs += [at(size), once(size), at(size), angle(size)]
        args += list(block)
    if angles is not None:
        in_specs.append(angle(m))
        args.append(angles)
    if before is not None:
        in_specs.append(at(m))
        args.append(before)
    twice = [size for size in sizes for _ in range(2)]
    return pl.pallas_call(
        functools.partial(
            attend_back_kernel, blocks=len(blocks), start=before is None, finish=angles is not None
        ),
        grid_spec=pltpu.PrefetchScalarGridSpec(
            num_scalar_prefetch=1,
            grid=(rows, pairs),
            in_specs=in_specs,
            out_specs=[out(m)] + [out(size) for size in twice],
            scratch_shapes=[
                pltpu.VMEM((m, 256), BF),
                pltpu.VMEM((m, 256), BF),
                pltpu.VMEM((256, n), BF),
                pltpu.VMEM((256, n), BF),
                pltpu.VMEM((n, 128), BF),
                pltpu.VMEM((128, m), BF),
                pltpu.VMEM((128, m), BF),
                pltpu.VMEM((m, n), BF),
                pltpu.VMEM((m, n), BF),
                pltpu.VMEM((m, 128), F32),
                pltpu.VMEM((128, n), F32),
                pltpu.VMEM((128, n), F32),
            ],
        ),
        out_shape=[shape(m, F32 if angles is None else BF)] + [shape(size, BF) for size in twice],
        compiler_params=pltpu.CompilerParams(vmem_limit_bytes=60 * MIB),
        cost_estimate=QUICK,
        name="attend_back",
    )(core, *args)


def frame_table(seg_lengths, frames):
    place = jnp.arange(seg_lengths.shape[1])
    upto = place[None, :] <= place[:, None]
    ends = jnp.sum(jnp.where(upto, seg_lengths[:, None, :], 0), axis=2)
    starts = ends - seg_lengths
    at = frames[None, :, None]
    inside = (at >= starts[:, None, :]) & (at < ends[:, None, :])
    offsets = frames[None, :] - jnp.sum(jnp.where(inside, starts[:, None, :], 0), axis=2)
    return inside.astype(F32), offsets


def rotary_angles(offsets, head_dim):
    halves = head_dim // 2
    frequency = jnp.exp(-math.log(THETA) * 2.0 * jnp.arange(halves, dtype=F32) / head_dim)
    angles = offsets.astype(F32)[:, None, :] * frequency[:, None]
    return jnp.stack([jnp.cos(angles), jnp.sin(angles)], axis=1)


def shards(
    noisy_mel, cond_mel, text_feat, time_embed, seg_lengths, audio_drop, text_drop, w_in, b_in,
    ada_w, ada_b, w_qkv, b_qkv, w_out, b_out, w_up, b_up, w_down, b_down, cotangent,
):
    rows, span, mel = noisy_mel.shape
    model = w_qkv.shape[0]
    half = model // 2
    head_dim = model // HEADS
    core, sx = lax.axis_index("core"), lax.axis_index("sx")
    chips = lax.axis_size("sx")
    seq = chips * 2
    seq_index = sx * 2 + core
    place = jnp.stack([sx, core]).astype(jnp.int32)
    core_arg = place[1:]
    as_row = lambda v: v.astype(F32).reshape(1, -1)
    flat = lambda a: a.reshape(-1, a.shape[-1])

    ramp = jnp.arange(span, dtype=jnp.int32)

    def chip_frames(chip):
        return jnp.concatenate([(chip * 2 + core) * span + ramp, (chip * 2 + 1 - core) * span + ramp])

    member, _ = frame_table(seg_lengths, seq_index * span + ramp)
    keep_audio = 1.0 - jnp.sum(member * audio_drop.astype(F32)[:, None, :], axis=2)
    keep_text = 1.0 - jnp.sum(member * text_drop.astype(F32)[:, None, :], axis=2)
    keep = jnp.stack([keep_audio, keep_text], axis=2)
    frame_valid = 1.0 - member[:, :, -1:]
    width = w_in.shape[0]
    inputs = jnp.concatenate(
        [
            noisy_mel,
            cond_mel * keep_audio[..., None].astype(BF),
            text_feat * keep_text[..., None].astype(BF),
            jnp.zeros((rows, span, -width % 128), BF),
        ],
        axis=2,
    )
    inputs_other = flip(inputs, "core", 1)
    far_blocks = [shift(inputs, "sx", -t) for t in range(1, chips)]

    time_float = time_embed.astype(F32)
    time_act = jax.nn.silu(time_float).astype(BF)
    embedding = (dot_nn(time_act, ada_w) + ada_b.astype(F32)).reshape(rows, 6, model)

    def tables(frame_ids):
        inside, offsets = frame_table(seg_lengths, frame_ids)
        pad = jnp.zeros(inside.shape[:2] + (128 - inside.shape[2],), F32)
        angles = rotary_angles(offsets, head_dim)
        return jnp.concatenate([inside, pad], axis=2), angles

    inside_near, ang_near = tables(chip_frames(sx))
    qx = jnp.where(jnp.arange(128) < seg_lengths.shape[1], 1.0 - inside_near, 0.0).astype(BF)
    kx_near = (MASKED * inside_near).astype(BF)
    bq, bi = as_row(b_qkv), as_row(b_in)
    mod_near, q, k_near, v_near = front(
        core_arg, inputs, inputs_other, w_in, bi, embedding, w_qkv, bq, ang_near,
        ("q", "k", "v"),
    )
    q, far_blocks = lax.optimization_barrier((q, far_blocks))
    far = []
    for t in range(1, chips):
        block = far_blocks[t - 1]
        inside, angles = tables(chip_frames((sx + t) % chips))
        made = front(
            core_arg, block, flip(block, "core", 1), w_in, bi, embedding, w_qkv, bq,
            angles, ("k", "v"),
        )
        far.append((*made, (MASKED * inside).astype(BF), angles))
    join = lambda n, axis: far[0][n] if chips == 2 else jnp.concatenate([f[n] for f in far], axis=axis)
    k_far, v_far, kx_far, ang_far = join(1, 1), join(2, 1), join(3, 1), join(4, 3)
    o_mine, o_give, lse = attend(
        core_arg, q, qx, k_far, k_near, kx_far, kx_near, v_far, v_near
    )

    o_other = flip(o_give, "core", 1)
    d_resid, d_o_mine, d_o_give, d_br, sums, up_sums, result, mod_two, act, d_hid, d_ff = mid(
        core_arg, inputs, o_mine, o_other, cotangent, frame_valid, embedding, w_in, bi,
        w_out, as_row(b_out), w_up, as_row(b_up), w_down, as_row(b_down),
    )
    d_o_other = flip(d_o_give, "core", 1)

    early = outer(
        core_arg, *[flat(a) for a in (mod_two, act, o_mine, o_other, d_hid, d_ff, d_br)]
    )
    early, d_o_other = lax.optimization_barrier((early, d_o_other))
    early = lax.psum_scatter(early, ("sx", "core"), scatter_dimension=0, tiled=False)

    pairs = half // 128
    queries = (q, qx, o_mine, o_give, d_o_mine, d_o_other, lse)
    keys_far = (k_far, kx_far, v_far, ang_far)
    keys_near = (k_near, kx_near, v_near, ang_near)

    def far_part(far_grads):
        made = []
        for t in range(chips - 1):
            cut = slice(2 * span * t, 2 * span * (t + 1))
            grads = [(j, [a[:, cut] if chips > 2 else a for a in g]) for j, g in far_grads]
            made.append(d_mod(core_arg, grads, w_qkv, span))
        return made

    def outers(dq, dk_far, dk, dv_far, dv):
        pieces = []
        for r in range(rows):
            block = lambda a, t: a[r, 2 * span * t : 2 * span * (t + 1)]
            others = [
                (far[t][0][r], block(dk_far, t), block(dv_far, t)) for t in range(chips - 1)
            ]
            pieces.append(qkv_outer(place, mod_near[r], dq[r], dk[r], dv[r], others))
        if rows == 1:
            return pieces[0]
        kept, given, sums = zip(*pieces)
        return total(kept), total(given), sum(sums)

    def send(blocks):
        return [shift(b, "sx", t + 1) for t, b in enumerate(blocks)]

    tie = lambda *trees: lax.optimization_barrier(trees)

    order = (0, 1, 3, 2, 4)
    cut = 128 * (pairs - 1)
    made = attend_back(core_arg, queries, (keys_far, keys_near), 0, pairs - 1, angles=ang_near)
    first_made = [made[n] for n in order]
    first_made, early = tie(first_made, early)
    early_give = rows_give([early])
    first_made, early_give = tie(first_made, early_give)
    early_recv = flip(early_give, "ry", 1)
    first_kept, first_given, first_sums = outers(*first_made)
    first_given = flip(first_given, "core", 1)
    first_blocks = [
        jnp.concatenate([first_kept[t], first_given[t]], axis=0) for t in range(1, chips)
    ]
    queries, first_blocks = tie(queries, first_blocks)
    first_got = send(first_blocks)
    made = attend_back(core_arg, queries, (keys_far, keys_near), pairs - 1, 1, angles=ang_near)
    last_made = [made[n] for n in order]
    last_made, early_recv, first_got = tie(last_made, early_recv, first_got)

    def first_half(i):
        return total(
            [jnp.where(i == 0, first_kept[0], first_given[0])] + [part_of(g, i, 2) for g in first_got]
        )

    y = lax.axis_index("ry")
    zbits = bits("rz")
    early = rows_mine([early], early_recv)
    early_give = give_half(early, "rz", zbits[0])
    first_give = first_half(1 - y)
    last_made, early_give, first_give = tie(last_made, early_give, first_give)
    early_got = near_flip(early_give, "rz", zbits[0])
    first_recv = flip(first_give, "ry", 1)
    last_kept, last_given, last_sums = outers(*last_made)
    last_made, last_given = tie(last_made, last_given)
    far_parts = far_part([(j, [m[2 * j - 1] for m in (first_made, last_made)]) for j in (1, 2)])
    near_grads = [(0, [m[0] for m in (first_made, last_made)])]
    near_grads += [(j, [m[2 * j] for m in (first_made, last_made)]) for j in (1, 2)]
    far_parts, early_got = tie(far_parts, early_got)
    early = keep_half(early, early_got, "rz", zbits[0])
    for bit in zbits[1:-1]:
        early = keep_half(early, near_flip(give_half(early, "rz", bit), "rz", bit), "rz", bit)
    early_give = give_half(early, "rz", zbits[-1])
    near_arrays, early_give = tie([g for _, g in near_grads], early_give)
    early_got = near_flip(early_give, "rz", zbits[-1])
    near_mine, near_give = d_mod(core_arg, list(enumerate(near_arrays)), w_qkv, span)
    far_parts, near_mine, near_give, last_given, first_recv, early_got = tie(
        far_parts, near_mine, near_give, last_given, first_recv, early_got
    )
    near_recv = flip(near_give, "core", 1)
    far_parts = [(mine, flip(give, "core", 1)) for mine, give in far_parts]
    last_given = flip(last_given, "core", 1)
    first_late = total([first_half(y), first_recv])
    first_give = give_half(first_late, "rz", zbits[0])
    last_blocks = [jnp.concatenate([last_kept[t], last_given[t]], axis=1) for t in range(1, chips)]
    early = keep_half(early, early_got, "rz", zbits[-1])
    far_parts, near_recv, early, last_blocks, first_give = tie(
        far_parts, near_recv, early, last_blocks, first_give
    )
    early_got = near_flip(early, "rz", zbits[-1])
    first_recv = near_flip(first_give, "rz", zbits[0])
    last_got = send(last_blocks)
    d_blocks = [(inputs, near_mine, near_recv)]
    d_blocks += [(far_blocks[t], *far_parts[t]) for t in range(chips - 1)]
    in_kept, in_given, in_sums, *far_sums = in_outer(place, d_blocks, d_resid, embedding, w_in, bi)
    in_kept, in_given, in_sums, far_sums, last_got, early_got, first_recv = tie(
        in_kept, in_given, in_sums, far_sums, last_got, early_got, first_recv
    )
    if rows > 1:
        in_kept, in_given = [jnp.sum(a.astype(F32), axis=0).astype(BF) for a in (in_kept, in_given)]
    else:
        in_kept, in_given = in_kept[0], in_given[0]

    emb_partial = jnp.stack(
        [in_sums[:, 0], in_sums[:, 1], sums[:, 4], sums[:, 2], sums[:, 3], sums[:, 0]], axis=1
    )
    over = lambda a: jnp.sum(a, axis=0)
    bias_mine = jnp.concatenate(
        [first_sums[0].reshape(3, -1), last_sums[0].reshape(3, -1)], axis=1
    )
    gap = jnp.zeros_like(bias_mine)
    b_qkv_grad = jnp.stack(
        [jnp.where(core == 0, bias_mine, gap), jnp.where(core == 0, gap, bias_mine)], axis=1
    )
    bias_sizes = [model, 3 * model, model, w_up.shape[1], model]
    biases = jnp.concatenate(
        [over(in_sums[:, 2]), b_qkv_grad.reshape(-1), over(sums[:, 5]), over(up_sums[:, 0]), over(sums[:, 1])]
    )
    vector = jnp.concatenate([emb_partial.reshape(-1), biases])

    in_given = flip(in_given, "core", 1)
    other = flip(vector, "core", 1)
    first_late = keep_half(first_late, first_recv, "rz", zbits[0])
    for bit in zbits[1:-1]:
        first_give = give_half(first_late, "rz", bit)
        first_late = keep_half(first_late, near_flip(first_give, "rz", bit), "rz", bit)
    early = join_halves(early, early_got, "rz", zbits[-1])
    for bit in zbits[-2:0:-1]:
        early = join_halves(early, near_flip(early, "rz", bit), "rz", bit)
    early_got = near_flip(early, "rz", zbits[0])
    in_given, other, first_late = tie(in_given, other, first_late)
    in_blocks = [total([in_kept[t], in_given[t]]) for t in range(1, chips)]
    vector = vector + other
    in_blocks, vector, far_sums, first_late = tie(in_blocks, vector, far_sums, first_late)
    in_got = send(in_blocks)
    vector = sum_small(vector, "sx")
    first_got = near_flip(give_half(first_late, "rz", zbits[-1]), "rz", zbits[-1])
    in_got, vector, first_got = tie(in_got, vector, first_got)
    far_got = [shift(p, "sx", t + 1) for t, p in enumerate(far_sums)]
    in_terms = [in_kept[0], in_given[0]] + in_got
    last_terms = [jnp.concatenate([last_kept[0], last_given[0]], axis=1)] + last_got
    in_give = jnp.concatenate([rows_give(in_terms), rows_give(last_terms)], axis=0)
    emb_size = rows * 6 * model
    d_embedding = vector[:emb_size].reshape(rows, 6 * model).astype(BF)
    biases = vector[emb_size:]
    shares, at = [], 0
    for size in bias_sizes:
        share = size // seq
        shares.append(lax.dynamic_slice_in_dim(biases, at + seq_index * share, share, 0))
        at += size
    width_share = model // seq
    act_share = lax.dynamic_slice_in_dim(time_act, seq_index * width_share, width_share, 1)
    shares = jnp.concatenate(shares)
    bias_share = shares.shape[0]
    shares = jnp.concatenate([shares[None], jnp.zeros((rows - 1, bias_share), F32)], axis=0)
    joined = jnp.concatenate([shares, act_share.astype(F32), d_embedding.astype(F32)], axis=1)
    first_late = keep_half(first_late, first_got, "rz", zbits[-1])
    time_float, in_give, joined, first_late = tie(time_float, in_give, joined, first_late)
    in_recv = flip(in_give, "ry", 1)
    joined = gather_small(joined, "ry")
    for bit in zbits[:0:-1]:
        first_late = join_halves(first_late, near_flip(first_late, "rz", bit), "rz", bit)
    _, silu_pull = jax.vjp(jax.nn.silu, time_float)
    time_grad = ada(d_embedding, ada_w, True)
    in_mine = [total([part_of(t, y, 2) for t in terms]) for terms in (in_terms, last_terms)]
    in_mine = jnp.concatenate(in_mine, axis=0)
    joined, in_recv, time_grad, in_mine, early_got, first_late = tie(
        joined, in_recv, time_grad, in_mine, early_got, first_late
    )
    time_grad = silu_pull(time_grad)[0]
    in_mine = total([in_mine, in_recv])
    early = join_halves(early, early_got, "rz", zbits[0])
    in_mine, first_late, early = tie(in_mine, first_late, early)
    early_other = flip(early, "ry", 1)
    for n, bit in enumerate(bits("rz")):
        in_got = near_flip(in_mine, "rz", bit)
        far_bit = bits("rz")[::-1][n]
        joined = jnp.concatenate([joined, near_flip(joined, "rz", far_bit)], axis=0)
        if n == 1:
            noisy_grad, cond_grad, text_grad = d_in(
                inputs, d_resid, embedding, keep, w_in, bi, [near_mine, near_recv] + far_got, mel
            )
            in_got, joined, noisy_grad = tie(in_got, joined, noisy_grad)
        in_mine = total([in_mine, in_got])
        if n == 0:
            first_got = near_flip(first_late, "rz", zbits[0])
            in_mine, joined, first_got = tie(in_mine, joined, first_got)
            first_late = join_halves(first_late, first_got, "rz", zbits[0])
            first_other = flip(first_late, "ry", 1)
        else:
            in_mine, joined = tie(in_mine, joined)
    in_mine, noisy_grad = tie(in_mine, noisy_grad)
    in_recv = flip(in_mine, "ry", 1)
    all_act = joined[:, bias_share : bias_share + width_share].astype(BF)
    all_emb = joined[:, bias_share + width_share :]
    ada_w_grad = dot_tn(all_act, all_emb.astype(BF))
    early = by_row(early, early_other).astype(F32)
    block = model // seq
    w_up_grad = jnp.concatenate([early[:block], early[block : 2 * block]], axis=1)
    w_down_grad = early[2 * block : 4 * block]
    w_out_grad = early[4 * block :]
    in_recv, ada_w_grad, first_other, w_up_grad, w_down_grad, w_out_grad = tie(
        in_recv, ada_w_grad, first_other, w_up_grad, w_down_grad, w_out_grad
    )
    share = in_mine.shape[0] // 2
    w_in_grad = by_row(in_mine[:share], in_recv[:share])[:, :width].astype(F32).T
    last_late = by_row(in_mine[share:], in_recv[share:])

    low, high = jnp.where(y == 0, first_late, first_other), jnp.where(y == 0, first_other, first_late)
    first_late = [jnp.where(core == 0, low, high), jnp.where(core == 0, high, low)]
    low, high = last_late[:, : 3 * 128], last_late[:, 3 * 128 :]
    last_late = [jnp.where(core == 0, low, high), jnp.where(core == 0, high, low)]
    w_qkv_grad = jnp.concatenate(
        [
            part[c][:, j * size : (j + 1) * size].astype(F32)
            for j in range(3)
            for c in range(2)
            for part, size in ((first_late, cut), (last_late, 128))
        ],
        axis=1,
    )
    shares = jnp.sum(joined[:, :bias_share], axis=0)
    b_in_grad, b_qkv_grad, b_out_grad, b_up_grad, b_down_grad = jnp.split(
        shares, [sum(bias_sizes[:n]) // seq for n in range(1, 5)]
    )
    emb_share = 6 * model // seq
    ada_b_grad = lax.dynamic_slice_in_dim(
        jnp.sum(all_emb, axis=0), seq_index * emb_share, emb_share, 0
    )
    return (
        result,
        noisy_grad,
        cond_grad,
        text_grad,
        time_grad,
        w_in_grad,
        b_in_grad,
        ada_w_grad,
        ada_b_grad,
        w_qkv_grad,
        b_qkv_grad,
        w_out_grad,
        b_out_grad,
        w_up_grad,
        b_up_grad,
        w_down_grad,
        b_down_grad,
    )


def solution(mesh):
    rows, seq = mesh.shape["rows"], mesh.shape["seq"]
    mesh = Mesh(mesh.devices.reshape(rows // 2, 2, seq // 2, 2), ("rz", "ry", "sx", "core"))
    r, s = ("rz", "ry"), ("sx", "core")
    in_specs = (
        (P(r, s, None),) * 3 + (P(r, None),) * 4 + (P(),) * 12 + (P(r, s, None),)
    )
    out_specs = (
        (P(r, s, None),) * 4
        + (P(r, None), P(None, s), P(s))
        + (P(s, None), P(s)) * 5
    )
    return jax.shard_map(shards, mesh=mesh, in_specs=in_specs, out_specs=out_specs, check_vma=False)
```

```python
import functools
import math

import jax
import jax.numpy as jnp
from jax import lax
from jax.experimental import pallas as pl
from jax.experimental.pallas import tpu as pltpu
from jax.sharding import Mesh, PartitionSpec as P

HEADS = 16
EPS = 1e-06
THETA = 10000.0
MASKED = -1e30
F32 = jnp.float32
BF = jnp.bfloat16
MIB = 2**20
QUICK = pl.CostEstimate(flops=1, bytes_accessed=1, transcendentals=0)


def dot_nn(a, b):
    return jnp.dot(a, b, preferred_element_type=F32)


def dot_tn(a, b):
    return lax.dot_general(a, b, (((0,), (0,)), ((), ())), preferred_element_type=F32)


def dot_nt(a, b):
    return lax.dot_general(a, b, (((1,), (1,)), ((), ())), preferred_element_type=F32)


def shift(v, axis, step):
    size = lax.axis_size(axis)
    return lax.ppermute(v, axis, [(i, (i + step) % size) for i in range(size)])


def flip(v, axis, bit):
    size = lax.axis_size(axis)
    return lax.ppermute(v, axis, [(i, i ^ bit) for i in range(size)])


def gray(i):
    return i ^ (i >> 1)


def near_flip(v, axis, bit):
    size = lax.axis_size(axis)
    place = {gray(i): i for i in range(size)}
    return lax.ppermute(v, axis, [(i, place[gray(i) ^ bit]) for i in range(size)])


def bits(axis):
    size = lax.axis_size(axis)
    assert size & (size - 1) == 0
    return [1 << b for b in range(size.bit_length() - 1)]


def sum_small(v, axis):
    for bit in bits(axis):
        v = v + flip(v, axis, bit)
    return v


def gather_small(v, axis):
    for bit in bits(axis):
        v = jnp.concatenate([v, flip(v, axis, bit)], axis=0)
    return v


def pick(v, index):
    return lax.dynamic_index_in_dim(v, index, 0, keepdims=False)


def part_of(v, index, count):
    size = v.shape[0] // count
    return lax.dynamic_slice_in_dim(v, index * size, size, 0)


def total(terms):
    acc = terms[0].astype(F32)
    for term in terms[1:]:
        acc = acc + term.astype(F32)
    return acc.astype(BF)


def rows_give(terms):
    return total([part_of(t, 1 - lax.axis_index("ry"), 2) for t in terms])


def rows_mine(terms, recv):
    return total([part_of(t, lax.axis_index("ry"), 2) for t in terms] + [recv])


def side(axis, bit):
    return (gray(lax.axis_index(axis)) // bit) % 2


def give_half(v, axis, bit):
    return part_of(v, 1 - side(axis, bit), 2)


def keep_half(v, recv, axis, bit):
    return total([part_of(v, side(axis, bit), 2), recv])


def join_halves(mine, recv, axis, bit):
    low = side(axis, bit) == 0
    return jnp.concatenate([jnp.where(low, mine, recv), jnp.where(low, recv, mine)], axis=0)


def by_row(mine, recv):
    low = lax.axis_index("ry") == 0
    return jnp.concatenate([jnp.where(low, mine, recv), jnp.where(low, recv, mine)], axis=0)


def sum_chips(blocks):
    return list(blocks[0]) + [shift(total(blocks[t]), "sx", t) for t in range(1, len(blocks))]


def turn(x, cos, sin, lane):
    partner = jnp.where(lane % 64 < 32, pltpu.roll(x, 96, 1), pltpu.roll(x, 32, 1))
    return x * cos + partner * sin


def wide_tables(angles):
    cos, sin = angles[0], angles[1]
    return (
        jnp.concatenate([cos, cos, cos, cos], axis=0).T,
        jnp.concatenate([-sin, sin, -sin, sin], axis=0).T,
    )


def front_kernel(core, x0_ref, x1_ref, win_ref, bin_ref, emb_ref, *rest, parts):
    weights = rest[: 2 * len(parts)]
    angle_ref, mod_ref = rest[2 * len(parts) : 2 * len(parts) + 2]
    outs = rest[2 * len(parts) + 2 :]
    x = jnp.where(pl.program_id(1) == 0, x0_ref[...], x1_ref[...])[:, : win_ref.shape[0]]
    angles = angle_ref[...]
    span = x0_ref.shape[0]
    angles = jnp.where(pl.program_id(1) == 0, angles[:, :, :span], angles[:, :, span:])
    cos, sin = wide_tables(angles)
    resid = dot_nn(x, win_ref[...]) + bin_ref[...]
    center = resid - jnp.mean(resid, axis=1, keepdims=True)
    inv = lax.rsqrt(jnp.mean(center * center, axis=1, keepdims=True) + EPS)
    mod = (center * inv * (1.0 + emb_ref[1:2, :]) + emb_ref[0:1, :]).astype(BF)
    mod_ref[...] = mod.T
    lane = lax.broadcasted_iota(jnp.int32, (1, 128), 1)
    for n, part in enumerate(parts):
        y = dot_nn(mod, weights[2 * n][...]) + weights[2 * n + 1][...]
        if part == "v":
            outs[n][...] = y.astype(BF)
            continue
        scale = 0.125 if part == "q" else 1.0
        for t in range(0, y.shape[1], 128):
            z = turn(y[:, t : t + 128], cos, sin, lane)
            outs[n][:, t : t + 128] = (z * scale).astype(BF)


def front(core, x0, x1, w_in, b_in, emb, w_qkv, b_qkv, angles, parts):
    rows, span, width = x0.shape
    n = 2 * span
    model = w_in.shape[1]
    half = model // 2
    place = {"q": 0, "k": 1, "v": 2}
    one = pl.BlockSpec((None, span, width), lambda r, i, c: (r, 0, 0))
    frame = lambda w: pl.BlockSpec((None, span, w), lambda r, i, c: (r, i, 0))
    whole = lambda a, b: pl.BlockSpec((a, b), lambda r, i, c: (0, 0))
    w_specs, w_args = [], []
    for part in parts:
        j = place[part]
        w_specs.append(pl.BlockSpec((model, half), lambda r, i, c, j=j: (0, 2 * j + c[0])))
        w_specs.append(pl.BlockSpec((1, half), lambda r, i, c, j=j: (0, 2 * j + c[0])))
        w_args += [w_qkv, b_qkv]
    return pl.pallas_call(
        functools.partial(front_kernel, parts=parts),
        grid_spec=pltpu.PrefetchScalarGridSpec(
            num_scalar_prefetch=1,
            grid=(rows, 2),
            in_specs=[one, one, whole(*w_in.shape), whole(1, model)]
            + [pl.BlockSpec((None, 6, model), lambda r, i, c: (r, 0, 0))]
            + w_specs
            + [pl.BlockSpec((None, 2, 32, n), lambda r, i, c: (r, 0, 0, 0))],
            out_specs=[pl.BlockSpec((None, None, model, span), lambda r, i, c: (r, i, 0, 0))]
            + [frame(half)] * len(parts),
        ),
        out_shape=[jax.ShapeDtypeStruct((rows, 2, model, span), BF)]
        + [jax.ShapeDtypeStruct((rows, n, half), BF)] * len(parts),
        compiler_params=pltpu.CompilerParams(vmem_limit_bytes=60 * MIB),
        cost_estimate=QUICK,
        name="front",
    )(core, x0, x1, w_in, b_in, emb, *w_args, angles)


def ada_kernel(t_ref, w_ref, out_ref, *, turned):
    out_ref[...] = (dot_nt if turned else dot_nn)(t_ref[...], w_ref[...])


def ada(t, w, turned):
    rows = t.shape[0]
    n = w.shape[0] if turned else w.shape[1]
    step = 256 if turned else 1024
    block = (step, w.shape[1]) if turned else (w.shape[0], step)
    return pl.pallas_call(
        functools.partial(ada_kernel, turned=turned),
        grid=(n // step,),
        in_specs=[
            pl.BlockSpec(t.shape, lambda i: (0, 0)),
            pl.BlockSpec(block, lambda i: (i, 0) if turned else (0, i)),
        ],
        out_specs=pl.BlockSpec((rows, step), lambda i: (0, i)),
        out_shape=jax.ShapeDtypeStruct((rows, n), F32),
        compiler_params=pltpu.CompilerParams(vmem_limit_bytes=60 * MIB),
        cost_estimate=QUICK,
        name="ada",
    )(t, w)


def mid_kernel(
    core, x_ref, om_ref, oo_ref, g_hbm, valid_ref, emb_ref,
    win_ref, bin_ref, wom_ref, woo_ref, bout_ref, wup_hbm, bup_ref, wdn_hbm, bdn_ref,
    dom_ref, doo_ref, sums_ref, bupg_ref,
    out_hbm, mod_hbm, act_hbm, dhid_hbm, dff_hbm, dres_hbm, dbr_hbm,
    slope_ref, wup_ref, wdn_ref, out_ref, mod_ref, act_ref, dhid_ref, dff_ref, dres_ref, dbr_ref,
    g_ref, come, go,
):
    hidden_width = wup_ref.shape[1]
    step = 512
    row = pl.program_id(0)
    fetch_up = pltpu.make_async_copy(wup_hbm, wup_ref, come.at[0])
    fetch_down = pltpu.make_async_copy(wdn_hbm, wdn_ref, come.at[1])
    fetch_g = pltpu.make_async_copy(g_hbm.at[row], g_ref, come.at[2])
    fetch_up.start()
    fetch_down.start()
    fetch_g.start()
    gone = []

    def leave(ref, hbm):
        copy = pltpu.make_async_copy(ref, hbm.at[row], go.at[len(gone)])
        copy.start()
        gone.append(copy)

    gate_one, shift_two = emb_ref[2:3, :], emb_ref[3:4, :]
    scale_two, gate_two = emb_ref[4:5, :], emb_ref[5:6, :]
    total = lambda v: jnp.sum(v, axis=0, keepdims=True)
    mean = lambda v: jnp.mean(v, axis=1, keepdims=True)
    resid = dot_nn(x_ref[:, : win_ref.shape[0]], win_ref[...]) + bin_ref[...]
    branch = dot_nn(om_ref[...], wom_ref[...]) + dot_nn(oo_ref[...], woo_ref[...]) + bout_ref[...]
    branch = branch * valid_ref[...]
    resid = resid + gate_one * branch
    center = resid - mean(resid)
    inv = lax.rsqrt(mean(center * center) + EPS)
    normed = center * inv
    mod = (normed * (1.0 + scale_two) + shift_two).astype(BF)
    mod_ref[...] = mod
    leave(mod_ref, mod_hbm)
    fetch_up.wait()
    fetch_down.wait()
    ff = None
    for j in range(0, hidden_width, step):
        h = dot_nn(mod, wup_ref[:, j : j + step]) + bup_ref[:, j : j + step]
        square = h * h
        t = jnp.tanh(h * (0.7978845608028654 + 0.035677408136300125 * square))
        up = 0.5 + 0.5 * t
        act = (h * up).astype(BF)
        act_ref[:, j : j + step] = act
        slope = up + h * (0.5 - 0.5 * t * t) * (0.7978845608028654 + 0.10703222440890037 * square)
        slope_ref[:, j : j + step] = slope.astype(BF)
        part = dot_nn(act, wdn_ref[j : j + step, :])
        ff = part if ff is None else ff + part
    leave(act_ref, act_hbm)
    ff = ff + bdn_ref[...]
    out_ref[...] = (resid + gate_two * ff).astype(BF)
    leave(out_ref, out_hbm)
    fetch_g.wait()
    g = g_ref[...].astype(F32)
    sums_ref[0:1, :] = total(g * ff)
    d_ff = (g * gate_two).astype(BF)
    dff_ref[...] = d_ff
    leave(dff_ref, dff_hbm)
    sums_ref[1:2, :] = total(d_ff.astype(F32))
    d_mod = None
    for j in range(0, hidden_width, step):
        d_act = dot_nt(d_ff, wdn_ref[j : j + step, :])
        d_hid = (d_act * slope_ref[:, j : j + step].astype(F32)).astype(BF)
        dhid_ref[:, j : j + step] = d_hid
        bupg_ref[:, j : j + step] = total(d_hid.astype(F32))
        part = dot_nt(d_hid, wup_ref[:, j : j + step])
        d_mod = part if d_mod is None else d_mod + part
    leave(dhid_ref, dhid_hbm)
    sums_ref[2:3, :] = total(d_mod)
    sums_ref[3:4, :] = total(d_mod * normed)
    u = d_mod * (1.0 + scale_two)
    d_res = g + inv * (u - mean(u) - normed * mean(u * normed))
    dres_ref[...] = d_res
    leave(dres_ref, dres_hbm)
    sums_ref[4:5, :] = total(d_res * branch)
    d_branch = (d_res * gate_one * valid_ref[...]).astype(BF)
    dbr_ref[...] = d_branch
    leave(dbr_ref, dbr_hbm)
    sums_ref[5:6, :] = total(d_branch.astype(F32))
    dom_ref[...] = dot_nt(d_branch, wom_ref[...]).astype(BF)
    doo_ref[...] = dot_nt(d_branch, woo_ref[...]).astype(BF)
    for copy in gone:
        copy.wait()


def mid(core, x, o_mine, o_other, g, valid, emb, w_in, b_in, w_out, b_out, w_up, b_up, w_down, b_down):
    rows, span, width = x.shape
    model, hidden = w_up.shape
    half = model // 2
    frame = lambda w: pl.BlockSpec((None, span, w), lambda r, c: (r, 0, 0))
    whole = lambda a, b: pl.BlockSpec(
        (a, b), lambda r, c: (0, 0), pipeline_mode=pl.Buffered(buffer_count=1)
    )
    out_half = lambda f: pl.BlockSpec(
        (half, model), lambda r, c: (f(c[0]), 0), pipeline_mode=pl.Buffered(buffer_count=1)
    )
    anywhere = pl.BlockSpec(memory_space=pl.ANY)
    shape = lambda w, t: jax.ShapeDtypeStruct((rows, span, w), t)
    return pl.pallas_call(
        mid_kernel,
        grid_spec=pltpu.PrefetchScalarGridSpec(
            num_scalar_prefetch=1,
            grid=(rows,),
            in_specs=[
                frame(width), frame(half), frame(half), anywhere, frame(1),
                pl.BlockSpec((None, 6, model), lambda r, c: (r, 0, 0)),
                whole(*w_in.shape), whole(1, model),
                out_half(lambda c: c), out_half(lambda c: 1 - c), whole(1, model),
                anywhere, whole(1, hidden), anywhere, whole(1, model),
            ],
            out_specs=[
                frame(half), frame(half),
                pl.BlockSpec((None, 8, model), lambda r, c: (r, 0, 0)),
                pl.BlockSpec((None, 1, hidden), lambda r, c: (r, 0, 0)),
            ] + [anywhere] * 7,
            scratch_shapes=[
                pltpu.VMEM((span, hidden), BF),
                pltpu.VMEM((model, hidden), BF),
                pltpu.VMEM((hidden, model), BF),
                pltpu.VMEM((span, model), BF),
                pltpu.VMEM((span, model), BF),
                pltpu.VMEM((span, hidden), BF),
                pltpu.VMEM((span, hidden), BF),
                pltpu.VMEM((span, model), BF),
                pltpu.VMEM((span, model), F32),
                pltpu.VMEM((span, model), BF),
                pltpu.VMEM((span, model), BF),
                pltpu.SemaphoreType.DMA((3,)),
                pltpu.SemaphoreType.DMA((7,)),
            ],
        ),
        out_shape=[
            shape(half, BF), shape(half, BF),
            jax.ShapeDtypeStruct((rows, 8, model), F32),
            jax.ShapeDtypeStruct((rows, 1, hidden), F32),
            shape(model, BF), shape(model, BF), shape(hidden, BF), shape(hidden, BF),
            shape(model, BF), shape(model, F32), shape(model, BF),
        ],
        compiler_params=pltpu.CompilerParams(vmem_limit_bytes=60 * MIB),
        cost_estimate=QUICK,
        name="mid",
    )(core, x, o_mine, o_other, g, valid, emb, w_in, b_in, w_out, w_out, b_out, w_up, b_up, w_down, b_down)


def outer_kernel(core, mod_ref, act_ref, om_ref, oo_ref, dhid_ref, dff_ref, dbr_ref, out_ref, left):
    step = pl.program_id(0)
    seq, r, model = out_ref.shape

    def put(rows, right):
        product = dot_nn(rows, right).astype(BF)
        for n in range(seq):
            out_ref[n] = product[n * r : (n + 1) * r]

    @pl.when(step == 0)
    def _():
        left[:model, :] = mod_ref[...].T

    @pl.when(step == 2)
    def _():
        left[...] = act_ref[...].T

    @pl.when(step == 4)
    def _():
        mine, other = om_ref[...], oo_ref[...]
        low = core[0] == 0
        half = model // 2
        left[:half, :] = jnp.where(low, mine, other).T
        left[half:model, :] = jnp.where(low, other, mine).T

    @pl.when(step < 2)
    def _():
        put(left[:model, :], dhid_ref[...])

    for j in range(2):

        @pl.when(step == 2 + j)
        def _():
            at = [(2 * n + j) * r for n in range(seq)]
            put(jnp.concatenate([left[a : a + r, :] for a in at], axis=0), dff_ref[...])

    @pl.when(step == 4)
    def _():
        put(left[:model, :], dbr_ref[...])


def outer(core, mod, act, o_mine, o_other, d_hid, d_ff, d_br):
    n, model = mod.shape
    seq = lax.axis_size("sx") * 2
    rows = model // seq
    once = lambda w: pl.BlockSpec((n, w), lambda i, c: (0, 0))
    return pl.pallas_call(
        outer_kernel,
        grid_spec=pltpu.PrefetchScalarGridSpec(
            num_scalar_prefetch=1,
            grid=(5,),
            in_specs=[
                once(model), once(act.shape[1]), once(model // 2), once(model // 2),
                pl.BlockSpec((n, model), lambda i, c: (0, jnp.minimum(i, 1))),
                once(model), once(model),
            ],
            out_specs=pl.BlockSpec((seq, rows, model), lambda i, c: (0, i, 0)),
            scratch_shapes=[pltpu.VMEM((act.shape[1], n), BF)],
        ),
        out_shape=jax.ShapeDtypeStruct((seq, 5 * rows, model), BF),
        compiler_params=pltpu.CompilerParams(vmem_limit_bytes=60 * MIB),
        cost_estimate=QUICK,
        name="outer",
    )(core, mod, act, o_mine, o_other, d_hid, d_ff, d_br)


def qkv_outer_kernel(place, *refs, far):
    near_ref, dq_ref, dk_ref, dv_ref = refs[:4]
    far_refs = refs[4 : 4 + 3 * far]
    keep_ref, give_ref, sums_ref = refs[-3:]
    chips, rows, width = keep_ref.shape
    width //= 3
    span = near_ref.shape[2]
    acc_q, acc = None, None
    add = lambda a, b: b if a is None else a + b
    for i in range(2):
        cut = slice(i * span, (i + 1) * span)
        both = jnp.concatenate([dk_ref[cut, :], dv_ref[cut, :]], axis=1)
        acc_q = add(acc_q, dot_nn(near_ref[i], dq_ref[cut, :]))
        acc = add(acc, dot_nn(near_ref[i], both))
    for f in range(far):
        mod_ref, dkf_ref, dvf_ref = far_refs[3 * f : 3 * f + 3]
        for i in range(2):
            cut = slice(i * span, (i + 1) * span)
            both = jnp.concatenate([dkf_ref[cut, :], dvf_ref[cut, :]], axis=1)
            acc = add(acc, dot_nn(mod_ref[i], both))
    parts = [acc_q.astype(BF), acc[:, :width].astype(BF), acc[:, width:].astype(BF)]
    column = lambda ref: jnp.sum(ref[...].astype(F32), axis=0, keepdims=True)
    sums = [column(dq_ref), column(dk_ref), column(dv_ref)]
    for f in range(far):
        for j in (1, 2):
            sums[j] = sums[j] + column(far_refs[3 * f + j])
    for j in range(3):
        sums_ref[:, j * width : (j + 1) * width] = jnp.broadcast_to(sums[j], (8, width))
    for side in range(2):
        for out_ref, core in ((keep_ref, side), (give_ref, 1 - side)):
            @pl.when(place[1] == core)
            def _():
                for n in range(side, 2 * chips, 2):
                    chip = (n // 2 + chips - place[0]) % chips
                    for j, part in enumerate(parts):
                        out_ref[chip, :, j * width : (j + 1) * width] = part[
                            n * rows : (n + 1) * rows
                        ]


def qkv_outer(place, mod_near, dq, dk, dv, far):
    model = mod_near.shape[1]
    width = dq.shape[1]
    chips = lax.axis_size("sx")
    shape = (chips, model // (2 * chips), 3 * width)
    args = [mod_near, dq, dk, dv]
    whole = lambda a: pl.BlockSpec(a.shape, lambda i, c: (0,) * a.ndim)
    for item in far:
        args += list(item)
    specs = [whole(a) for a in args]
    return pl.pallas_call(
        functools.partial(qkv_outer_kernel, far=len(far)),
        grid_spec=pltpu.PrefetchScalarGridSpec(
            num_scalar_prefetch=1,
            grid=(1,),
            in_specs=specs,
            out_specs=[pl.BlockSpec(shape, lambda i, c: (0,) * 3)] * 2
            + [pl.BlockSpec((8, 3 * width), lambda i, c: (0, 0))],
        ),
        out_shape=[jax.ShapeDtypeStruct(shape, BF)] * 2
        + [jax.ShapeDtypeStruct((8, 3 * width), F32)],
        compiler_params=pltpu.CompilerParams(vmem_limit_bytes=60 * MIB),
        cost_estimate=QUICK,
        name="qkv_outer",
    )(place, *args)


def d_mod_kernel(core, *refs, parts):
    acc, at = None, 0
    for n, count in enumerate(parts):
        left = jnp.concatenate([ref[...] for ref in refs[at : at + count]], axis=1)
        part = dot_nt(left, refs[sum(parts) + n][...])
        acc = part if acc is None else acc + part
        at += count
    mine_ref, other_ref = refs[-2:]

    @pl.when(pl.program_id(1) % 2 == 0)
    def _():
        mine_ref[...] = acc.astype(BF)

    @pl.when(pl.program_id(1) % 2 == 1)
    def _():
        other_ref[...] = acc.astype(BF)


def d_mod(core, grads, w_qkv, span):
    arrays = [a for _, g in grads for a in g]
    rows, n = arrays[0].shape[:2]
    model = w_qkv.shape[0]
    half = model // 2
    specs = [pl.BlockSpec((None, span, a.shape[2]), lambda r, i, c: (r, i, 0)) for a in arrays]
    specs += [
        pl.BlockSpec((model, half), lambda r, i, c, j=j: (0, 2 * j + c[0])) for j, _ in grads
    ]
    out = pl.BlockSpec((None, span, model), lambda r, i, c: (r, 0, 0))
    return pl.pallas_call(
        functools.partial(d_mod_kernel, parts=tuple(len(g) for _, g in grads)),
        grid_spec=pltpu.PrefetchScalarGridSpec(
            num_scalar_prefetch=1,
            grid=(rows, n // span),
            in_specs=specs,
            out_specs=[out, out],
        ),
        out_shape=[jax.ShapeDtypeStruct((rows, span, model), BF)] * 2,
        compiler_params=pltpu.CompilerParams(vmem_limit_bytes=60 * MIB),
        cost_estimate=QUICK,
        name="d_mod",
    )(core, *arrays, *[w_qkv] * len(grads))


def norm_back(normed, inv, upstream):
    mean = lambda v: jnp.mean(v, axis=1, keepdims=True)
    return inv * (upstream - mean(upstream) - normed * mean(upstream * normed))


def first_norm(x_ref, win_ref, bin_ref):
    resid = dot_nn(x_ref[:, : win_ref.shape[0]], win_ref[...]) + bin_ref[...]
    center = resid - jnp.mean(resid, axis=1, keepdims=True)
    inv = lax.rsqrt(jnp.mean(center * center, axis=1, keepdims=True) + EPS)
    return center * inv, inv


def in_outer_kernel(place, dres_hbm, emb_ref, win_ref, bin_ref, *refs, blocks):
    ins, refs = [refs[3 * n : 3 * n + 3] for n in range(blocks)], refs[3 * blocks :]
    keep_out, give_out, sums_ref = refs[:3]
    far_out, refs = refs[3 : 2 + blocks], refs[2 + blocks :]
    turned, joined, sems, dres_ref, *later = refs
    row = pl.program_id(0)
    come = [pltpu.make_async_copy(dres_hbm.at[row], dres_ref, sems.at[0])]
    far_hbm = [ref for block in ins[1:] for ref in block]
    for n, (src, dst) in enumerate(zip(far_hbm, later)):
        come.append(pltpu.make_async_copy(src.at[row], dst, sems.at[n + 1]))
    for copy in come:
        copy.start()
    ins = [ins[0]] + [later[3 * n : 3 * n + 3] for n in range(blocks - 1)]
    span = ins[0][0].shape[0]
    total = lambda v: jnp.sum(v, axis=0, keepdims=True)
    sums_ref[...] = jnp.zeros(sums_ref.shape, F32)
    for n, (x_ref, mine_ref, recv_ref) in enumerate(ins):
        cut = slice(n * span, (n + 1) * span)
        if n:
            for copy in come[3 * n - 2 : 3 * n + 1]:
                copy.wait()
        normed, inv = first_norm(x_ref, win_ref, bin_ref)
        d = mine_ref[...].astype(F32) + recv_ref[...].astype(F32)
        if n:
            far_out[n - 1][...] = d.astype(BF)
        sums_ref[0:1, :] += total(d)
        sums_ref[1:2, :] += total(d * normed)
        d = norm_back(normed, inv, d * (1.0 + emb_ref[1:2, :]))
        if n == 0:
            come[0].wait()
        d = (d if n else d + dres_ref[...]).astype(BF)
        sums_ref[2:3, :] += total(d.astype(F32))
        turned[:, cut] = d.T
        joined[cut, :] = x_ref[...]
    chips, rows = keep_out.shape[0], keep_out.shape[1]
    for t in range(chips):
        block = ((place[0] + t) % chips) * 2
        for out, core in ((give_out, 1 - place[1]), (keep_out, place[1])):
            at = pl.ds(pl.multiple_of((block + core) * rows, rows), rows)
            out[t] = dot_nn(turned[at, :], joined[...]).astype(BF)


def in_outer(place, blocks, d_res, emb, w_in, b_in):
    x = blocks[0][0]
    rows, span, width = x.shape
    model = w_in.shape[1]
    chips = lax.axis_size("sx")
    block = model // (2 * chips)
    frame = lambda w: pl.BlockSpec((None, span, w), lambda r, c: (r, 0, 0))
    whole = lambda a, b: pl.BlockSpec((a, b), lambda r, c: (0, 0))
    out = pl.BlockSpec((None, chips, block, width), lambda r, c: (r, 0, 0, 0))
    anywhere = pl.BlockSpec(memory_space=pl.ANY)
    return pl.pallas_call(
        functools.partial(in_outer_kernel, blocks=len(blocks)),
        grid_spec=pltpu.PrefetchScalarGridSpec(
            num_scalar_prefetch=1,
            grid=(rows,),
            in_specs=[
                anywhere, pl.BlockSpec((None, 6, model), lambda r, c: (r, 0, 0)),
                whole(*w_in.shape), whole(1, model), frame(width), frame(model), frame(model),
            ] + [anywhere] * (3 * len(blocks) - 3),
            out_specs=[out, out, pl.BlockSpec((None, 8, model), lambda r, c: (r, 0, 0))]
            + [frame(model)] * (len(blocks) - 1),
            scratch_shapes=[
                pltpu.VMEM((model, len(blocks) * span), BF),
                pltpu.VMEM((len(blocks) * span, width), BF),
                pltpu.SemaphoreType.DMA((3 * len(blocks) - 2,)),
                pltpu.VMEM((span, model), F32),
            ] + [pltpu.VMEM((span, w), BF) for w in (width, model, model)] * (len(blocks) - 1),
        ),
        out_shape=[
            jax.ShapeDtypeStruct((rows, chips, block, width), BF),
            jax.ShapeDtypeStruct((rows, chips, block, width), BF),
            jax.ShapeDtypeStruct((rows, 8, model), F32),
        ] + [jax.ShapeDtypeStruct((rows, span, model), BF)] * (len(blocks) - 1),
        compiler_params=pltpu.CompilerParams(vmem_limit_bytes=60 * MIB),
        cost_estimate=QUICK,
        name="in_outer",
    )(place, d_res, emb, w_in, b_in, *[a for b in blocks for a in b])


def d_in_kernel(*refs, parts, mel):
    x_ref, dres_ref, emb_ref, keep_ref, win_ref, bin_ref = refs[:6]
    noisy_ref, cond_ref, text_ref = refs[6 + parts :]
    normed, inv = first_norm(x_ref, win_ref, bin_ref)
    d = refs[6][...].astype(F32)
    for ref in refs[7 : 6 + parts]:
        d = d + ref[...].astype(F32)
    d = norm_back(normed, inv, d * (1.0 + emb_ref[1:2, :]))
    d_in = dot_nt((dres_ref[...] + d).astype(BF), win_ref[...])
    noisy_ref[...] = d_in[:, :mel]
    cond_ref[...] = d_in[:, mel : 2 * mel] * keep_ref[:, 0:1]
    text_ref[...] = d_in[:, 2 * mel :] * keep_ref[:, 1:2]


def d_in(x, d_res, emb, keep, w_in, b_in, parts, mel):
    rows, span, width = x.shape
    model = w_in.shape[1]
    frame = lambda w: pl.BlockSpec((None, span, w), lambda r: (r, 0, 0))
    whole = lambda a, b: pl.BlockSpec((a, b), lambda r: (0, 0))
    sizes = [mel, mel, w_in.shape[0] - 2 * mel]
    return pl.pallas_call(
        functools.partial(d_in_kernel, parts=len(parts), mel=mel),
        grid=(rows,),
        in_specs=[
            frame(width), frame(model), pl.BlockSpec((None, 6, model), lambda r: (r, 0, 0)),
            frame(2), whole(*w_in.shape), whole(1, model),
        ] + [frame(model)] * len(parts),
        out_specs=[frame(w) for w in sizes],
        out_shape=[jax.ShapeDtypeStruct((rows, span, w), F32) for w in sizes],
        compiler_params=pltpu.CompilerParams(vmem_limit_bytes=60 * MIB),
        cost_estimate=QUICK,
        name="d_in",
    )(x, d_res, emb, keep, w_in, b_in, *parts)


def rows_of(refs, start, stop):
    parts, at = [], 0
    for ref in refs:
        size = ref.shape[0]
        lo, hi = max(start - at, 0), min(stop - at, size)
        if lo < hi:
            parts.append(ref[lo:hi, :])
        at += size
    return parts[0] if len(parts) == 1 else jnp.concatenate(parts, axis=0)


def attend_kernel(
    flag, q_ref, qx_ref, kf_ref, kn_ref, kxf_ref, kxn_ref, vf_ref, vn_ref,
    o_mine_ref, o_other_ref, l_ref, s_ref, m_ref, acc_ref,
):
    frames = s_ref.shape[1]
    span = o_mine_ref.shape[0]
    lane = lax.broadcasted_iota(jnp.int32, (1, 128), 1)
    zero = jnp.zeros((), BF)
    step = 256 if frames % 256 == 0 else frames
    apart = lambda n: pl.when(flag[0] >= -n)
    for h in range(2):
        mine = (lane // 64) == h

        @apart(2 * h)
        def _():
            q2 = jnp.concatenate([q_ref[...], qx_ref[...]], axis=1)
            top = None
            for c in range(0, frames, step):
                keys = jnp.where(mine, rows_of((kf_ref, kn_ref), c, c + step), zero)
                labels = rows_of((kxf_ref, kxn_ref), c, c + step)
                s = dot_nt(q2, jnp.concatenate([keys, labels], axis=1))
                s_ref[:, c : c + step] = s
                for t in range(0, step, 128):
                    part = s[:, t : t + 128]
                    top = part if top is None else jnp.maximum(top, part)
            m_ref[...] = jnp.broadcast_to(jnp.max(top, axis=1, keepdims=True), m_ref.shape)

        @apart(2 * h + 1)
        def _():
            top = m_ref[:, :1]
            ones = jnp.broadcast_to(jnp.where(mine, 1.0, 0.0).astype(BF), (step, 128))
            acc = None
            for c in range(0, frames, step):
                p = jnp.exp(s_ref[:, c : c + step] - top).astype(BF)
                values = jnp.where(mine, rows_of((vf_ref, vn_ref), c, c + step), zero)
                d = dot_nn(p, jnp.concatenate([values, ones], axis=1))
                acc = d if acc is None else acc + d
            if h == 0:
                acc_ref[...] = acc
                l_ref[...] = m_ref[...]
            if h == 1:
                both = acc + acc_ref[...]
                total = both[:, 128:]
                o = (both[:, :128] / total).astype(BF)
                o_mine_ref[...] = o[:span]
                o_other_ref[...] = o[span:]
                l_ref[...] = jnp.where(mine, m_ref[...], l_ref[...]) + jnp.log(total)


def attend(core, q, qx, k_far, k_near, kx_far, kx_near, v_far, v_near):
    rows, m, width = q.shape
    span = m // 2
    far, near = k_far.shape[1], k_near.shape[1]
    n = far + near
    pairs = width // 128
    at = lambda size: pl.BlockSpec((None, size, 128), lambda r, p, c: (r, 0, p))
    once = lambda size: pl.BlockSpec((None, size, 128), lambda r, p, c: (r, 0, 0))
    return pl.pallas_call(
        attend_kernel,
        grid_spec=pltpu.PrefetchScalarGridSpec(
            num_scalar_prefetch=1,
            grid=(rows, pairs),
            in_specs=[at(m), once(m), at(far), at(near), once(far), once(near), at(far), at(near)],
            out_specs=[at(span), at(span), at(m)],
            scratch_shapes=[
                pltpu.VMEM((m, n), F32),
                pltpu.VMEM((m, 128), F32),
                pltpu.VMEM((m, 256), F32),
            ],
        ),
        out_shape=[
            jax.ShapeDtypeStruct((rows, span, width), BF),
            jax.ShapeDtypeStruct((rows, span, width), BF),
            jax.ShapeDtypeStruct((rows, m, width), F32),
        ],
        compiler_params=pltpu.CompilerParams(vmem_limit_bytes=60 * MIB),
        cost_estimate=QUICK,
        name="attend",
    )(core, q, qx, k_far, k_near, kx_far, kx_near, v_far, v_near)


def split3(x, lane, rest):
    hi = x.astype(BF).astype(F32)
    mid = (x - hi).astype(BF).astype(F32)
    low = x - hi - mid
    place = lane % 64
    return jnp.where(
        place == 8, hi, jnp.where(place == 9, mid, jnp.where(place == 10, low, rest))
    ).astype(BF)


def attend_back_kernel(flag, *refs, blocks, start, finish):
    q_ref, qx_ref, om_ref, oo_ref, dom_ref, doo_ref, l_ref = refs[:7]
    refs = refs[7:]
    keys_in, refs = [refs[4 * n : 4 * n + 4] for n in range(blocks)], refs[4 * blocks :]
    if finish:
        angle_ref, refs = refs[0], refs[1:]
    if not start:
        before_ref, refs = refs[0], refs[1:]
    dq_ref, refs = refs[0], refs[1:]
    keys_out, refs = [refs[2 * n : 2 * n + 2] for n in range(blocks)], refs[2 * blocks :]
    q2, d2, k2, v2, kk, qt, dt, p_s, s_s, dq_s, dk_s, dv_s = refs
    m, n = q_ref.shape[0], kk.shape[0]
    span = om_ref.shape[0]
    lane = lax.broadcasted_iota(jnp.int32, (1, 128), 1)
    zero = jnp.zeros((), BF)
    steps = [(c, min(c + 256, n)) for c in range(0, n, 256)] if n % 128 == 0 else [(0, n)]
    cuts, at = [], 0
    for k_ref, _, _, _ in keys_in:
        cuts.append(slice(at, at + k_ref.shape[0]))
        at += k_ref.shape[0]
    apart = pl.when(flag[0] >= 0)

    @apart
    def _():
        q2[:, :128] = q_ref[...]
        q2[:, 128:] = split3(l_ref[...], lane, qx_ref[...].astype(F32))
        same = (
            lax.broadcasted_iota(jnp.int32, (128, 128), 0) // 64
            == lax.broadcasted_iota(jnp.int32, (128, 128), 1) // 64
        )
        same = jnp.where(same, 1.0, 0.0).astype(BF)
        same = jnp.concatenate([same, same], axis=0)
        for at, do_ref, o_ref in ((0, dom_ref, om_ref), (span, doo_ref, oo_ref)):
            cut = slice(at, at + span)
            prod = do_ref[...].astype(F32) * o_ref[...].astype(F32)
            hi = prod.astype(BF)
            low = (prod - hi.astype(F32)).astype(BF)
            delta = dot_nn(jnp.concatenate([hi, low], axis=1), same)
            d2[cut, :128] = do_ref[...]
            d2[cut, 128:] = split3(delta, lane, jnp.zeros((span, 128), F32))
        qt[...] = q_ref[...].T
        dt[...] = d2[:, :128].T

    for h in range(2):
        mine = (lane // 64) == h
        half = slice(h * 64, (h + 1) * 64)

        @apart
        def _():
            less = (lane - 64 * h >= 8) & (lane - 64 * h < 11)
            for cut, (k_ref, kx_ref, v_ref, _) in zip(cuts, keys_in):
                keys = jnp.where(mine, k_ref[...], zero)
                kk[cut, :] = keys
                k2[:128, cut] = keys.T
                k2[128:, cut] = jnp.where(less, -1.0, kx_ref[...].astype(F32)).astype(BF).T
                v2[:128, cut] = jnp.where(mine, v_ref[...], zero).T
            v2[128:, :] = jnp.broadcast_to(jnp.where(less, -1.0, 0.0), (n, 128)).astype(BF).T

        @apart
        def _():
            for c, e in steps:
                s = dot_nn(q2[...], k2[:, c:e])
                d = dot_nn(d2[...], v2[:, c:e])
                p = jnp.exp(s)
                p_s[:, c:e] = p.astype(BF)
                s_s[:, c:e] = (p * d).astype(BF)

        @apart
        def _():
            acc = dot_nn(s_s[...], kk[...])
            if h == 0:
                dq_s[...] = acc if start else acc + before_ref[...]
            if h == 1:
                acc = dq_s[...] + acc
                if finish:
                    cos, sin = wide_tables(angle_ref)
                    acc = turn(acc * 0.125, cos, -sin, lane)
                dq_ref[...] = acc.astype(dq_ref.dtype)

        @apart
        def _():
            for c, e in steps:
                dk_s[half, c:e] = dot_nn(qt[half, :], s_s[:, c:e])
                dv_s[half, c:e] = dot_nn(dt[half, :], p_s[:, c:e])

    @apart
    def _():
        for cut, (_, _, _, ang_ref), (dk_ref, dv_ref) in zip(cuts, keys_in, keys_out):
            cos, sin = ang_ref[0], ang_ref[1]
            turned = []
            for h in range(2):
                a, b = dk_s[64 * h : 64 * h + 32, cut], dk_s[64 * h + 32 : 64 * h + 64, cut]
                turned += [a * cos + b * sin, b * cos - a * sin]
            dk_ref[...] = jnp.concatenate(turned, axis=0).astype(BF).T
            dv_ref[...] = dv_s[:, cut].astype(BF).T


def attend_back(core, queries, blocks, first, pairs, angles=None, before=None):
    q, qx, o_mine, o_other, d_mine, d_other, lse = queries
    rows, m, width = q.shape
    span = m // 2
    sizes = [k.shape[1] for k, _, _, _ in blocks]
    n = sum(sizes)
    at = lambda size: pl.BlockSpec((None, size, 128), lambda r, p, c: (r, 0, first + p))
    out = lambda size: pl.BlockSpec((None, size, 128), lambda r, p, c: (r, 0, p))
    once = lambda size: pl.BlockSpec((None, size, 128), lambda r, p, c: (r, 0, 0))
    angle = lambda size: pl.BlockSpec((None, 2, 32, size), lambda r, p, c: (r, 0, 0, 0))
    shape = lambda size, t: jax.ShapeDtypeStruct((rows, size, pairs * 128), t)
    in_specs = [at(m), once(m), at(span), at(span), at(span), at(span), at(m)]
    args = [q, qx, o_mine, o_other, d_mine, d_other, lse]
    for size, block in zip(sizes, blocks):
        in_specs += [at(size), once(size), at(size), angle(size)]
        args += list(block)
    if angles is not None:
        in_specs.append(angle(m))
        args.append(angles)
    if before is not None:
        in_specs.append(at(m))
        args.append(before)
    twice = [size for size in sizes for _ in range(2)]
    return pl.pallas_call(
        functools.partial(
            attend_back_kernel, blocks=len(blocks), start=before is None, finish=angles is not None
        ),
        grid_spec=pltpu.PrefetchScalarGridSpec(
            num_scalar_prefetch=1,
            grid=(rows, pairs),
            in_specs=in_specs,
            out_specs=[out(m)] + [out(size) for size in twice],
            scratch_shapes=[
                pltpu.VMEM((m, 256), BF),
                pltpu.VMEM((m, 256), BF),
                pltpu.VMEM((256, n), BF),
                pltpu.VMEM((256, n), BF),
                pltpu.VMEM((n, 128), BF),
                pltpu.VMEM((128, m), BF),
                pltpu.VMEM((128, m), BF),
                pltpu.VMEM((m, n), BF),
                pltpu.VMEM((m, n), BF),
                pltpu.VMEM((m, 128), F32),
                pltpu.VMEM((128, n), F32),
                pltpu.VMEM((128, n), F32),
            ],
        ),
        out_shape=[shape(m, F32 if angles is None else BF)] + [shape(size, BF) for size in twice],
        compiler_params=pltpu.CompilerParams(vmem_limit_bytes=60 * MIB),
        cost_estimate=QUICK,
        name="attend_back",
    )(core, *args)


def frame_table(seg_lengths, frames):
    place = jnp.arange(seg_lengths.shape[1])
    upto = place[None, :] <= place[:, None]
    ends = jnp.sum(jnp.where(upto, seg_lengths[:, None, :], 0), axis=2)
    starts = ends - seg_lengths
    at = frames[None, :, None]
    inside = (at >= starts[:, None, :]) & (at < ends[:, None, :])
    offsets = frames[None, :] - jnp.sum(jnp.where(inside, starts[:, None, :], 0), axis=2)
    return inside.astype(F32), offsets


def rotary_angles(offsets, head_dim):
    halves = head_dim // 2
    frequency = jnp.exp(-math.log(THETA) * 2.0 * jnp.arange(halves, dtype=F32) / head_dim)
    angles = offsets.astype(F32)[:, None, :] * frequency[:, None]
    return jnp.stack([jnp.cos(angles), jnp.sin(angles)], axis=1)


def shards(
    noisy_mel, cond_mel, text_feat, time_embed, seg_lengths, audio_drop, text_drop, w_in, b_in,
    ada_w, ada_b, w_qkv, b_qkv, w_out, b_out, w_up, b_up, w_down, b_down, cotangent,
):
    rows, span, mel = noisy_mel.shape
    model = w_qkv.shape[0]
    half = model // 2
    head_dim = model // HEADS
    core, sx = lax.axis_index("core"), lax.axis_index("sx")
    chips = lax.axis_size("sx")
    seq = chips * 2
    seq_index = sx * 2 + core
    place = jnp.stack([sx, core]).astype(jnp.int32)
    core_arg = place[1:]
    as_row = lambda v: v.astype(F32).reshape(1, -1)
    flat = lambda a: a.reshape(-1, a.shape[-1])

    ramp = jnp.arange(span, dtype=jnp.int32)

    def chip_frames(chip):
        return jnp.concatenate([(chip * 2 + core) * span + ramp, (chip * 2 + 1 - core) * span + ramp])

    member, _ = frame_table(seg_lengths, seq_index * span + ramp)
    keep_audio = 1.0 - jnp.sum(member * audio_drop.astype(F32)[:, None, :], axis=2)
    keep_text = 1.0 - jnp.sum(member * text_drop.astype(F32)[:, None, :], axis=2)
    keep = jnp.stack([keep_audio, keep_text], axis=2)
    frame_valid = 1.0 - member[:, :, -1:]
    width = w_in.shape[0]
    inputs = jnp.concatenate(
        [
            noisy_mel,
            cond_mel * keep_audio[..., None].astype(BF),
            text_feat * keep_text[..., None].astype(BF),
            jnp.zeros((rows, span, -width % 128), BF),
        ],
        axis=2,
    )
    inputs_other = flip(inputs, "core", 1)
    far_blocks = [shift(inputs, "sx", -t) for t in range(1, chips)]

    time_float = time_embed.astype(F32)
    time_act = jax.nn.silu(time_float).astype(BF)
    embedding = (dot_nn(time_act, ada_w) + ada_b.astype(F32)).reshape(rows, 6, model)

    def tables(frame_ids):
        inside, offsets = frame_table(seg_lengths, frame_ids)
        pad = jnp.zeros(inside.shape[:2] + (128 - inside.shape[2],), F32)
        angles = rotary_angles(offsets, head_dim)
        return jnp.concatenate([inside, pad], axis=2), angles

    inside_near, ang_near = tables(chip_frames(sx))
    qx = jnp.where(jnp.arange(128) < seg_lengths.shape[1], 1.0 - inside_near, 0.0).astype(BF)
    kx_near = (MASKED * inside_near).astype(BF)
    bq, bi = as_row(b_qkv), as_row(b_in)
    mod_near, q, k_near, v_near = front(
        core_arg, inputs, inputs_other, w_in, bi, embedding, w_qkv, bq, ang_near,
        ("q", "k", "v"),
    )
    q, far_blocks = lax.optimization_barrier((q, far_blocks))
    far = []
    for t in range(1, chips):
        block = far_blocks[t - 1]
        inside, angles = tables(chip_frames((sx + t) % chips))
        made = front(
            core_arg, block, flip(block, "core", 1), w_in, bi, embedding, w_qkv, bq,
            angles, ("k", "v"),
        )
        far.append((*made, (MASKED * inside).astype(BF), angles))
    join = lambda n, axis: far[0][n] if chips == 2 else jnp.concatenate([f[n] for f in far], axis=axis)
    k_far, v_far, kx_far, ang_far = join(1, 1), join(2, 1), join(3, 1), join(4, 3)
    o_mine, o_give, lse = attend(
        core_arg, q, qx, k_far, k_near, kx_far, kx_near, v_far, v_near
    )

    o_other = flip(o_give, "core", 1)
    d_o_mine, d_o_give, sums, up_sums, result, mod_two, act, d_hid, d_ff, d_resid, d_br = mid(
        core_arg, inputs, o_mine, o_other, cotangent, frame_valid, embedding, w_in, bi,
        w_out, as_row(b_out), w_up, as_row(b_up), w_down, as_row(b_down),
    )
    d_o_other = flip(d_o_give, "core", 1)

    early = outer(
        core_arg, *[flat(a) for a in (mod_two, act, o_mine, o_other, d_hid, d_ff, d_br)]
    )
    early, d_o_other = lax.optimization_barrier((early, d_o_other))
    early = lax.psum_scatter(early, ("sx", "core"), scatter_dimension=0, tiled=False)

    pairs = half // 128
    queries = (q, qx, o_mine, o_give, d_o_mine, d_o_other, lse)
    keys_far = (k_far, kx_far, v_far, ang_far)
    keys_near = (k_near, kx_near, v_near, ang_near)

    def far_part(far_grads):
        made = []
        for t in range(chips - 1):
            cut = slice(2 * span * t, 2 * span * (t + 1))
            grads = [(j, [a[:, cut] if chips > 2 else a for a in g]) for j, g in far_grads]
            made.append(d_mod(core_arg, grads, w_qkv, span))
        return made

    def outers(dq, dk_far, dk, dv_far, dv):
        pieces = []
        for r in range(rows):
            block = lambda a, t: a[r, 2 * span * t : 2 * span * (t + 1)]
            others = [
                (far[t][0][r], block(dk_far, t), block(dv_far, t)) for t in range(chips - 1)
            ]
            pieces.append(qkv_outer(place, mod_near[r], dq[r], dk[r], dv[r], others))
        if rows == 1:
            return pieces[0]
        kept, given, sums = zip(*pieces)
        return total(kept), total(given), sum(sums)

    def send(blocks):
        return [shift(b, "sx", t + 1) for t, b in enumerate(blocks)]

    tie = lambda *trees: lax.optimization_barrier(trees)

    order = (0, 1, 3, 2, 4)
    cut = 128 * (pairs - 1)
    made = attend_back(core_arg, queries, (keys_far, keys_near), 0, pairs - 1, angles=ang_near)
    first_made = [made[n] for n in order]
    first_made, early = tie(first_made, early)
    early_give = rows_give([early])
    first_made, early_give = tie(first_made, early_give)
    early_recv = flip(early_give, "ry", 1)
    first_kept, first_given, first_sums = outers(*first_made)
    first_given = flip(first_given, "core", 1)
    first_blocks = [
        jnp.concatenate([first_kept[t], first_given[t]], axis=0) for t in range(1, chips)
    ]
    queries, first_blocks = tie(queries, first_blocks)
    first_got = send(first_blocks)
    made = attend_back(core_arg, queries, (keys_far, keys_near), pairs - 1, 1, angles=ang_near)
    last_made = [made[n] for n in order]
    last_made, early_recv, first_got = tie(last_made, early_recv, first_got)

    def first_half(i):
        return total(
            [jnp.where(i == 0, first_kept[0], first_given[0])] + [part_of(g, i, 2) for g in first_got]
        )

    y = lax.axis_index("ry")
    zbits = bits("rz")
    early = rows_mine([early], early_recv)
    early_give = give_half(early, "rz", zbits[0])
    first_give = first_half(1 - y)
    last_made, early_give, first_give = tie(last_made, early_give, first_give)
    early_got = near_flip(early_give, "rz", zbits[0])
    first_recv = flip(first_give, "ry", 1)
    last_kept, last_given, last_sums = outers(*last_made)
    last_made, last_given = tie(last_made, last_given)
    far_parts = far_part([(j, [m[2 * j - 1] for m in (first_made, last_made)]) for j in (1, 2)])
    near_grads = [(0, [m[0] for m in (first_made, last_made)])]
    near_grads += [(j, [m[2 * j] for m in (first_made, last_made)]) for j in (1, 2)]
    far_parts, early_got = tie(far_parts, early_got)
    early = keep_half(early, early_got, "rz", zbits[0])
    for bit in zbits[1:-1]:
        early = keep_half(early, near_flip(give_half(early, "rz", bit), "rz", bit), "rz", bit)
    early_give = give_half(early, "rz", zbits[-1])
    near_arrays, early_give = tie([g for _, g in near_grads], early_give)
    early_got = near_flip(early_give, "rz", zbits[-1])
    near_mine, near_give = d_mod(core_arg, list(enumerate(near_arrays)), w_qkv, span)
    far_parts, near_mine, near_give, last_given, first_recv, early_got = tie(
        far_parts, near_mine, near_give, last_given, first_recv, early_got
    )
    near_recv = flip(near_give, "core", 1)
    far_parts = [(mine, flip(give, "core", 1)) for mine, give in far_parts]
    last_given = flip(last_given, "core", 1)
    first_late = total([first_half(y), first_recv])
    first_give = give_half(first_late, "rz", zbits[0])
    last_blocks = [jnp.concatenate([last_kept[t], last_given[t]], axis=1) for t in range(1, chips)]
    early = keep_half(early, early_got, "rz", zbits[-1])
    far_parts, near_recv, early, last_blocks, first_give = tie(
        far_parts, near_recv, early, last_blocks, first_give
    )
    early_got = near_flip(early, "rz", zbits[-1])
    first_recv = near_flip(first_give, "rz", zbits[0])
    last_got = send(last_blocks)
    d_blocks = [(inputs, near_mine, near_recv)]
    d_blocks += [(far_blocks[t], *far_parts[t]) for t in range(chips - 1)]
    in_kept, in_given, in_sums, *far_sums = in_outer(place, d_blocks, d_resid, embedding, w_in, bi)
    in_kept, in_given, in_sums, far_sums, last_got, early_got, first_recv = tie(
        in_kept, in_given, in_sums, far_sums, last_got, early_got, first_recv
    )
    if rows > 1:
        in_kept, in_given = [jnp.sum(a.astype(F32), axis=0).astype(BF) for a in (in_kept, in_given)]
    else:
        in_kept, in_given = in_kept[0], in_given[0]

    emb_partial = jnp.stack(
        [in_sums[:, 0], in_sums[:, 1], sums[:, 4], sums[:, 2], sums[:, 3], sums[:, 0]], axis=1
    )
    over = lambda a: jnp.sum(a, axis=0)
    bias_mine = jnp.concatenate(
        [first_sums[0].reshape(3, -1), last_sums[0].reshape(3, -1)], axis=1
    )
    gap = jnp.zeros_like(bias_mine)
    b_qkv_grad = jnp.stack(
        [jnp.where(core == 0, bias_mine, gap), jnp.where(core == 0, gap, bias_mine)], axis=1
    )
    bias_sizes = [model, 3 * model, model, w_up.shape[1], model]
    biases = jnp.concatenate(
        [over(in_sums[:, 2]), b_qkv_grad.reshape(-1), over(sums[:, 5]), over(up_sums[:, 0]), over(sums[:, 1])]
    )
    vector = jnp.concatenate([emb_partial.reshape(-1), biases])

    in_given = flip(in_given, "core", 1)
    other = flip(vector, "core", 1)
    first_late = keep_half(first_late, first_recv, "rz", zbits[0])
    for bit in zbits[1:-1]:
        first_give = give_half(first_late, "rz", bit)
        first_late = keep_half(first_late, near_flip(first_give, "rz", bit), "rz", bit)
    early = join_halves(early, early_got, "rz", zbits[-1])
    for bit in zbits[-2:0:-1]:
        early = join_halves(early, near_flip(early, "rz", bit), "rz", bit)
    early_got = near_flip(early, "rz", zbits[0])
    in_given, other, first_late = tie(in_given, other, first_late)
    in_blocks = [total([in_kept[t], in_given[t]]) for t in range(1, chips)]
    vector = vector + other
    in_blocks, vector, far_sums, first_late = tie(in_blocks, vector, far_sums, first_late)
    in_got = send(in_blocks)
    vector = sum_small(vector, "sx")
    first_got = near_flip(give_half(first_late, "rz", zbits[-1]), "rz", zbits[-1])
    in_got, vector, first_got = tie(in_got, vector, first_got)
    far_got = [shift(p, "sx", t + 1) for t, p in enumerate(far_sums)]
    in_terms = [in_kept[0], in_given[0]] + in_got
    last_terms = [jnp.concatenate([last_kept[0], last_given[0]], axis=1)] + last_got
    in_give = jnp.concatenate([rows_give(in_terms), rows_give(last_terms)], axis=0)
    emb_size = rows * 6 * model
    d_embedding = vector[:emb_size].reshape(rows, 6 * model).astype(BF)
    biases = vector[emb_size:]
    shares, at = [], 0
    for size in bias_sizes:
        share = size // seq
        shares.append(lax.dynamic_slice_in_dim(biases, at + seq_index * share, share, 0))
        at += size
    width_share = model // seq
    act_share = lax.dynamic_slice_in_dim(time_act, seq_index * width_share, width_share, 1)
    shares = jnp.concatenate(shares)
    bias_share = shares.shape[0]
    shares = jnp.concatenate([shares[None], jnp.zeros((rows - 1, bias_share), F32)], axis=0)
    joined = jnp.concatenate([shares, act_share.astype(F32), d_embedding.astype(F32)], axis=1)
    first_late = keep_half(first_late, first_got, "rz", zbits[-1])
    time_float, in_give, joined, first_late = tie(time_float, in_give, joined, first_late)
    in_recv = flip(in_give, "ry", 1)
    joined = gather_small(joined, "ry")
    for bit in zbits[:0:-1]:
        first_late = join_halves(first_late, near_flip(first_late, "rz", bit), "rz", bit)
    _, silu_pull = jax.vjp(jax.nn.silu, time_float)
    time_grad = ada(d_embedding, ada_w, True)
    in_mine = [total([part_of(t, y, 2) for t in terms]) for terms in (in_terms, last_terms)]
    in_mine = jnp.concatenate(in_mine, axis=0)
    joined, in_recv, time_grad, in_mine, early_got, first_late = tie(
        joined, in_recv, time_grad, in_mine, early_got, first_late
    )
    time_grad = silu_pull(time_grad)[0]
    in_mine = total([in_mine, in_recv])
    early = join_halves(early, early_got, "rz", zbits[0])
    in_mine, first_late, early = tie(in_mine, first_late, early)
    early_other = flip(early, "ry", 1)
    for n, bit in enumerate(bits("rz")):
        in_got = near_flip(in_mine, "rz", bit)
        far_bit = bits("rz")[::-1][n]
        joined = jnp.concatenate([joined, near_flip(joined, "rz", far_bit)], axis=0)
        if n == 1:
            noisy_grad, cond_grad, text_grad = d_in(
                inputs, d_resid, embedding, keep, w_in, bi, [near_mine, near_recv] + far_got, mel
            )
            in_got, joined, noisy_grad = tie(in_got, joined, noisy_grad)
        in_mine = total([in_mine, in_got])
        if n == 0:
            first_got = near_flip(first_late, "rz", zbits[0])
            in_mine, joined, first_got = tie(in_mine, joined, first_got)
            first_late = join_halves(first_late, first_got, "rz", zbits[0])
            first_other = flip(first_late, "ry", 1)
        else:
            in_mine, joined = tie(in_mine, joined)
    in_mine, noisy_grad = tie(in_mine, noisy_grad)
    in_recv = flip(in_mine, "ry", 1)
    all_act = joined[:, bias_share : bias_share + width_share].astype(BF)
    all_emb = joined[:, bias_share + width_share :]
    ada_w_grad = dot_tn(all_act, all_emb.astype(BF))
    early = by_row(early, early_other).astype(F32)
    block = model // seq
    w_up_grad = jnp.concatenate([early[:block], early[block : 2 * block]], axis=1)
    w_down_grad = early[2 * block : 4 * block]
    w_out_grad = early[4 * block :]
    in_recv, ada_w_grad, first_other, w_up_grad, w_down_grad, w_out_grad = tie(
        in_recv, ada_w_grad, first_other, w_up_grad, w_down_grad, w_out_grad
    )
    share = in_mine.shape[0] // 2
    w_in_grad = by_row(in_mine[:share], in_recv[:share])[:, :width].astype(F32).T
    last_late = by_row(in_mine[share:], in_recv[share:])

    low, high = jnp.where(y == 0, first_late, first_other), jnp.where(y == 0, first_other, first_late)
    first_late = [jnp.where(core == 0, low, high), jnp.where(core == 0, high, low)]
    low, high = last_late[:, : 3 * 128], last_late[:, 3 * 128 :]
    last_late = [jnp.where(core == 0, low, high), jnp.where(core == 0, high, low)]
    w_qkv_grad = jnp.concatenate(
        [
            part[c][:, j * size : (j + 1) * size].astype(F32)
            for j in range(3)
            for c in range(2)
            for part, size in ((first_late, cut), (last_late, 128))
        ],
        axis=1,
    )
    shares = jnp.sum(joined[:, :bias_share], axis=0)
    b_in_grad, b_qkv_grad, b_out_grad, b_up_grad, b_down_grad = jnp.split(
        shares, [sum(bias_sizes[:n]) // seq for n in range(1, 5)]
    )
    emb_share = 6 * model // seq
    ada_b_grad = lax.dynamic_slice_in_dim(
        jnp.sum(all_emb, axis=0), seq_index * emb_share, emb_share, 0
    )
    return (
        result,
        noisy_grad,
        cond_grad,
        text_grad,
        time_grad,
        w_in_grad,
        b_in_grad,
        ada_w_grad,
        ada_b_grad,
        w_qkv_grad,
        b_qkv_grad,
        w_out_grad,
        b_out_grad,
        w_up_grad,
        b_up_grad,
        w_down_grad,
        b_down_grad,
    )


def solution(mesh):
    rows, seq = mesh.shape["rows"], mesh.shape["seq"]
    mesh = Mesh(mesh.devices.reshape(rows // 2, 2, seq // 2, 2), ("rz", "ry", "sx", "core"))
    r, s = ("rz", "ry"), ("sx", "core")
    in_specs = (
        (P(r, s, None),) * 3 + (P(r, None),) * 4 + (P(),) * 12 + (P(r, s, None),)
    )
    out_specs = (
        (P(r, s, None),) * 4
        + (P(r, None), P(None, s), P(s))
        + (P(s, None), P(s)) * 5
    )
    return jax.shard_map(shards, mesh=mesh, in_specs=in_specs, out_specs=out_specs, check_vma=False)
```
